32 devices in a mesh: dp: 16 (over z, x, core), mp: 2 (over y).
Axes of the slice: x: 2, y: 2, z: 4, core: 2. Of those that a mesh axis runs over, the one named last changes fastest.
Arguments:
- pixels: bfloat16 [16384, 192], P('dp'), may hold values from -4 to 4
- valid_mask: int32 [16384, 192], P('dp'), may hold values from 0 to 1, as said below
- code_index: int32 [16384], P('dp'), may hold values from 0 to 8191
- attention_weight: float32 [2, 4, 512, 512], P(None, None, 'dp', 'mp')
- attention_moment: float32 [2, 4, 512, 512], P(None, None, 'dp', 'mp')
- attention_square: float32 [2, 4, 512, 512], P(None, None, 'dp', 'mp'), as said below
- feedforward_weight: float32 [2, 2, 512, 2048], P(None, None, 'dp', 'mp')
- feedforward_moment: float32 [2, 2, 512, 2048], P(None, None, 'dp', 'mp')
- feedforward_square: float32 [2, 2, 512, 2048], P(None, None, 'dp', 'mp'), as said below
- pixel_weight: float32 [2, 192, 512], P(None, None, 'dp')
- pixel_moment: float32 [2, 192, 512], P(None, None, 'dp')
- pixel_square: float32 [2, 192, 512], P(None, None, 'dp'), as said below
- code_weight: float32 [2, 32, 512], P(None, None, 'dp')
- code_moment: float32 [2, 32, 512], P(None, None, 'dp')
- code_square: float32 [2, 32, 512], P(None, None, 'dp'), as said below
- codebook: float32 [8192, 32], P('dp'), may hold values from -6 to 6
- codebook_moment: float32 [8192, 32], P('dp')
- codebook_square: float32 [8192, 32], P('dp'), as said below
- norm_gains: float32 [6, 512], P(None, 'dp'), as said below
- gains_moment: float32 [6, 512], P(None, 'dp')
- gains_square: float32 [6, 512], P(None, 'dp'), as said below
Outputs:
- attention_updated: float32 [2, 4, 512, 512], P(None, None, 'dp', 'mp')
- attention_momentum: float32 [2, 4, 512, 512], P(None, None, 'dp', 'mp')
- attention_variance: float32 [2, 4, 512, 512], P(None, None, 'dp', 'mp')
- feedforward_updated: float32 [2, 2, 512, 2048], P(None, None, 'dp', 'mp')
- feedforward_momentum: float32 [2, 2, 512, 2048], P(None, None, 'dp', 'mp')
- feedforward_variance: float32 [2, 2, 512, 2048], P(None, None, 'dp', 'mp')
- pixel_updated: float32 [2, 192, 512], P(None, None, 'dp')
- pixel_momentum: float32 [2, 192, 512], P(None, None, 'dp')
- pixel_variance: float32 [2, 192, 512], P(None, None, 'dp')
- code_updated: float32 [2, 32, 512], P(None, None, 'dp')
- code_momentum: float32 [2, 32, 512], P(None, None, 'dp')
- code_variance: float32 [2, 32, 512], P(None, None, 'dp')
- codebook_updated: float32 [8192, 32], P('dp')
- codebook_momentum: float32 [8192, 32], P('dp')
- codebook_variance: float32 [8192, 32], P('dp')
- gains_updated: float32 [6, 512], P(None, 'dp')
- gains_momentum: float32 [6, 512], P(None, 'dp')
- gains_variance: float32 [6, 512], P(None, 'dp')
- loss_sum: float32 [], replicated
- valid_count: float32 [], replicated
- gradient_norm: float32 [], replicated
The draws below stay inside these ranges and needn't reach their ends.
Inputs may be any that keep to these rules, and one draw needn't show every extreme that they name: `valid_mask`: 1 marks a pixel value that counts in the loss. `norm_gains`: positive. `attention_square`: positive. `feedforward_square`: positive. `pixel_square`: positive. `code_square`: positive. `codebook_square`: positive. `gains_square`: positive.
All inputs are finite; a program needn't handle non-finite values.
Results may differ from the reference program's by a relative error of at most 0.01.
The reference program's roundings to bfloat16 on the way count: a program that leaves them out, or rounds other values in their place, can miss the bound.
Values may be sent and summed in bfloat16 or wider, within the bound.
No kernel may reach another device: no remote copies, remote signals or barrier semaphores. Data moves between devices by JAX's collectives and lax.ppermute only.
A program may use at most 128 MiB of HBM per device.

```python
import math
import jax
import jax.numpy as jnp
from jax import lax

D = 512
HEADS = 8
HD = 64
FF = 2048
PATCH = 192
CODES = 8192
CDIM = 32
SEQ = 1024
STACK = 2
STEP = 10
IMAGES = 16
TOKENS = 16384
PARAMS = 6786048


clip_norm = 0.003


def step_size(factor):
    return factor * clip_norm / math.sqrt(PARAMS)


def first_moment(key, array_shape, factor):
    return 0.11 * step_size(factor) * jax.random.normal(key, array_shape, jnp.float32)


def second_moment(key, array_shape, factor):
    spread = jnp.exp(jax.random.uniform(key, array_shape, jnp.float32, math.log(0.5), math.log(8.0)))
    return 0.001 * step_size(factor) * step_size(factor) * spread


def draw_valid_mask(key, part):
    key = jax.random.fold_in(key, 11)
    roll_key, place_key = jax.random.split(key)
    values = SEQ * PATCH
    scale_range = 1048576
    base_level = max(524, 2 * scale_range // values)
    image_line = lax.iota(jnp.int32, IMAGES)
    limits = base_level * (IMAGES + 2 * image_line) // IMAGES
    rolled = jax.random.randint(roll_key, (IMAGES, values), 0, scale_range)
    placed = jax.random.randint(place_key, (IMAGES, 1), 0, values)
    chosen = (rolled < limits[:, None]) | (lax.iota(jnp.int32, values)[None, :] == placed)
    return chosen.astype(jnp.int32).reshape(TOKENS, PATCH)


def draw_attention_weight(key, part):
    key = jax.random.fold_in(key, 21)
    scales = jnp.array([1.0, 1.0, 1.0, 12.0], jnp.float32).reshape(1, 4, 1, 1) * D ** (-0.5)
    return jax.random.normal(key, (STACK, 4, D, D), jnp.float32) * scales


def draw_feedforward_weight(key, part):
    key = jax.random.fold_in(key, 22)
    scales = jnp.array([D ** (-0.5), FF ** (-0.5)], jnp.float32).reshape(1, 2, 1, 1)
    return jax.random.normal(key, (STACK, 2, D, FF), jnp.float32) * scales


def draw_pixel_weight(key, part):
    key = jax.random.fold_in(key, 23)
    scales = jnp.array([PATCH ** (-0.5), D ** (-0.5)], jnp.float32).reshape(2, 1, 1)
    return jax.random.normal(key, (2, PATCH, D), jnp.float32) * scales


def draw_code_weight(key, part):
    key = jax.random.fold_in(key, 24)
    scales = jnp.array([D ** (-0.5), 1.0], jnp.float32).reshape(2, 1, 1)
    return jax.random.normal(key, (2, CDIM, D), jnp.float32) * scales


def draw_norm_gains(key, part):
    key = jax.random.fold_in(key, 25)
    ramp_line = lax.iota(jnp.float32, D) / (D - 1)
    base_gain = 0.6 + 1.2 * ramp_line
    jitter = jax.random.uniform(key, (3 * STACK, D), jnp.float32, 0.8, 1.25)
    return base_gain[None, :] * jitter


def draw_attention_moment(key, part):
    return first_moment(jax.random.fold_in(key, 31), (STACK, 4, D, D), 1.0)


def draw_feedforward_moment(key, part):
    return first_moment(jax.random.fold_in(key, 32), (STACK, 2, D, FF), 1.0)


def draw_pixel_moment(key, part):
    return first_moment(jax.random.fold_in(key, 33), (2, PATCH, D), 1.0)


def draw_code_moment(key, part):
    return first_moment(jax.random.fold_in(key, 34), (2, CDIM, D), 1.0)


def draw_codebook_moment(key, part):
    return first_moment(jax.random.fold_in(key, 35), (CODES, CDIM), 0.5)


def draw_gains_moment(key, part):
    return first_moment(jax.random.fold_in(key, 36), (3 * STACK, D), 4.0)


def draw_attention_square(key, part):
    return second_moment(jax.random.fold_in(key, 41), (STACK, 4, D, D), 1.0)


def draw_feedforward_square(key, part):
    return second_moment(jax.random.fold_in(key, 42), (STACK, 2, D, FF), 1.0)


def draw_pixel_square(key, part):
    return second_moment(jax.random.fold_in(key, 43), (2, PATCH, D), 1.0)


def draw_code_square(key, part):
    return second_moment(jax.random.fold_in(key, 44), (2, CDIM, D), 1.0)


def draw_codebook_square(key, part):
    return second_moment(jax.random.fold_in(key, 45), (CODES, CDIM), 0.5)


def draw_gains_square(key, part):
    return second_moment(jax.random.fold_in(key, 46), (3 * STACK, D), 4.0)


def plant(values, rng, low, top_value):
    dims = values.shape
    index_at = [jax.random.randint(jax.random.fold_in(rng, axis), (), 0, dims[axis]) for axis in range(len(dims))]
    values = values.at[tuple(index_at)].set(low)
    longest = dims.index(max(dims))
    index_at[longest] = (index_at[longest] + 1) % dims[longest]
    return values.at[tuple(index_at)].set(top_value)


def steps_of(key, shape, pieces, least, high):
    loudness = 1.0
    for axis_at, blocks in pieces:
        steps = jax.random.uniform(jax.random.fold_in(jax.random.fold_in(key, 6), axis_at), (blocks,), jnp.float32, least / len(pieces), high / len(pieces))
        loudness = loudness * jnp.repeat(jnp.exp(steps), shape[axis_at] // blocks).reshape((-1,) + (1,) * (len(shape) - 1 - axis_at))
    return loudness


def noise(own_key, extent, scale, bound, cuts=(), held_as=jnp.bfloat16):
    values = scale * jax.random.normal(own_key, extent, jnp.float32)
    if cuts:
        values = values * steps_of(own_key, extent, cuts, -0.22, 0.18)
    return jnp.clip(values, -bound, bound).astype(held_as)


def setup_inputs(seed: int = 0) -> dict:
    seeds = jax.random.split(jax.random.key(seed), 22)
    return {
        "pixels": noise(seeds[0], (TOKENS, PATCH), 1.0, 4.0, ((0, 16),)),
        "valid_mask": draw_valid_mask(jax.random.fold_in(seeds[21], 71), 0),
        "code_index": plant(jax.random.randint(seeds[2], (TOKENS,), 0, CODES), jax.random.fold_in(seeds[2], 1), 0, CODES - 1).astype(jnp.int32),
        "attention_weight": draw_attention_weight(jax.random.fold_in(seeds[21], 71), 0),
        "attention_moment": draw_attention_moment(jax.random.fold_in(seeds[21], 71), 0),
        "attention_square": draw_attention_square(jax.random.fold_in(seeds[21], 71), 0),
        "feedforward_weight": draw_feedforward_weight(jax.random.fold_in(seeds[21], 71), 0),
        "feedforward_moment": draw_feedforward_moment(jax.random.fold_in(seeds[21], 71), 0),
        "feedforward_square": draw_feedforward_square(jax.random.fold_in(seeds[21], 71), 0),
        "pixel_weight": draw_pixel_weight(jax.random.fold_in(seeds[21], 71), 0),
        "pixel_moment": draw_pixel_moment(jax.random.fold_in(seeds[21], 71), 0),
        "pixel_square": draw_pixel_square(jax.random.fold_in(seeds[21], 71), 0),
        "code_weight": draw_code_weight(jax.random.fold_in(seeds[21], 71), 0),
        "code_moment": draw_code_moment(jax.random.fold_in(seeds[21], 71), 0),
        "code_square": draw_code_square(jax.random.fold_in(seeds[21], 71), 0),
        "codebook": noise(seeds[15], (CODES, CDIM), 1.0, 6.0, ((0, 16),), jnp.float32),
        "codebook_moment": draw_codebook_moment(jax.random.fold_in(seeds[21], 71), 0),
        "codebook_square": draw_codebook_square(jax.random.fold_in(seeds[21], 71), 0),
        "norm_gains": draw_norm_gains(jax.random.fold_in(seeds[21], 71), 0),
        "gains_moment": draw_gains_moment(jax.random.fold_in(seeds[21], 71), 0),
        "gains_square": draw_gains_square(jax.random.fold_in(seeds[21], 71), 0),
    }


norm_epsilon = 1e-05
commit_weight = 0.25
clip_norm = 0.003
learn_rates = (0.2, 0.02, 0.04, 0.5, 0.5, 0.6)
first_decay = 0.9
second_decay = 0.999
weight_decay = 0.01
adam_epsilon = 1e-08
highest = lax.Precision.HIGHEST

@jax.custom_vjp
def low(v):
    return lax.optimization_barrier(v.astype(jnp.bfloat16)).astype(jnp.float32)

@jax.custom_vjp
def low_back(v):
    return v

def low_keep(v):
    return (low(v), None)

def low_pass(kept, grad):
    return (grad,)

def back_keep(v):
    return (v, None)

def back_low(kept, grad):
    return (low(grad),)
low.defvjp(low_keep, low_pass)
low_back.defvjp(back_keep, back_low)

def matmul(left, right):
    return jnp.dot(left, right, precision=highest, preferred_element_type=jnp.float32)

def layer_norm(hidden, gain_row):
    centred = hidden - lax.optimization_barrier(jnp.mean(hidden, axis=-1, keepdims=True))
    spread = lax.optimization_barrier(jnp.mean(centred * centred, axis=-1, keepdims=True))
    return centred * lax.rsqrt(spread + norm_epsilon) * gain_row

def unit_norm(vector):
    return vector * lax.rsqrt(lax.optimization_barrier(jnp.sum(vector * vector, axis=-1, keepdims=True)) + 1.0)

def block(hidden, attention, feedforward, gain_one, gain_two):
    normed = low(layer_norm(hidden, gain_one))
    query_heads = low_back(low(matmul(normed, attention[0]))).reshape(SEQ, HEADS, HD)
    key_heads = low_back(low(matmul(normed, attention[1]))).reshape(SEQ, HEADS, HD)
    value_heads = low_back(low(matmul(normed, attention[2]))).reshape(SEQ, HEADS, HD)
    scores = low_back(jnp.einsum('qhe,khe->hqk', query_heads, key_heads, precision=highest) * HD ** (-0.5))
    exponent = jnp.exp(scores - lax.optimization_barrier(jnp.max(scores, axis=-1, keepdims=True)))
    probabilities = low(exponent / lax.optimization_barrier(jnp.sum(exponent, axis=-1, keepdims=True)))
    mixed_heads = jnp.einsum('hqk,khe->qhe', probabilities, value_heads, precision=highest)
    mixed_heads = low_back(low(mixed_heads)).reshape(SEQ, D)
    middle = hidden + low_back(matmul(mixed_heads, attention[3].T))
    normed_two = low(layer_norm(middle, gain_two))
    before = low_back(matmul(normed_two, feedforward[0]))
    active = low(jax.nn.gelu(before, approximate=True))
    return middle + low_back(matmul(active, feedforward[1].T))

def image_loss(weights, pixel_rows, valid_rows, index_rows):
    attention, feedforward, pixel_mats, code_mats, book_unit, gain_rows = weights
    hidden = low_back(matmul(pixel_rows, pixel_mats[0]))
    hidden = block(hidden, attention[0], feedforward[0], gain_rows[0], gain_rows[1])
    final_low = low(layer_norm(hidden, gain_rows[2]))
    latent = unit_norm(low_back(matmul(final_low, code_mats[0].T)))
    onehot = (index_rows[:, None] == jnp.arange(CODES, dtype=jnp.int32)[None, :]).astype(jnp.float32)
    looked = low_back(matmul(onehot, book_unit))
    decoded = low_back(matmul(looked, code_mats[1]))
    decoded = block(decoded, attention[1], feedforward[1], gain_rows[3], gain_rows[4])
    output = low_back(matmul(low(layer_norm(decoded, gain_rows[5])), pixel_mats[1].T))
    pixel_gap = output - pixel_rows
    pixel_term = jnp.sum(valid_rows * (pixel_gap * pixel_gap + jnp.sqrt(pixel_gap * pixel_gap + 1.0) - 1.0))
    distance = latent - looked
    return pixel_term + commit_weight * jnp.sum(distance * distance)

def total_loss(masters, pixels_float, valid_float, code_index):
    attention, feedforward, pixel_mats, code_mats, book_rows, gain_rows = [low(member) for member in masters]
    book_unit = low(unit_norm(book_rows))
    weights = (attention, feedforward, pixel_mats, code_mats, book_unit, gain_rows)
    step_loss = jax.checkpoint(image_loss)

    def accumulate(running, operands):
        return (running + step_loss(weights, operands[0], operands[1], operands[2]), None)
    operands = (pixels_float.reshape(IMAGES, SEQ, PATCH), valid_float.reshape(IMAGES, SEQ, PATCH), code_index.reshape(IMAGES, SEQ))
    return lax.scan(accumulate, jnp.zeros((), jnp.float32), operands)[0]

def adam_update(master, moment, square, clipped, rate):
    moment_new = first_decay * moment + (1.0 - first_decay) * clipped
    square_new = second_decay * square + (1.0 - second_decay) * clipped * clipped
    moment_hat = moment_new / (1.0 - first_decay ** STEP)
    square_hat = square_new / (1.0 - second_decay ** STEP)
    updated = master - rate * (moment_hat / (jnp.sqrt(square_hat) + adam_epsilon) + weight_decay * master)
    return (updated, moment_new, square_new)

def reference(pixels, valid_mask, code_index, attention_weight, attention_moment, attention_square, feedforward_weight, feedforward_moment, feedforward_square, pixel_weight, pixel_moment, pixel_square, code_weight, code_moment, code_square, codebook, codebook_moment, codebook_square, norm_gains, gains_moment, gains_square):
    masters = (attention_weight, feedforward_weight, pixel_weight, code_weight, codebook, norm_gains)
    moments = (attention_moment, feedforward_moment, pixel_moment, code_moment, codebook_moment, gains_moment)
    squares = (attention_square, feedforward_square, pixel_square, code_square, codebook_square, gains_square)
    pixels_float = pixels.astype(jnp.float32)
    valid_float = valid_mask.astype(jnp.float32)
    valid_total = jnp.sum(valid_float)
    loss_total, pullback = jax.vjp(lambda params: total_loss(params, pixels_float, valid_float, code_index), masters)
    gradients = pullback(1.0 / valid_total)[0]
    norm_total = jnp.sqrt(sum((jnp.sum(member * member) for member in gradients)))
    factor = clip_norm / jnp.maximum(norm_total, clip_norm)
    results = [adam_update(master, moment, square, member * factor, rate) for master, moment, square, member, rate in zip(masters, moments, squares, gradients, learn_rates)]
    return (results[0][0], results[0][1], results[0][2], results[1][0], results[1][1], results[1][2], results[2][0], results[2][1], results[2][2], results[3][0], results[3][1], results[3][2], results[4][0], results[4][1], results[4][2], results[5][0], results[5][1], results[5][2], loss_total, valid_total, norm_total)
```

```python
import jax
import jax.numpy as jnp
from jax import lax
from jax.sharding import PartitionSpec as P

HD = 64
SEQ = 1024
STEP = 10

norm_epsilon = 1e-05
commit_weight = 0.25
clip_norm = 0.003
learn_rates = (0.2, 0.02, 0.04, 0.5, 0.5, 0.6)
first_decay = 0.9
second_decay = 0.999
weight_decay = 0.01
adam_epsilon = 1e-08

bf16 = jnp.bfloat16
f32 = jnp.float32


def layer_norm(hidden, gain_row):
    centred = hidden - jnp.mean(hidden, axis=-1, keepdims=True)
    spread = jnp.mean(centred * centred, axis=-1, keepdims=True)
    return centred * lax.rsqrt(spread + norm_epsilon) * gain_row


def unit_norm(vector):
    return vector * lax.rsqrt(jnp.sum(vector * vector, axis=-1, keepdims=True) + 1.0)


def gelu_tanh(inputs):
    return jax.nn.gelu(inputs, approximate=True)


def dot(spec, left, right):
    return jnp.einsum(spec, left, right, preferred_element_type=f32)


def swap_dp(value, bit):
    size = lax.axis_size("dp")
    return lax.ppermute(value, "dp", [(i, i ^ (1 << bit)) for i in range(size)])


def swap_mp(value):
    return lax.ppermute(value, "mp", [(0, 1), (1, 0)])


def bits_of(size):
    return size.bit_length() - 1


def gather_xor(blocks, orders):
    bits = bits_of(lax.axis_size("dp"))
    held = [b.reshape((1,) * bits + b.shape) for b in blocks]
    for step in range(bits):
        got = [swap_dp(h, order[step]) for h, order in zip(held, orders)]
        held = [
            jnp.concatenate([h, g], axis=order[step]) for h, g, order in zip(held, got, orders)
        ]
    return [h.reshape((-1, h.shape[-1])) for h in held]


def scatter_xor(arrays, orders):
    size = lax.axis_size("dp")
    bits = bits_of(size)
    held = [a.reshape((2,) * bits + (a.shape[0] // size, a.shape[1])) for a in arrays]
    for step in range(bits):
        sent = [
            swap_dp(lax.slice_in_dim(h, 1, 2, axis=order[step]).astype(bf16), order[step])
            for h, order in zip(held, orders)
        ]
        held = [
            lax.slice_in_dim(h, 0, 1, axis=order[step]) + s.astype(f32)
            for h, s, order in zip(held, sent, orders)
        ]
    return [h.reshape(h.shape[-2:]) for h in held]


def gather_orders(bits):
    high = list(range(bits - 1, 1, -1))
    return (high + [1, 0], [1] + high + [0])


def scatter_orders(bits):
    low = list(range(2, bits))
    return ([0, 1] + low, [0] + low + [1])


def all_sum(value):
    for bit in range(bits_of(lax.axis_size("dp"))):
        value = value + swap_dp(value, bit)
    return value + swap_mp(value)


def attention_forward(q, k, v):
    heads = q.shape[1] // HD
    q, k, v = (a.reshape(SEQ, heads, HD) for a in (q, k, v))
    s = dot("qhe,khe->hqk", q, k) * HD**-0.5
    peak = jnp.max(s, axis=-1, keepdims=True)
    e = jnp.exp(s - peak)
    total = jnp.sum(e, axis=-1, keepdims=True)
    p = (e / total).astype(bf16)
    o = dot("hqk,khe->qhe", p, v).astype(bf16).reshape(SEQ, heads * HD)
    return o, peak + jnp.log(total)


def attention_backward(q, k, v, log_total, go):
    heads = q.shape[1] // HD
    q, k, v, go = (a.reshape(SEQ, heads, HD) for a in (q, k, v, go))
    s = dot("qhe,khe->hqk", q, k) * HD**-0.5
    p = jnp.exp(s - log_total)
    gp = dot("qhe,khe->hqk", go, v)
    gs = (p * (gp - jnp.sum(gp * p, axis=-1, keepdims=True))).astype(bf16)
    gq = dot("hqk,khe->qhe", gs, k) * HD**-0.5
    gk = dot("hqk,qhe->khe", gs, q) * HD**-0.5
    gv = dot("hqk,qhe->khe", p.astype(bf16), go)
    return tuple(g.astype(bf16).reshape(SEQ, heads * HD) for g in (gq, gk, gv))


def adam_update(master, moment, square, clipped, rate):
    moment_new = first_decay * moment + (1.0 - first_decay) * clipped
    square_new = second_decay * square + (1.0 - second_decay) * clipped * clipped
    moment_hat = moment_new / (1.0 - first_decay**STEP)
    square_hat = square_new / (1.0 - second_decay**STEP)
    updated = master - rate * (
        moment_hat / (jnp.sqrt(square_hat) + adam_epsilon) + weight_decay * master
    )
    return (updated, moment_new, square_new)


def body(
    pixels,
    valid_mask,
    code_index,
    attention_weight,
    attention_moment,
    attention_square,
    feedforward_weight,
    feedforward_moment,
    feedforward_square,
    pixel_weight,
    pixel_moment,
    pixel_square,
    code_weight,
    code_moment,
    code_square,
    codebook,
    codebook_moment,
    codebook_square,
    norm_gains,
    gains_moment,
    gains_square,
):
    side = lax.axis_index("mp")
    place = lax.axis_index("dp")
    parts = lax.axis_size("dp")
    bits = bits_of(parts)
    encoder = side == 0
    rows = attention_weight.shape[2]
    width = rows * parts
    half = attention_weight.shape[3]
    units = feedforward_weight.shape[3]
    patch = pixel_weight.shape[1]
    cdim = code_weight.shape[1]
    codes_here = codebook.shape[0]

    def mine(array):
        return jnp.where(encoder, array[0], array[1])

    def other(array):
        return jnp.where(encoder, array[1], array[0])

    def columns(attention, feedforward):
        qkv = attention[:3].transpose(1, 0, 2).reshape(rows, 3 * half)
        rest = jnp.concatenate([attention[3], feedforward[0], feedforward[1]], axis=1)
        return qkv, rest

    attention_low = attention_weight.astype(bf16)
    feedforward_low = feedforward_weight.astype(bf16)
    qkv_own, rest_own = columns(mine(attention_low), mine(feedforward_low))
    qkv_sent, rest_sent = columns(other(attention_low), other(feedforward_low))
    qkv_got, rest_got = swap_mp(qkv_sent), swap_mp(rest_sent)

    count_here = jnp.sum(valid_mask)
    digits = jnp.stack([count_here & 255, (count_here >> 8) & 255, count_here >> 16])
    digit_rows = jnp.where(lax.iota(jnp.int32, rows)[:, None] == 0, digits[None, :], 0)
    gains_low = norm_gains.astype(bf16).reshape(2, 3, rows)
    small = jnp.concatenate(
        [
            mine(pixel_weight.astype(bf16)).T,
            mine(code_weight.astype(bf16)).T,
            mine(gains_low).T,
            digit_rows.astype(bf16),
            jnp.zeros((rows, 256 - patch - cdim - 6), bf16),
        ],
        axis=1,
    )
    book_rows = codebook.astype(bf16).astype(f32)
    book_unit, book_pull = jax.vjp(unit_norm, book_rows)
    book_block = book_unit.astype(bf16).T.reshape(rows, cdim * codes_here // rows)

    order_a, order_b = gather_orders(bits)
    qkv_a, qkv_b, small_all, book_all = gather_xor(
        [qkv_own, qkv_got, small, book_block], [order_a, order_b, order_a, order_b]
    )
    rest_a, rest_b = gather_xor([rest_own, rest_got], [order_a, order_b])

    a_qkv = [
        jnp.concatenate([qkv_a[:, i * half : (i + 1) * half], qkv_b[:, i * half : (i + 1) * half]], 1)
        for i in range(3)
    ]
    a_out = jnp.concatenate([rest_a[:, :half], rest_b[:, :half]], axis=1)
    f_up = jnp.concatenate([rest_a[:, half : half + units], rest_b[:, half : half + units]], axis=1)
    f_down = jnp.concatenate([rest_a[:, half + units :], rest_b[:, half + units :]], axis=1)
    pixel_t = small_all[:, :patch]
    code_t = small_all[:, patch : patch + cdim]
    gains = small_all[:, patch + cdim : patch + cdim + 3].astype(f32).T
    digit_sum = jnp.sum(
        small_all[:, patch + cdim + 3 : patch + cdim + 6].astype(f32), axis=0
    )
    count_total = digit_sum[0] + 256.0 * digit_sum[1] + 65536.0 * digit_sum[2]

    block = (code_index // codes_here) ^ place
    turned = jnp.zeros_like(block)
    for bit in range(bits):
        turned = turned | (((block >> bit) & 1) << (bits - 1 - bit))
    code_place = turned * codes_here + code_index % codes_here
    onehot = (
        code_place[:, None] == lax.iota(jnp.int32, codes_here * parts)[None, :]
    ).astype(bf16)
    book_t = book_all.reshape(parts, cdim, codes_here).transpose(1, 0, 2).reshape(cdim, -1)
    looked = dot("tc,ec->te", onehot, book_t)
    looked_low = looked.astype(bf16)

    hidden = jnp.where(
        encoder, dot("tp,dp->td", pixels, pixel_t), dot("tc,dc->td", looked_low, code_t)
    )
    normed, pull_one = jax.vjp(layer_norm, hidden, gains[0])
    normed = normed.astype(bf16)
    q, k, v = (dot("td,dc->tc", normed, w).astype(bf16) for w in a_qkv)
    mixed, log_total = attention_forward(q, k, v)
    middle = hidden + dot("tc,dc->td", mixed, a_out)
    normed_two, pull_two = jax.vjp(layer_norm, middle, gains[1])
    normed_two = normed_two.astype(bf16)
    before = dot("td,df->tf", normed_two, f_up)
    active, pull_gelu = jax.vjp(gelu_tanh, before)
    active = active.astype(bf16)
    result = middle + dot("tf,df->td", active, f_down)

    final, pull_final = jax.vjp(layer_norm, result, gains[2])
    final = final.astype(bf16)
    raw = dot("td,dc->tc", final, code_t)
    latent, pull_latent = jax.vjp(unit_norm, raw)
    latent_there = swap_mp(latent)
    output = dot("td,dp->tp", final, pixel_t)
    valid = valid_mask.astype(f32)
    gap = output - pixels.astype(f32)
    root = jnp.sqrt(gap * gap + 1.0)
    loss_here = jnp.where(
        encoder,
        commit_weight * jnp.sum((latent - looked) ** 2),
        jnp.sum(valid * (gap * gap + root - 1.0)),
    )
    g_out = (valid * (2.0 * gap + gap / root) / count_total).astype(bf16)
    g_raw = pull_latent(2.0 * commit_weight * (latent - looked) / count_total)[0].astype(bf16)
    g_final = jnp.where(
        encoder, dot("tc,dc->td", g_raw, code_t), dot("tp,dp->td", g_out, pixel_t)
    )
    g_result, g_gain_final = pull_final(g_final)

    g_low = g_result.astype(bf16)
    g_down = dot("td,tf->df", g_low, active)
    g_before = pull_gelu(dot("td,df->tf", g_low, f_down))[0].astype(bf16)
    g_up = dot("td,tf->df", normed_two, g_before)
    g_norm_two, g_gain_two = pull_two(dot("tf,df->td", g_before, f_up))
    g_middle = g_result + g_norm_two
    g_branch = g_middle.astype(bf16)
    g_proj = dot("td,tc->dc", g_branch, mixed)
    g_mixed = dot("td,dc->tc", g_branch, a_out).astype(bf16)

    scatter_a, scatter_b = scatter_orders(bits)
    rest_own, rest_sent = scatter_xor(
        [
            jnp.concatenate([g_proj[:, :half], g_up[:, :units], g_down[:, :units]], axis=1),
            jnp.concatenate([g_proj[:, half:], g_up[:, units:], g_down[:, units:]], axis=1),
        ],
        [scatter_a, scatter_b],
    )

    gq, gk, gv = attention_backward(q, k, v, log_total, g_mixed)
    g_qkv = [dot("td,tc->dc", normed, g) for g in (gq, gk, gv)]
    g_normed = sum(dot("tc,dc->td", g, w) for g, w in zip((gq, gk, gv), a_qkv))
    g_norm_one, g_gain_one = pull_one(g_normed)
    g_hidden = (g_middle + g_norm_one).astype(bf16)
    g_pixel = dot(
        "td,tp->dp",
        jnp.where(encoder, g_hidden, final),
        jnp.where(encoder, pixels, g_out),
    )
    g_code = dot(
        "td,tc->dc",
        jnp.where(encoder, final, g_hidden),
        jnp.where(encoder, g_raw, looked_low),
    )
    g_looked = dot("td,dc->tc", g_hidden, code_t) + 2.0 * commit_weight * (
        looked - latent_there
    ) / count_total
    g_looked = jnp.where(encoder, 0.0, g_looked).astype(bf16)
    g_book = dot("te,tc->ec", g_looked, onehot)
    g_book = g_book.reshape(cdim, parts, codes_here).transpose(1, 0, 2).reshape(width, -1)
    g_small = jnp.concatenate(
        [
            g_pixel,
            g_code,
            jnp.stack([g_gain_one, g_gain_two, g_gain_final], axis=1),
            jnp.zeros((width, 256 - patch - cdim - 3), f32),
        ],
        axis=1,
    )
    qkv_own, qkv_sent, small_own, book_own = scatter_xor(
        [
            jnp.concatenate([g[:, :half] for g in g_qkv], axis=1),
            jnp.concatenate([g[:, half:] for g in g_qkv], axis=1),
            g_small,
            g_book,
        ],
        [scatter_a, scatter_b, scatter_a, scatter_b],
    )
    book_own = book_pull(book_own.reshape(cdim, codes_here).T)[0].T
    squares_here = sum(
        jnp.sum(a * a) for a in (rest_own, rest_sent, qkv_own, qkv_sent, small_own, book_own)
    )
    rest_got, qkv_got, small_got, book_got = (
        swap_mp(a) for a in (rest_sent, qkv_sent, small_own, book_own)
    )
    totals = all_sum(jnp.stack([squares_here, loss_here]))
    norm_total = jnp.sqrt(totals[0])
    factor = clip_norm / jnp.maximum(norm_total, clip_norm)

    def both(own, got):
        return jnp.stack([jnp.where(encoder, own, got), jnp.where(encoder, got, own)])

    def attention_of(qkv, rest):
        parts_qkv = qkv.reshape(rows, 3, half).transpose(1, 0, 2)
        return jnp.concatenate([parts_qkv, rest[None, :, :half]], axis=0)

    def feedforward_of(rest):
        return rest[:, half:].reshape(rows, 2, units).transpose(1, 0, 2)

    small_t = both(small_own.T, small_got.T)
    book_sum = jnp.where(encoder, book_got, book_own).T
    shards = (
        both(attention_of(qkv_own, rest_own), attention_of(qkv_got, rest_got)),
        both(feedforward_of(rest_own), feedforward_of(rest_got)),
        small_t[:, :patch],
        small_t[:, patch : patch + cdim],
        book_sum,
        small_t[:, patch + cdim : patch + cdim + 3].reshape(6, rows),
    )
    masters = (
        attention_weight,
        feedforward_weight,
        pixel_weight,
        code_weight,
        codebook,
        norm_gains,
    )
    moments = (
        attention_moment,
        feedforward_moment,
        pixel_moment,
        code_moment,
        codebook_moment,
        gains_moment,
    )
    squares = (
        attention_square,
        feedforward_square,
        pixel_square,
        code_square,
        codebook_square,
        gains_square,
    )
    results = []
    for master, moment, square, member, rate in zip(masters, moments, squares, shards, learn_rates):
        results.extend(adam_update(master, moment, square, member * factor, rate))
    return tuple(results) + (totals[1], count_total, norm_total)


def solution(mesh):
    wide = P(None, None, "dp", "mp")
    thin = P(None, None, "dp")
    rows = P("dp", None)
    gain = P(None, "dp")
    weights = (wide,) * 6 + (thin,) * 6 + (rows,) * 3 + (gain,) * 3
    return jax.shard_map(
        body,
        mesh=mesh,
        in_specs=(rows, rows, P("dp")) + weights,
        out_specs=weights + (P(), P(), P()),
        check_vma=False,
    )
```

```python
import functools

import jax
import jax.numpy as jnp
from jax import lax
from jax.experimental import pallas as pl
from jax.experimental.pallas import tpu as pltpu
from jax.sharding import PartitionSpec as P

HD = 64
SEQ = 1024
STEP = 10

norm_epsilon = 1e-05
commit_weight = 0.25
clip_norm = 0.003
learn_rates = (0.2, 0.02, 0.04, 0.5, 0.5, 0.6)
first_decay = 0.9
second_decay = 0.999
weight_decay = 0.01
adam_epsilon = 1e-08

bf16 = jnp.bfloat16
f32 = jnp.float32


def layer_norm(hidden, gain_row):
    centred = hidden - jnp.mean(hidden, axis=-1, keepdims=True)
    spread = jnp.mean(centred * centred, axis=-1, keepdims=True)
    return centred * lax.rsqrt(spread + norm_epsilon) * gain_row


def unit_norm(vector):
    return vector * lax.rsqrt(jnp.sum(vector * vector, axis=-1, keepdims=True) + 1.0)


def gelu_tanh(inputs):
    return jax.nn.gelu(inputs, approximate=True)


def dot(spec, left, right):
    return jnp.einsum(spec, left, right, preferred_element_type=f32)


def swap_dp(value, bit):
    size = lax.axis_size("dp")
    return lax.ppermute(value, "dp", [(i, i ^ (1 << bit)) for i in range(size)])


def swap_mp(value):
    return lax.ppermute(value, "mp", [(0, 1), (1, 0)])


def bits_of(size):
    return size.bit_length() - 1


def gather_xor(blocks, orders):
    bits = bits_of(lax.axis_size("dp"))
    held = [b.reshape((1,) * bits + b.shape) for b in blocks]
    for step in range(bits):
        got = [swap_dp(h, order[step]) for h, order in zip(held, orders)]
        held = [
            jnp.concatenate([h, g], axis=order[step]) for h, g, order in zip(held, got, orders)
        ]
    return [h.reshape((-1, h.shape[-1])) for h in held]


def scatter_xor(arrays, orders):
    size = lax.axis_size("dp")
    bits = bits_of(size)
    held = [a.reshape((2,) * bits + (a.shape[0] // size, a.shape[1])) for a in arrays]
    for step in range(bits):
        sent = [
            swap_dp(lax.slice_in_dim(h, 1, 2, axis=order[step]).astype(bf16), order[step])
            for h, order in zip(held, orders)
        ]
        held = [
            lax.slice_in_dim(h, 0, 1, axis=order[step]) + s.astype(f32)
            for h, s, order in zip(held, sent, orders)
        ]
    return [h.reshape(h.shape[-2:]) for h in held]


def gather_orders(bits):
    high = list(range(bits - 1, 1, -1))
    return (high + [1, 0], [1] + high + [0])


def scatter_orders(bits):
    low = list(range(2, bits))
    return ([0, 1] + low, [0] + low + [1])


def all_sum(value):
    for bit in range(bits_of(lax.axis_size("dp"))):
        value = value + swap_dp(value, bit)
    return value + swap_mp(value)


NN=(((1,),(0,)),((),())); NT=(((1,),(1,)),((),())); TN=(((0,),(0,)),((),()))
def mm(a,b,dims=NN): return lax.dot_general(a,b,dims,preferred_element_type=f32)

def attention_forward_kernel(chunk, q_ref, k_ref, v_ref, o_ref, log_ref, vt_ref):
    vt_ref[...] = v_ref[...].T
    keys = k_ref[...]
    low = lax.broadcasted_iota(jnp.int32, (chunk, 2 * HD), 1) < HD
    for start in range(0, SEQ, chunk):
        rows = pl.ds(start, chunk)
        q = q_ref[rows, :] * jnp.asarray(HD**-0.5, bf16)
        zero = jnp.zeros_like(q)
        mixed = []
        for head in range(2):
            own = jnp.where(low if head == 0 else ~low, q, zero)
            s = mm(keys, own, NT)
            peak = jnp.max(s, axis=0, keepdims=True)
            e = jnp.exp(s - peak)
            total = jnp.sum(e, axis=0, keepdims=True)
            part = mm(vt_ref[head * HD : (head + 1) * HD, :], e.astype(bf16))
            mixed.append(part * (1.0 / total))
            log_ref[0, head : head + 1, rows] = peak + jnp.log(total)
        o_ref[rows, :] = jnp.concatenate(mixed, axis=0).T.astype(bf16)

def attention_forward(q, k, v, chunk=256):
    width = q.shape[1]
    pairs = width // (2 * HD)
    block = pl.BlockSpec((SEQ, 2 * HD), lambda i: (0, i))
    return pl.pallas_call(
        functools.partial(attention_forward_kernel, chunk),
        grid=(pairs,),
        in_specs=[block] * 3,
        out_specs=[block, pl.BlockSpec((1, 2, SEQ), lambda i: (i, 0, 0))],
        out_shape=[jax.ShapeDtypeStruct((SEQ, width), bf16), jax.ShapeDtypeStruct((pairs, 2, SEQ), f32)],
        scratch_shapes=[pltpu.VMEM((2 * HD, SEQ), bf16)],
        compiler_params=pltpu.CompilerParams(vmem_limit_bytes=48 << 20),
        name="attend",
    )(q, k, v)

def attention_backward_kernel(chunk, q_ref, k_ref, v_ref, o_ref, go_ref, log_ref, gq_ref, gk_ref, gv_ref, kt_ref, sk_ref, sv_ref):
    kt_ref[...] = k_ref[...].T
    keys = k_ref[...]
    values = v_ref[...]
    low = lax.broadcasted_iota(jnp.int32, (chunk, 2 * HD), 1) < HD
    scale = HD**-0.5
    for start in range(0, SEQ, chunk):
        rows = pl.ds(start, chunk)
        q = q_ref[rows, :] * jnp.asarray(scale, bf16)
        go = go_ref[rows, :]
        product = (go.astype(f32) * o_ref[rows, :].astype(f32)).T
        zero = jnp.zeros_like(q)
        grads = []
        key_sum = None
        for head in range(2):
            here = low if head == 0 else ~low
            own = jnp.where(here, q, zero)
            own_go = jnp.where(here, go, zero)
            inner = jnp.sum(product[head * HD : (head + 1) * HD, :], axis=0, keepdims=True)
            p = jnp.exp(mm(keys, own, NT) - log_ref[0, head : head + 1, rows])
            gp = mm(values, own_go, NT)
            gs = (p * (gp - inner)).astype(bf16)
            gk = mm(gs, own)
            gv = mm(p.astype(bf16), own_go)
            key_sum = (gk, gv) if head == 0 else (key_sum[0] + gk, key_sum[1] + gv)
            grads.append(mm(kt_ref[head * HD : (head + 1) * HD, :], gs))
        gq_ref[rows, :] = (jnp.concatenate(grads, axis=0).T * scale).astype(bf16)
        if start == 0:
            sk_ref[...] = key_sum[0]
            sv_ref[...] = key_sum[1]
        elif start + chunk < SEQ:
            sk_ref[...] += key_sum[0]
            sv_ref[...] += key_sum[1]
        else:
            gk_ref[...] = (sk_ref[...] + key_sum[0]).astype(bf16)
            gv_ref[...] = (sv_ref[...] + key_sum[1]).astype(bf16)

def attention_backward(q, k, v, o, go, log_total, chunk=256):
    width = q.shape[1]
    pairs = width // (2 * HD)
    block = pl.BlockSpec((SEQ, 2 * HD), lambda i: (0, i))
    return pl.pallas_call(
        functools.partial(attention_backward_kernel, chunk),
        grid=(pairs,),
        in_specs=[block] * 5 + [pl.BlockSpec((1, 2, SEQ), lambda i: (i, 0, 0))],
        out_specs=[block] * 3,
        out_shape=[jax.ShapeDtypeStruct((SEQ, width), bf16)] * 3,
        scratch_shapes=[pltpu.VMEM((2 * HD, SEQ), bf16), pltpu.VMEM((SEQ, 2 * HD), f32), pltpu.VMEM((SEQ, 2 * HD), f32)],
        compiler_params=pltpu.CompilerParams(vmem_limit_bytes=48 << 20),
        name="attend_back",
    )(q, k, v, o, go, log_total)


VMEM_LIMIT = 56 << 20
LO = 128


def normed_of(hidden):
    centred = hidden - jnp.mean(hidden, axis=-1, keepdims=True)
    spread = jnp.mean(centred * centred, axis=-1, keepdims=True)
    inverse = lax.rsqrt(spread + norm_epsilon)
    return centred * inverse, inverse


def norm_pull(grad, unit, inverse, gain):
    scaled = grad * gain
    return inverse * (
        scaled
        - jnp.mean(scaled, axis=-1, keepdims=True)
        - unit * jnp.mean(scaled * unit, axis=-1, keepdims=True)
    )


def lanes(rows, columns):
    return lax.broadcasted_iota(jnp.int32, (rows, columns), 1)


def enter_kernel(
    patch, cdim, flag_ref, code_ref, patches_ref, book_ref, small_ref, qkv_a_ref, qkv_b_ref,
    hidden_ref, looked_ref, q_ref, k_ref, v_ref, gains_ref,
):
    step = pl.program_id(0)
    tokens = code_ref.shape[0]
    half = qkv_a_ref.shape[1] // 3

    @pl.when(step == 0)
    def _():
        turned = small_ref[:, 128:].astype(f32).T
        first = patch + cdim - 128
        digits = [
            jnp.sum(turned[first + 3 + i : first + 4 + i, :], axis=1, keepdims=True) for i in range(3)
        ]
        count = digits[0] + 256.0 * digits[1] + 65536.0 * digits[2]
        gains_ref[...] = jnp.zeros_like(gains_ref)
        gains_ref[0:3, :] = turned[first : first + 3, :]
        gains_ref[3:4, :] = jnp.broadcast_to(count, (1, gains_ref.shape[1]))

    code = code_ref[...]
    low, high = code & (LO - 1), code // LO
    onehot = (lanes(tokens, LO) == low).astype(bf16)
    spread = mm(onehot, book_ref[...])
    group = lanes(tokens, 128) // cdim
    per = 128 // cdim
    picked = jnp.zeros((tokens, 128), f32)
    for i in range(spread.shape[1] // 128):
        picked += jnp.where(group + i * per == high, spread[:, i * 128 : (i + 1) * 128], 0.0)
    fold = (
        lax.broadcasted_iota(jnp.int32, (128, 256), 0) % cdim + patch == lanes(128, 256)
    ) & (lanes(128, 256) < patch + cdim)
    looked = mm(picked.astype(bf16), fold.astype(bf16)).astype(bf16)
    looked_ref[...] = looked
    encoder = flag_ref[0] == 0
    entered = jnp.where(encoder, patches_ref[...].astype(f32), looked.astype(f32)).astype(bf16)
    hidden = mm(entered, small_ref[...], NT)
    hidden_ref[...] = hidden
    unit, _ = normed_of(hidden)
    normed = (unit * gains_ref[0:1, :]).astype(bf16)
    got_a = mm(normed, qkv_a_ref[...]).astype(bf16)
    got_b = mm(normed, qkv_b_ref[...]).astype(bf16)
    for i, ref in enumerate((q_ref, k_ref, v_ref)):
        ref[:, :half] = got_a[:, i * half : (i + 1) * half]
        ref[:, half:] = got_b[:, i * half : (i + 1) * half]


def whole(array):
    return pl.BlockSpec(memory_space=pltpu.VMEM)


SCALAR = pl.BlockSpec(memory_space=pltpu.SMEM)


def rows_of(block, width):
    return pl.BlockSpec((block, width), lambda i: (i, 0))


def fixed(shape):
    return pl.BlockSpec(shape, lambda i: (0,) * len(shape))


def enter(flag, code, patches, book, small, qkv_a, qkv_b, patch, cdim, block=256):
    width = small.shape[0]
    sd = jax.ShapeDtypeStruct
    return pl.pallas_call(
        functools.partial(enter_kernel, patch, cdim),
        grid=(SEQ // block,),
        in_specs=[SCALAR, rows_of(block, 1), rows_of(block, 256)] + [whole(None)] * 4,
        out_specs=[rows_of(block, width), rows_of(block, 256)]
        + [rows_of(block, width)] * 3
        + [fixed((8, width))],
        out_shape=[sd((SEQ, width), f32), sd((SEQ, 256), bf16)]
        + [sd((SEQ, width), bf16)] * 3
        + [sd((8, width), f32)],
        compiler_params=pltpu.CompilerParams(vmem_limit_bytes=VMEM_LIMIT),
        name="enter",
    )(flag, code, patches, book, small, qkv_a, qkv_b)


GELU_A, GELU_B = 0.7978845608028654, 0.044715


def middle_kernel(
    patch, cdim, flag_ref, mixed_ref, hidden_ref, patches_ref, looked_ref, valid_ref,
    rest_a_ref, rest_b_ref, small_ref, gains_ref,
    go_ref, gm_ref, latent_ref, grad_a_ref, grad_b_ref, grad_small_ref, stat_ref,
    active_ref, gbefore_ref, low_t_ref, two_t_ref, branch_t_ref, final_t_ref, head_ref,
):
    step = pl.program_id(0)
    tokens = hidden_ref.shape[0]
    half = mixed_ref.shape[1] // 2
    units = (rest_a_ref.shape[1] - half) // 2
    rows = pl.ds(pl.multiple_of(step * tokens, tokens), tokens)
    encoder = flag_ref[0] == 0
    rests = (rest_a_ref, rest_b_ref)
    up, down = slice(half, half + units), slice(half + units, half + 2 * units)

    @pl.when(step == 0)
    def _():
        stat_ref[...] = jnp.zeros_like(stat_ref)

    gain_two, gain_final = gains_ref[1:2, :], gains_ref[2:3, :]
    mixed = mixed_ref[rows, :]
    middle = hidden_ref[...]
    for i, ref in enumerate(rests):
        middle += mm(mixed[:, i * half : (i + 1) * half], ref[:, :half], NT)
    unit_two, inverse_two = normed_of(middle)
    two = (unit_two * gain_two).astype(bf16)
    two_t_ref[:, rows] = two.T
    slopes = []
    for i, ref in enumerate(rests):
        before = mm(two, ref[:, up])
        square = before * before
        bent = jnp.tanh(GELU_A * before * (1.0 + GELU_B * square))
        active = (0.5 * before * (1.0 + bent)).astype(bf16)
        slopes.append(
            0.5 * (1.0 + bent)
            + (0.5 * GELU_A) * before * (1.0 - bent * bent) * (1.0 + 3.0 * GELU_B * square)
        )
        active_ref[rows, i * units : (i + 1) * units] = active

    @pl.when(step >= 0)
    def _():
        total = middle
        for i, ref in enumerate(rests):
            total += mm(active_ref[rows, i * units : (i + 1) * units], ref[:, down], NT)
        gm_ref[...] = total

    result = gm_ref[...]
    unit, inverse = normed_of(result)
    final = (unit * gain_final).astype(bf16)
    final_t_ref[:, rows] = final.T
    out = mm(final, small_ref[...])
    lane = lanes(tokens, 256)
    is_code = (lane >= patch) & (lane < patch + cdim)
    count = gains_ref[3:4, 0:1]
    patches = patches_ref[...].astype(f32)
    looked = looked_ref[...].astype(f32)
    valid = valid_ref[...].astype(f32)
    gap = jnp.where(lane < patch, out - patches, 0.0)
    root = jnp.sqrt(gap * gap + 1.0)
    g_out = valid * (2.0 * gap + gap / root) / count
    raw = jnp.where(is_code, out, 0.0)
    shrink = lax.rsqrt(jnp.sum(raw * raw, axis=-1, keepdims=True) + 1.0)
    latent = raw * shrink
    away = latent - looked
    g_latent = (2.0 * commit_weight) * away / count
    g_raw = shrink * (g_latent - latent * jnp.sum(g_latent * latent, axis=-1, keepdims=True))
    losses = jnp.where(
        encoder, commit_weight * away * away, valid * (gap * gap + root - 1.0)
    )
    stat_ref[3:4, 0:256] += jnp.sum(losses, axis=0, keepdims=True)
    start = patch // 128 * 128
    latent_ref[...] = latent[:, start : start + 128].T[patch - start : patch - start + cdim, :]
    g_head = jnp.where(encoder, jnp.where(is_code, g_raw, 0.0), jnp.where(lane < patch, g_out, 0.0)).astype(bf16)
    head_ref[rows, :] = g_head
    g_final = mm(g_head, small_ref[...], NT)
    stat_ref[2:3, :] += jnp.sum(g_final * unit, axis=0, keepdims=True)
    g_result = norm_pull(g_final, unit, inverse, gain_final)

    low = g_result.astype(bf16)
    low_t_ref[:, rows] = low.T
    g_two = None
    for i, ref in enumerate(rests):
        g_before = (mm(low, ref[:, down]) * slopes[i]).astype(bf16)
        gbefore_ref[rows, i * units : (i + 1) * units] = g_before
        part = mm(g_before, ref[:, up], NT)
        g_two = part if g_two is None else g_two + part
    stat_ref[1:2, :] += jnp.sum(g_two * unit_two, axis=0, keepdims=True)
    g_middle = g_result + norm_pull(g_two, unit_two, inverse_two, gain_two)
    gm_ref[...] = g_middle
    branch = g_middle.astype(bf16)
    branch_t_ref[:, rows] = branch.T
    for i, ref in enumerate(rests):
        go_ref[:, i * half : (i + 1) * half] = mm(branch, ref[:, :half]).astype(bf16)

    @pl.when(step == pl.num_programs(0) - 1)
    def _():
        grad_small_ref[...] = mm(final_t_ref[...], head_ref[...])
        for i, ref in enumerate((grad_a_ref, grad_b_ref)):
            ref[:, :half] = mm(branch_t_ref[...], mixed_ref[:, i * half : (i + 1) * half]).astype(bf16)
            for at in range(0, units, 512):
                columns = slice(i * units + at, i * units + at + 512)
                ref[:, half + at : half + at + 512] = mm(two_t_ref[...], gbefore_ref[:, columns]).astype(bf16)
                ref[:, half + units + at : half + units + at + 512] = mm(
                    low_t_ref[...], active_ref[:, columns]
                ).astype(bf16)


def middle(flag, mixed, hidden, patches, looked, valid, rest_a, rest_b, small, gains, patch, cdim, block=256):
    width = small.shape[0]
    half = mixed.shape[1] // 2
    hiddens = rest_a.shape[1] - half
    sd = jax.ShapeDtypeStruct
    return pl.pallas_call(
        functools.partial(middle_kernel, patch, cdim),
        grid=(SEQ // block,),
        in_specs=[SCALAR, whole(None), rows_of(block, width)]
        + [rows_of(block, 256)] * 3
        + [whole(None)] * 4,
        out_specs=[
            rows_of(block, 2 * half),
            rows_of(block, width),
            pl.BlockSpec((cdim, block), lambda i: (0, i)),
            whole(None),
            whole(None),
            whole(None),
            whole(None),
        ],
        out_shape=[
            sd((SEQ, 2 * half), bf16),
            sd((SEQ, width), f32),
            sd((cdim, SEQ), f32),
            sd(rest_a.shape, bf16),
            sd(rest_a.shape, bf16),
            sd((width, 256), f32),
            sd((8, width), f32),
        ],
        scratch_shapes=[
            pltpu.VMEM((SEQ, hiddens), bf16),
            pltpu.VMEM((SEQ, hiddens), bf16),
            pltpu.VMEM((width, SEQ), bf16),
            pltpu.VMEM((width, SEQ), bf16),
            pltpu.VMEM((width, SEQ), bf16),
            pltpu.VMEM((width, SEQ), bf16),
            pltpu.VMEM((SEQ, 256), bf16),
        ],
        compiler_params=pltpu.CompilerParams(vmem_limit_bytes=VMEM_LIMIT),
        name="middle",
    )(flag, mixed, hidden, patches, looked, valid, rest_a, rest_b, small, gains)


def leave_kernel(
    patch, cdim, flag_ref, code_ref, code_row_ref, gq_ref, gk_ref, gv_ref, hidden_ref, gm_ref,
    patches_ref, looked_ref, latent_ref, qkv_a_ref, qkv_b_ref, small_ref, gains_ref,
    head_ref, stat_ref,
    grad_a_ref, grad_b_ref, book_ref,
    normed_t_ref, gin_t_ref, entered_ref, gain_ref, sum_ref,
):
    step = pl.program_id(0)
    tokens = hidden_ref.shape[0]
    half = gq_ref.shape[1] // 2
    rows = pl.ds(pl.multiple_of(step * tokens, tokens), tokens)
    encoder = flag_ref[0] == 0
    grads = (gq_ref, gk_ref, gv_ref)

    @pl.when(step == 0)
    def _():
        gain_ref[...] = jnp.zeros_like(gain_ref)
        sum_ref[...] = jnp.zeros_like(sum_ref)

    gain = gains_ref[0:1, :]
    unit, inverse = normed_of(hidden_ref[...])
    normed_t_ref[:, rows] = (unit * gain).astype(bf16).T
    g_normed = None
    for i, ref in enumerate((qkv_a_ref, qkv_b_ref)):
        together = jnp.concatenate([g[rows, i * half : (i + 1) * half] for g in grads], axis=1)
        part = mm(together, ref[...], NT)
        g_normed = part if g_normed is None else g_normed + part
    offset = patch + cdim - 128
    gain_ref[offset : offset + 1, :] += jnp.sum(g_normed * unit, axis=0, keepdims=True)
    g_in = (gm_ref[...] + norm_pull(g_normed, unit, inverse, gain)).astype(bf16)
    gin_t_ref[:, rows] = g_in.T
    looked = looked_ref[...]
    entered_ref[rows, :] = jnp.where(encoder, patches_ref[...].astype(f32), looked.astype(f32)).astype(bf16)

    start = patch // 128 * 128
    before, after = patch - start, 128 - (patch - start) - cdim
    pieces = [jnp.zeros((before, tokens), f32)] if before else []
    pieces.append(latent_ref[...])
    pieces += [jnp.zeros((after, tokens), f32)] if after else []
    latent = jnp.concatenate(pieces, axis=0).T
    latent = jnp.concatenate([jnp.zeros((tokens, start), f32), latent], axis=1)
    lane = lanes(tokens, 256)
    is_code = (lane >= patch) & (lane < patch + cdim)
    count = gains_ref[3:4, 0:1]
    g_looked = mm(g_in, small_ref[...]) + (2.0 * commit_weight) * (looked.astype(f32) - latent) / count
    g_looked = jnp.where(encoder | ~is_code, 0.0, g_looked).astype(bf16)
    row = lax.broadcasted_iota(jnp.int32, (256, 128), 0)
    tiled = (lanes(256, 128) % cdim + patch == row).astype(bf16)
    copies = mm(g_looked, tiled)
    high = code_ref[...] // LO
    group = lanes(tokens, 128) // cdim
    per = 128 // cdim
    spread = jnp.concatenate(
        [
            jnp.where(group + i * per == high, copies, 0.0).astype(bf16)
            for i in range(sum_ref.shape[1] // 128)
        ],
        axis=1,
    )
    low_row = code_row_ref[...] & (LO - 1)
    onehot = (lax.broadcasted_iota(jnp.int32, (LO, tokens), 0) == low_row).astype(bf16)
    sum_ref[...] += mm(onehot, spread)

    @pl.when(step == pl.num_programs(0) - 1)
    def _():
        book_ref[...] = sum_ref[...].astype(bf16)
        gain_ref[offset + 1 : offset + 3, :] = stat_ref[1:3, :]
        wide = 3 * half
        for i, ref in enumerate((grad_a_ref, grad_b_ref)):
            for j, g in enumerate(grads):
                ref[:, j * half : (j + 1) * half] = mm(
                    normed_t_ref[...], g[:, i * half : (i + 1) * half]
                ).astype(bf16)
        thin = head_ref[...] + mm(gin_t_ref[...], entered_ref[...])
        grad_a_ref[:, wide : wide + 128] = thin[:, :128].astype(bf16)
        grad_a_ref[:, wide + 128 : wide + 256] = (thin[:, 128:] + gain_ref[...].T).astype(bf16)


def leave(flag, code, code_row, gq, gk, gv, hidden, gm, patches, looked, latent, qkv_a, qkv_b, small, gains, head, stat, patch, cdim, book_width, block=256):
    width = small.shape[0]
    wide = qkv_a.shape[1]
    sd = jax.ShapeDtypeStruct
    return pl.pallas_call(
        functools.partial(leave_kernel, patch, cdim),
        grid=(SEQ // block,),
        in_specs=[SCALAR, rows_of(block, 1), pl.BlockSpec((1, block), lambda i: (0, i))]
        + [whole(None)] * 3
        + [rows_of(block, width)] * 2
        + [rows_of(block, 256)] * 2
        + [pl.BlockSpec((cdim, block), lambda i: (0, i))]
        + [whole(None)] * 6,
        out_specs=[whole(None)] * 3,
        out_shape=[
            sd((width, wide + 256), bf16),
            sd((width, wide), bf16),
            sd((LO, book_width), bf16),
        ],
        scratch_shapes=[
            pltpu.VMEM((width, SEQ), bf16),
            pltpu.VMEM((width, SEQ), bf16),
            pltpu.VMEM((SEQ, 256), bf16),
            pltpu.VMEM((128, width), f32),
            pltpu.VMEM((LO, book_width), f32),
        ],
        compiler_params=pltpu.CompilerParams(vmem_limit_bytes=VMEM_LIMIT),
        name="leave",
    )(flag, code, code_row, gq, gk, gv, hidden, gm, patches, looked, latent, qkv_a, qkv_b, small, gains, head, stat)


def adam_update(master, moment, square, clipped, rate):
    moment_new = first_decay * moment + (1.0 - first_decay) * clipped
    square_new = second_decay * square + (1.0 - second_decay) * clipped * clipped
    moment_hat = moment_new / (1.0 - first_decay**STEP)
    square_hat = square_new / (1.0 - second_decay**STEP)
    updated = master - rate * (
        moment_hat / (jnp.sqrt(square_hat) + adam_epsilon) + weight_decay * master
    )
    return (updated, moment_new, square_new)


def body(
    pixels,
    valid_mask,
    code_index,
    attention_weight,
    attention_moment,
    attention_square,
    feedforward_weight,
    feedforward_moment,
    feedforward_square,
    pixel_weight,
    pixel_moment,
    pixel_square,
    code_weight,
    code_moment,
    code_square,
    codebook,
    codebook_moment,
    codebook_square,
    norm_gains,
    gains_moment,
    gains_square,
):
    side = lax.axis_index("mp")
    place = lax.axis_index("dp")
    parts = lax.axis_size("dp")
    bits = bits_of(parts)
    encoder = side == 0
    rows = attention_weight.shape[2]
    width = rows * parts
    half = attention_weight.shape[3]
    units = feedforward_weight.shape[3]
    patch = pixel_weight.shape[1]
    cdim = code_weight.shape[1]
    codes_here = codebook.shape[0]

    def mine(array):
        return jnp.where(encoder, array[0], array[1])

    def other(array):
        return jnp.where(encoder, array[1], array[0])

    def columns(attention, feedforward):
        qkv = attention[:3].transpose(1, 0, 2).reshape(rows, 3 * half)
        rest = jnp.concatenate([attention[3], feedforward[0], feedforward[1]], axis=1)
        return qkv, rest

    attention_low = attention_weight.astype(bf16)
    feedforward_low = feedforward_weight.astype(bf16)
    qkv_own, rest_own = columns(mine(attention_low), mine(feedforward_low))
    qkv_sent, rest_sent = columns(other(attention_low), other(feedforward_low))
    qkv_got, rest_got = swap_mp(qkv_sent), swap_mp(rest_sent)

    count_here = jnp.sum(valid_mask)
    digits = jnp.stack([count_here & 255, (count_here >> 8) & 255, count_here >> 16])
    digit_rows = jnp.where(lax.iota(jnp.int32, rows)[:, None] == 0, digits[None, :], 0)
    gains_low = norm_gains.astype(bf16).reshape(2, 3, rows)
    small = jnp.concatenate(
        [
            mine(pixel_weight.astype(bf16)).T,
            mine(code_weight.astype(bf16)).T,
            mine(gains_low).T,
            digit_rows.astype(bf16),
            jnp.zeros((rows, 256 - patch - cdim - 6), bf16),
        ],
        axis=1,
    )
    book_rows = codebook.astype(bf16).astype(f32)
    book_unit, book_pull = jax.vjp(unit_norm, book_rows)
    book_block = (
        book_unit.astype(bf16)
        .reshape(codes_here // LO, LO, cdim)
        .transpose(1, 0, 2)
        .reshape(rows, cdim * codes_here // rows)
    )

    order_a, order_b = gather_orders(bits)
    qkv_a, qkv_b, small_all, book_all = gather_xor(
        [qkv_own, qkv_got, small, book_block], [order_a, order_b, order_a, order_b]
    )
    rest_a, rest_b = gather_xor([rest_own, rest_got], [order_a, order_b])

    block = (code_index // codes_here) ^ place
    turned = jnp.zeros_like(block)
    for bit in range(bits):
        turned = turned | (((block >> bit) & 1) << (bits - 1 - bit))
    code_place = turned * codes_here + code_index % codes_here
    per = codes_here // LO
    book_all = book_all.reshape(parts, LO, per * cdim).transpose(1, 0, 2).reshape(LO, -1)
    flag = side.astype(jnp.int32).reshape(1)
    patches = jnp.pad(pixels, ((0, 0), (0, 256 - patch)))
    valid = jnp.pad(valid_mask.astype(bf16), ((0, 0), (0, 256 - patch)))
    code_column, code_row = code_place[:, None], code_place[None, :]

    hidden, looked, q, k, v, gains_all = enter(
        flag, code_column, patches, book_all, small_all, qkv_a, qkv_b, patch, cdim
    )
    mixed, log_total = attention_forward(q, k, v, 1024)
    g_mixed, g_middle, latent, g_rest_a, g_rest_b, g_head, stat = middle(
        flag, mixed, hidden, patches, looked, valid, rest_a, rest_b, small_all, gains_all, patch, cdim
    )
    latent_there = swap_mp(latent)
    loss_here = jnp.sum(stat[3])
    scatter_a, scatter_b = scatter_orders(bits)
    rest_own, rest_sent = scatter_xor([g_rest_a, g_rest_b], [scatter_a, scatter_b])

    gq, gk, gv = attention_backward(q, k, v, mixed, g_mixed, log_total, 512)
    g_qkv_a, g_qkv_b, g_book = leave(
        flag, code_column, code_row, gq, gk, gv, hidden, g_middle, patches, looked, latent_there,
        qkv_a, qkv_b, small_all, gains_all, g_head, stat, patch, cdim, book_all.shape[1],
    )
    g_book = g_book.reshape(LO, parts, per * cdim).transpose(1, 0, 2).reshape(width, -1)
    tail_a, tail_b = scatter_xor(
        [g_qkv_a, jnp.concatenate([g_qkv_b, g_book], axis=1)], [scatter_a, scatter_b]
    )
    qkv_own, small_own = tail_a[:, : 3 * half], tail_a[:, 3 * half :]
    qkv_sent, book_own = tail_b[:, : 3 * half], tail_b[:, 3 * half :]
    book_own = book_own.reshape(LO, per, cdim).transpose(1, 0, 2).reshape(codes_here, cdim)
    book_own = book_pull(book_own)[0].T
    squares_here = sum(
        jnp.sum(a * a) for a in (rest_own, rest_sent, qkv_own, qkv_sent, small_own, book_own)
    )
    rest_got, qkv_got, small_got, book_got = (
        swap_mp(a) for a in (rest_sent, qkv_sent, small_own, book_own)
    )
    totals = all_sum(jnp.stack([squares_here, loss_here]))
    norm_total = jnp.sqrt(totals[0])
    factor = clip_norm / jnp.maximum(norm_total, clip_norm)

    def both(own, got):
        return jnp.stack([jnp.where(encoder, own, got), jnp.where(encoder, got, own)])

    def attention_of(qkv, rest):
        parts_qkv = qkv.reshape(rows, 3, half).transpose(1, 0, 2)
        return jnp.concatenate([parts_qkv, rest[None, :, :half]], axis=0)

    def feedforward_of(rest):
        return rest[:, half:].reshape(rows, 2, units).transpose(1, 0, 2)

    small_t = both(small_own.T, small_got.T)
    book_sum = jnp.where(encoder, book_got, book_own).T
    shards = (
        both(attention_of(qkv_own, rest_own), attention_of(qkv_got, rest_got)),
        both(feedforward_of(rest_own), feedforward_of(rest_got)),
        small_t[:, :patch],
        small_t[:, patch : patch + cdim],
        book_sum,
        small_t[:, patch + cdim : patch + cdim + 3].reshape(6, rows),
    )
    masters = (
        attention_weight,
        feedforward_weight,
        pixel_weight,
        code_weight,
        codebook,
        norm_gains,
    )
    moments = (
        attention_moment,
        feedforward_moment,
        pixel_moment,
        code_moment,
        codebook_moment,
        gains_moment,
    )
    squares = (
        attention_square,
        feedforward_square,
        pixel_square,
        code_square,
        codebook_square,
        gains_square,
    )
    results = []
    for master, moment, square, member, rate in zip(masters, moments, squares, shards, learn_rates):
        results.extend(adam_update(master, moment, square, member * factor, rate))
    return tuple(results) + (totals[1], gains_all[3, 0], norm_total)


def solution(mesh):
    wide = P(None, None, "dp", "mp")
    thin = P(None, None, "dp")
    rows = P("dp", None)
    gain = P(None, "dp")
    weights = (wide,) * 6 + (thin,) * 6 + (rows,) * 3 + (gain,) * 3
    return jax.shard_map(
        body,
        mesh=mesh,
        in_specs=(rows, rows, P("dp")) + weights,
        out_specs=weights + (P(), P(), P()),
        check_vma=False,
    )
```

```python
import functools

import jax
import jax.numpy as jnp
from jax import lax
from jax.experimental import pallas as pl
from jax.experimental.pallas import tpu as pltpu
from jax.sharding import PartitionSpec as P

HD = 64
SEQ = 1024
STEP = 10

norm_epsilon = 1e-05
commit_weight = 0.25
clip_norm = 0.003
learn_rates = (0.2, 0.02, 0.04, 0.5, 0.5, 0.6)
first_decay = 0.9
second_decay = 0.999
weight_decay = 0.01
adam_epsilon = 1e-08

bf16 = jnp.bfloat16
f32 = jnp.float32


def swap_mp(value):
    return lax.ppermute(value, "mp", [(0, 1), (1, 0)])


def bits_of(size):
    return size.bit_length() - 1


def step_orders(bits):
    high = list(range(bits - 1, 1, -1))
    return (high + [1], [1] + high)


def swap_step(value, step):
    size = lax.axis_size("dp")
    orders = step_orders(bits_of(size))
    return lax.ppermute(value, "dp", [(i, i ^ (1 << orders[i & 1][step])) for i in range(size)])


def swap_core(value):
    return lax.ppermute(value, "dp", [(i, i ^ 1) for i in range(lax.axis_size("dp"))])


def place_of(mask, core, bits):
    places = [
        sum(((mask >> bit) & 1) << step for step, bit in enumerate(order))
        for order in step_orders(bits)
    ]
    same = mask & 1 == 0
    return jnp.where(same == (core == 0), places[0], places[1]) + jnp.where(same, 0, 1 << (bits - 1))


def after(value, *others):
    return lax.optimization_barrier((value,) + others)[0]


def together(*arrays):
    return lax.optimization_barrier(arrays)


def widen(held, step):
    return jnp.concatenate([held, swap_step(held, step)], axis=0)


def halves(total):
    split = total.shape[0] // 2
    return together(total[:split], total[split:].astype(bf16))


def fold(pair, step, later=()):
    keep, sent = pair
    got = swap_core(sent) if step is None else swap_step(sent, step)
    if later:
        keep = after(keep, *later)
    return keep.astype(f32) + got.astype(f32)


def all_sum(value):
    size = lax.axis_size("dp")
    for bit in range(bits_of(size)):
        value = value + lax.ppermute(value, "dp", [(i, i ^ (1 << bit)) for i in range(size)])
    return value + swap_mp(value)


NN = (((1,), (0,)), ((), ()))
NT = (((1,), (1,)), ((), ()))
VMEM_LIMIT = 48 << 20
LO = 128


def mm(a, b, dims=NN):
    return lax.dot_general(a, b, dims, preferred_element_type=f32)


def whole():
    return pl.BlockSpec(memory_space=pltpu.VMEM)


def rows_of(block, width):
    return pl.BlockSpec((block, width), lambda i: (i, 0))


def columns_of(height, block):
    return pl.BlockSpec((height, block), lambda i: (0, i))


def call(kernel, name, out, flops=0, nbytes=0, exps=0, limit=VMEM_LIMIT, **kw):
    return pl.pallas_call(
        kernel,
        name=name,
        out_shape=[jax.ShapeDtypeStruct(s, d) for s, d in out],
        compiler_params=pltpu.CompilerParams(vmem_limit_bytes=limit),
        cost_estimate=pl.CostEstimate(flops=flops, bytes_accessed=nbytes, transcendentals=exps),
        **kw,
    )


SCALAR = pl.BlockSpec(memory_space=pltpu.SMEM)


def attend_kernel(q_ref, k_ref, v_ref, o_ref, log_ref, vt_ref):
    vt_ref[...] = v_ref[...].T
    keys = k_ref[...]
    q = q_ref[...] * jnp.asarray(HD**-0.5, bf16)
    low = lax.broadcasted_iota(jnp.int32, q.shape, 1) < HD
    zero = jnp.zeros_like(q)
    mixed = []
    for head in range(2):
        own = jnp.where(low if head == 0 else ~low, q, zero)
        s = mm(keys, own, NT)
        peak = jnp.max(s, axis=0, keepdims=True)
        e = jnp.exp(s - peak)
        total = jnp.sum(e, axis=0, keepdims=True)
        part = mm(vt_ref[head * HD : (head + 1) * HD, :], e.astype(bf16))
        mixed.append(part * (1.0 / total))
        log_ref[0, head : head + 1, :] = peak + jnp.log(total)
    o_ref[...] = jnp.concatenate(mixed, axis=0).T.astype(bf16)


def column_block(at):
    return pl.BlockSpec((SEQ, 2 * HD), lambda i: (0, at + i))


def attend(qkv):
    width = qkv.shape[1] // 3
    pairs = width // (2 * HD)
    return call(
        attend_kernel,
        "attend",
        [((SEQ, width), bf16), ((pairs, 2, SEQ), f32)],
        flops=pairs * 8 * SEQ * SEQ * 256,
        nbytes=8 * SEQ * width,
        limit=28 << 20,
        grid=(pairs,),
        in_specs=[column_block(0), column_block(pairs), column_block(2 * pairs)],
        out_specs=[column_block(0), pl.BlockSpec((1, 2, SEQ), lambda i: (i, 0, 0))],
        scratch_shapes=[pltpu.VMEM((2 * HD, SEQ), bf16)],
    )(qkv, qkv, qkv)


def attend_back_kernel(
    chunk, q_ref, k_ref, v_ref, o_ref, go_ref, log_ref, gq_ref, gk_ref, gv_ref, kt_ref, sk_ref, sv_ref
):
    kt_ref[...] = k_ref[...].T
    keys = k_ref[...]
    values = v_ref[...]
    low = lax.broadcasted_iota(jnp.int32, (chunk, 2 * HD), 1) < HD
    scale = HD**-0.5
    for start in range(0, SEQ, chunk):
        rows = pl.ds(start, chunk)
        q = q_ref[rows, :] * jnp.asarray(scale, bf16)
        go = go_ref[rows, :]
        product = (go.astype(f32) * o_ref[rows, :].astype(f32)).T
        zero = jnp.zeros_like(q)
        grads = []
        sums = None
        for head in range(2):
            here = low if head == 0 else ~low
            own = jnp.where(here, q, zero)
            own_go = jnp.where(here, go, zero)
            inner = jnp.sum(product[head * HD : (head + 1) * HD, :], axis=0, keepdims=True)
            p = jnp.exp(mm(keys, own, NT) - log_ref[0, head : head + 1, rows])
            gp = mm(values, own_go, NT)
            gs = (p * (gp - inner)).astype(bf16)
            gk = mm(gs, own)
            gv = mm(p.astype(bf16), own_go)
            sums = (gk, gv) if head == 0 else (sums[0] + gk, sums[1] + gv)
            grads.append(mm(kt_ref[head * HD : (head + 1) * HD, :], gs))
        gq_ref[rows, :] = (jnp.concatenate(grads, axis=0).T * scale).astype(bf16)
        if start == 0:
            sk_ref[...] = sums[0]
            sv_ref[...] = sums[1]
        elif start + chunk < SEQ:
            sk_ref[...] += sums[0]
            sv_ref[...] += sums[1]
        else:
            gk_ref[...] = (sk_ref[...] + sums[0]).astype(bf16)
            gv_ref[...] = (sv_ref[...] + sums[1]).astype(bf16)


def attend_back(qkv, o, go, log_total, pair, chunk=512):
    pairs = o.shape[1] // (2 * HD)
    return call(
        functools.partial(attend_back_kernel, chunk),
        "attend_back",
        [((SEQ, 2 * HD), bf16)] * 3,
        flops=20 * SEQ * SEQ * 256,
        nbytes=16 * SEQ * 128,
        limit=28 << 20,
        grid=(1,),
        in_specs=[
            column_block(pair),
            column_block(pairs + pair),
            column_block(2 * pairs + pair),
            column_block(pair),
            column_block(pair),
            pl.BlockSpec((1, 2, SEQ), lambda i: (pair, 0, 0)),
        ],
        out_specs=[column_block(0)] * 3,
        scratch_shapes=[
            pltpu.VMEM((2 * HD, SEQ), bf16),
            pltpu.VMEM((SEQ, 2 * HD), f32),
            pltpu.VMEM((SEQ, 2 * HD), f32),
        ],
    )(qkv, qkv, qkv, o, go, log_total)


def lanes(rows, columns):
    return lax.broadcasted_iota(jnp.int32, (rows, columns), 1)


def normed_of(hidden):
    centred = hidden - jnp.mean(hidden, axis=-1, keepdims=True)
    spread = jnp.mean(centred * centred, axis=-1, keepdims=True)
    inverse = lax.rsqrt(spread + norm_epsilon)
    return centred * inverse, inverse


def norm_pull(grad, unit, inverse, gain):
    scaled = grad * gain
    return inverse * (
        scaled
        - jnp.mean(scaled, axis=-1, keepdims=True)
        - unit * jnp.mean(scaled * unit, axis=-1, keepdims=True)
    )


def by_two(value, low_ref, high_ref, columns=slice(None)):
    split = low_ref.shape[0]
    return mm(value[:, :split], low_ref[:, columns]) + mm(value[:, split:], high_ref[:, columns])


def to_two(value, low_ref, high_ref, columns=slice(None)):
    return jnp.concatenate(
        [mm(value, low_ref[:, columns], NT), mm(value, high_ref[:, columns], NT)], axis=1
    )


def pack_first_kernel(
    side_ref, attention_ref, pixel_ref, code_ref, book_ref, gains_ref, valid_ref,
    own_ref, sent_ref, turn_ref,
):
    side = side_ref[0]
    rows, half = attention_ref.shape[2], attention_ref.shape[3]
    patch, cdim = pixel_ref.shape[2], code_ref.shape[1]
    for j in range(3):
        own_ref[:, j * half : (j + 1) * half] = attention_ref[side, j].astype(bf16)
        sent_ref[:, j * half : (j + 1) * half] = attention_ref[1 - side, j].astype(bf16)
    count = jnp.sum(valid_ref[...], axis=0, keepdims=True)
    count = jnp.sum(count.astype(f32), axis=1, keepdims=True).astype(jnp.int32)
    at = 3 * half
    first = patch - 128
    turn_ref[...] = jnp.zeros_like(turn_ref)
    turn_ref[first : first + cdim, 0:rows] = code_ref[side]
    first += cdim
    turn_ref[first : first + 3, 0:rows] = jnp.where(side == 0, gains_ref[0:3, :], gains_ref[3:6, :])
    digits = (count & 255, (count >> 8) & 255, count >> 16)
    for i, digit in enumerate(digits):
        turn_ref[first + 3 + i : first + 4 + i, 0:1] = digit.astype(f32)
    own_ref[:, at + 128 : at + 256] = turn_ref[...].T[0:rows, :].astype(bf16)
    own_ref[:, at : at + patch] = pixel_ref[side].astype(bf16)
    at += 256
    book = book_ref[...].astype(bf16).astype(f32)
    unit = book * lax.rsqrt(jnp.sum(book * book, axis=0, keepdims=True) + 1.0)
    per = book.shape[1] // LO
    tall = jnp.concatenate([unit[:, i * LO : (i + 1) * LO] for i in range(per)], axis=0)
    if per * cdim < 128:
        tall = jnp.concatenate([tall, jnp.zeros((128 - per * cdim, LO), f32)], axis=0)
    wide = tall.T
    step = per * cdim
    for j in range(LO // rows):
        own_ref[:, at + j * step : at + (j + 1) * step] = wide[
            j * rows : (j + 1) * rows, :step
        ].astype(bf16)


def pack_first(side, attention, pixel_t, code, book_t, gains, valid_t):
    _, _, rows, half = attention.shape
    cdim, codes = book_t.shape
    return call(
        pack_first_kernel,
        "pack_first",
        [((rows, 3 * half + 256 + cdim * codes // rows), bf16), ((rows, 3 * half), bf16)],
        nbytes=2 << 20,
        limit=12 << 20,
        in_specs=[SCALAR] + [whole()] * 6,
        out_specs=[whole()] * 2,
        scratch_shapes=[pltpu.VMEM((128, 128), f32)],
    )(side, attention, pixel_t, code, book_t, gains, valid_t)


def pack_rest_kernel(
    side_ref, attention_ref, feedforward_ref, pixels_ref, valid_ref, code_ref,
    own_ref, sent_ref, patches_ref, mask_ref, column_ref,
):
    side = side_ref[0]
    half, units = attention_ref.shape[3], feedforward_ref.shape[3]
    for ref, which in ((own_ref, side), (sent_ref, 1 - side)):
        ref[:, :half] = attention_ref[which, 3].astype(bf16)
        ref[:, half : half + units] = feedforward_ref[which, 0].astype(bf16)
        ref[:, half + units :] = feedforward_ref[which, 1].astype(bf16)
    patch, tokens = pixels_ref.shape
    zeros = jnp.zeros((256 - patch, tokens), f32)
    patches_ref[...] = jnp.concatenate([pixels_ref[...].astype(f32), zeros], axis=0).T.astype(bf16)
    mask_ref[...] = jnp.concatenate([valid_ref[...].astype(f32), zeros], axis=0).T.astype(bf16)
    column_ref[...] = jnp.broadcast_to(code_ref[...].astype(f32), (128, tokens)).T.astype(jnp.int32)


def pack_rest(side, attention, feedforward, pixels_t, valid_t, code_row):
    rows, half = attention.shape[2:]
    units = feedforward.shape[3]
    return call(
        pack_rest_kernel,
        "pack_rest",
        [((rows, half + 2 * units), bf16)] * 2
        + [((SEQ, 256), bf16)] * 2
        + [((SEQ, 128), jnp.int32)],
        nbytes=5 << 20,
        limit=16 << 20,
        in_specs=[SCALAR] + [whole()] * 5,
        out_specs=[whole()] * 5,
    )(side, attention, feedforward, pixels_t, valid_t, code_row)


def enter_kernel(
    patch, cdim, aligned, side_ref, code_ref, patches_ref, low_a_ref, high_a_ref, low_b_ref, high_b_ref,
    *refs,
):
    if aligned:
        hidden_ref, looked_ref, qkv_a_ref, qkv_b_ref, normed_t_ref, gains_ref, book_ref = refs
    else:
        book_ref, hidden_ref, looked_ref, qkv_a_ref, qkv_b_ref, normed_t_ref, gains_ref = refs
    step = pl.program_id(0)
    tokens = code_ref.shape[0]
    wide = low_b_ref.shape[1]
    split = low_a_ref.shape[0]
    thin = slice(wide, wide + 256)

    @pl.when(step == 0)
    def _():
        first = patch + cdim - 128
        gains_ref[...] = jnp.zeros_like(gains_ref)
        digits = 0.0
        for i, ref in enumerate((low_a_ref, high_a_ref)):
            turned = ref[:, wide + 128 : wide + 256].astype(f32).T
            gains_ref[0:3, i * split : (i + 1) * split] = turned[first : first + 3, :]
            digits += jnp.sum(turned, axis=1, keepdims=True)
        count = (
            digits[first + 3 : first + 4]
            + 256.0 * digits[first + 4 : first + 5]
            + 65536.0 * digits[first + 5 : first + 6]
        )
        gains_ref[3:4, :] = jnp.broadcast_to(count, (1, gains_ref.shape[1]))
        if aligned:
            rows = aligned
            for i, ref in enumerate((low_a_ref, high_a_ref)):
                blocks = split // rows
                for b in range(blocks):
                    at = (i * blocks + b) * 128
                    for j in range(LO // rows):
                        column = wide + 256 + j * 128
                        book_ref[j * rows : (j + 1) * rows, at : at + 128] = ref[
                            b * rows : (b + 1) * rows, column : column + 128
                        ]

    code = code_ref[...]
    low, high = code & (LO - 1), code // LO
    lane = lanes(tokens, 128)
    onehot = jnp.where(lane == low, 1.0, 0.0).astype(bf16)
    spread = mm(onehot, book_ref[...])
    group = lane // cdim
    per = 128 // cdim
    away = high - group
    picked = jnp.zeros((tokens, 128), f32)
    for i in range(spread.shape[1] // 128):
        picked += jnp.where(away == i * per, spread[:, i * 128 : (i + 1) * 128], 0.0)
    lane_out = lanes(128, 256)
    fold_in = (
        lax.broadcasted_iota(jnp.int32, (128, 256), 0) % cdim + patch == lane_out
    ) & (lane_out < patch + cdim)
    looked = mm(picked.astype(bf16), jnp.where(fold_in, 1.0, 0.0).astype(bf16)).astype(bf16)
    looked_ref[...] = looked
    encoder = side_ref[0] == 0
    entered = jnp.where(encoder, patches_ref[...].astype(f32), looked.astype(f32)).astype(bf16)
    hidden = to_two(entered, low_a_ref, high_a_ref, thin)
    hidden_ref[...] = hidden
    unit, _ = normed_of(hidden)
    normed = (unit * gains_ref[0:1, :]).astype(bf16)
    normed_t_ref[...] = normed.T
    qkv_a_ref[...] = by_two(normed, low_a_ref, high_a_ref, slice(0, wide)).astype(bf16)
    qkv_b_ref[...] = by_two(normed, low_b_ref, high_b_ref).astype(bf16)


def enter(side, code, patches, a, b, book, aligned, patch, cdim, codes, block=256):
    width = 2 * a[0].shape[0]
    wide = b[0].shape[1]
    table = (LO, codes // LO * cdim)
    return call(
        functools.partial(enter_kernel, patch, cdim, aligned),
        "enter",
        [
            ((SEQ, width), f32),
            ((SEQ, 256), bf16),
            ((SEQ, wide), bf16),
            ((SEQ, wide), bf16),
            ((width, SEQ), bf16),
            ((8, width), f32),
        ],
        flops=8 << 30,
        nbytes=12 << 20,
        limit=28 << 20,
        grid=(SEQ // block,),
        in_specs=[SCALAR, rows_of(block, 128), rows_of(block, 256)]
        + [whole()] * (4 if aligned else 5),
        out_specs=[
            rows_of(block, width),
            rows_of(block, 256),
            rows_of(block, wide),
            rows_of(block, wide),
            columns_of(width, block),
            pl.BlockSpec((8, width), lambda i: (0, 0)),
        ],
        scratch_shapes=[pltpu.VMEM(table, bf16)] if aligned else [],
    )(side, code, patches, *a, *b, *([] if aligned else [book]))


GELU_A, GELU_B = 0.7978845608028654, 0.044715


def middle_kernel(
    patch, cdim, side_ref, mixed_a_ref, mixed_b_ref, hidden_ref, patches_ref, looked_ref, valid_ref,
    low_ref, high_ref, thin_low_ref, thin_high_ref, gains_ref,
    go_a_ref, go_b_ref, gm_ref, latent_ref, keep_ref, sent_ref,
    head_grad_ref, stat_ref,
    active_ref, gbefore_ref, low_t_ref, two_t_ref, branch_t_ref, final_t_ref, head_ref,
    full_a_ref, full_b_ref, thin_ref, copy_sem,
):
    step = pl.program_id(0)
    tokens = hidden_ref.shape[0]
    half = mixed_a_ref.shape[1]
    units = (low_ref.shape[1] // 2 - half) // 2
    rows = pl.ds(pl.multiple_of(step * tokens, tokens), tokens)
    encoder = side_ref[0] == 0
    rests = (full_a_ref, full_b_ref)
    mixeds = (mixed_a_ref, mixed_b_ref)
    out, up, down = slice(0, half), slice(half, half + units), slice(half + units, half + 2 * units)

    @pl.when(step == 0)
    def _():
        stat_ref[...] = jnp.zeros_like(stat_ref)
        split = low_ref.shape[0]
        each = half + 2 * units
        copies = [
            pltpu.make_async_copy(
                piece.at[:, pl.ds(i * each, each)],
                rests[i].at[pl.ds(j * split, split), :],
                copy_sem.at[2 * i + j],
            )
            for i in range(2)
            for j, piece in enumerate((low_ref, high_ref))
        ]
        for copy in copies:
            copy.start()
        thin_ref[:split, :] = thin_low_ref[...]
        thin_ref[split:, :] = thin_high_ref[...]
        for copy in copies:
            copy.wait()

    gain_two, gain_final = gains_ref[1:2, :], gains_ref[2:3, :]
    middle = hidden_ref[...]
    for ref, rest in zip(mixeds, rests):
        middle += mm(ref[rows, :], rest[:, out], NT)
    unit_two, inverse_two = normed_of(middle)
    two = (unit_two * gain_two).astype(bf16)
    two_t_ref[:, rows] = two.T
    slopes = []
    for i, rest in enumerate(rests):
        before = mm(two, rest[:, up])
        square = before * before
        bent = jnp.tanh(GELU_A * before * (1.0 + GELU_B * square))
        active_ref[rows, i * units : (i + 1) * units] = (0.5 * before * (1.0 + bent)).astype(bf16)
        slopes.append(
            0.5 * (1.0 + bent)
            + (0.5 * GELU_A) * before * (1.0 - bent * bent) * (1.0 + 3.0 * GELU_B * square)
        )

    @pl.when(step >= 0)
    def _():
        total = middle
        for i, rest in enumerate(rests):
            total += mm(active_ref[rows, i * units : (i + 1) * units], rest[:, down], NT)
        gm_ref[...] = total

    result = gm_ref[...]
    unit, inverse = normed_of(result)
    final = (unit * gain_final).astype(bf16)
    final_t_ref[:, rows] = final.T
    seen = mm(final, thin_ref[...])
    lane = lanes(tokens, 256)
    is_code = (lane >= patch) & (lane < patch + cdim)
    count = gains_ref[3:4, 0:1]
    patches = patches_ref[...].astype(f32)
    looked = looked_ref[...].astype(f32)
    valid = valid_ref[...].astype(f32)
    gap = jnp.where(lane < patch, seen - patches, 0.0)
    root = jnp.sqrt(gap * gap + 1.0)
    g_out = valid * (2.0 * gap + gap / root) / count
    raw = jnp.where(is_code, seen, 0.0)
    shrink = lax.rsqrt(jnp.sum(raw * raw, axis=-1, keepdims=True) + 1.0)
    latent = raw * shrink
    away = latent - looked
    g_latent = (2.0 * commit_weight) * away / count
    g_raw = shrink * (g_latent - latent * jnp.sum(g_latent * latent, axis=-1, keepdims=True))
    losses = jnp.where(encoder, commit_weight * away * away, valid * (gap * gap + root - 1.0))
    stat_ref[3:4, 0:256] += jnp.sum(losses, axis=0, keepdims=True)
    start = patch // 128 * 128
    latent_ref[...] = latent[:, start : start + 128].T[patch - start : patch - start + cdim, :]
    g_head = jnp.where(
        encoder, jnp.where(is_code, g_raw, 0.0), jnp.where(lane < patch, g_out, 0.0)
    ).astype(bf16)
    head_ref[rows, :] = g_head
    g_final = mm(g_head, thin_ref[...], NT)
    stat_ref[2:3, :] += jnp.sum(g_final * unit, axis=0, keepdims=True)
    g_result = norm_pull(g_final, unit, inverse, gain_final)

    low = g_result.astype(bf16)
    low_t_ref[:, rows] = low.T
    g_two = None
    for i, rest in enumerate(rests):
        g_before = (mm(low, rest[:, down]) * slopes[i]).astype(bf16)
        gbefore_ref[rows, i * units : (i + 1) * units] = g_before
        part = mm(g_before, rest[:, up], NT)
        g_two = part if g_two is None else g_two + part
    stat_ref[1:2, :] += jnp.sum(g_two * unit_two, axis=0, keepdims=True)
    g_middle = g_result + norm_pull(g_two, unit_two, inverse_two, gain_two)
    gm_ref[...] = g_middle
    branch = g_middle.astype(bf16)
    branch_t_ref[:, rows] = branch.T
    for ref, rest in zip((go_a_ref, go_b_ref), rests):
        ref[...] = mm(branch, rest[:, out]).astype(bf16)

    @pl.when(step == pl.num_programs(0) - 1)
    def _():
        head_grad_ref[...] = mm(final_t_ref[...], head_ref[...])
        split = keep_ref.shape[0]
        for i in range(2):
            first = i * (half + 2 * units)
            for ref, part in ((keep_ref, slice(0, split)), (sent_ref, slice(split, 2 * split))):
                ref[:, first : first + half] = mm(branch_t_ref[part, :], mixeds[i][...]).astype(bf16)
                for at in range(0, units, 512):
                    columns = slice(i * units + at, i * units + at + 512)
                    here = first + half + at
                    ref[:, here : here + 512] = mm(two_t_ref[part, :], gbefore_ref[:, columns]).astype(bf16)
                    here += units
                    ref[:, here : here + 512] = mm(low_t_ref[part, :], active_ref[:, columns]).astype(bf16)


def middle(side, mixed, hidden, patches, looked, valid, rest, thin, gains, at, patch, cdim, block=256):
    width = hidden.shape[1]
    half = mixed[0].shape[1]
    each = rest[0].shape[1] // 2
    hiddens = each - half
    thin_spec = pl.BlockSpec((width // 2, 256), lambda i: (0, at // 256))
    return call(
        functools.partial(middle_kernel, patch, cdim),
        "middle",
        [((SEQ, half), bf16)] * 2
        + [((SEQ, width), f32), ((cdim, SEQ), f32)]
        + [(rest[0].shape, bf16)] * 2
        + [((width, 256), f32), ((8, width), f32)],
        flops=16 << 30,
        nbytes=20 << 20,
        grid=(SEQ // block,),
        in_specs=[SCALAR]
        + [whole()] * 2
        + [rows_of(block, width)]
        + [rows_of(block, 256)] * 3
        + [pl.BlockSpec(memory_space=pl.ANY)] * 2
        + [thin_spec] * 2
        + [whole()],
        out_specs=[rows_of(block, half)] * 2
        + [rows_of(block, width), columns_of(cdim, block)]
        + [whole()] * 4,
        scratch_shapes=[
            pltpu.VMEM((SEQ, hiddens), bf16),
            pltpu.VMEM((SEQ, hiddens), bf16),
            pltpu.VMEM((width, SEQ), bf16),
            pltpu.VMEM((width, SEQ), bf16),
            pltpu.VMEM((width, SEQ), bf16),
            pltpu.VMEM((width, SEQ), bf16),
            pltpu.VMEM((SEQ, 256), bf16),
            pltpu.VMEM((width, each), bf16),
            pltpu.VMEM((width, each), bf16),
            pltpu.VMEM((width, 256), bf16),
            pltpu.SemaphoreType.DMA((4,)),
        ],
    )(side, *mixed, hidden, patches, looked, valid, *rest, *thin, gains)


def project_grad_kernel(normed_t_ref, *refs):
    grads, outs = refs[:6], refs[6:]
    split = outs[0].shape[0]
    for i, ref in enumerate(outs):
        normed_t = normed_t_ref[i * split : (i + 1) * split, :]
        for j in range(3):
            both = jnp.concatenate([grads[j][...], grads[3 + j][...]], axis=1)
            width = both.shape[1]
            ref[:, j * width : (j + 1) * width] = mm(normed_t, both).astype(bf16)


def project_grad(normed_t, first, second):
    width = normed_t.shape[0]
    return call(
        project_grad_kernel,
        "project_grad",
        [((width // 2, 12 * HD), bf16)] * 2,
        flops=2 << 30,
        nbytes=5 << 20,
        limit=16 << 20,
        in_specs=[whole()] * 7,
        out_specs=[whole()] * 2,
    )(normed_t, *first, *second)


def leave_kernel(
    patch, cdim, aligned, side_ref, code_ref, code_row_ref, *refs
):
    grads = refs[:12]
    (
        hidden_ref, gm_ref, patches_ref, looked_ref, latent_ref,
        low_a_ref, high_a_ref, low_b_ref, high_b_ref, thin_low_ref, thin_high_ref, gains_ref,
        head_ref, stat_ref, keep_ref, sent_ref, *more,
    ) = refs[12:]
    if aligned:
        gin_t_ref, entered_ref, gain_ref, sum_ref = more
    else:
        book_ref, gin_t_ref, entered_ref, gain_ref, sum_ref = more
    step = pl.program_id(0)
    tokens = hidden_ref.shape[0]
    rows = pl.ds(pl.multiple_of(step * tokens, tokens), tokens)
    encoder = side_ref[0] == 0

    @pl.when(step == 0)
    def _():
        gain_ref[...] = jnp.zeros_like(gain_ref)
        sum_ref[...] = jnp.zeros_like(sum_ref)

    gain = gains_ref[0:1, :]
    unit, inverse = normed_of(hidden_ref[...])
    g_normed = None
    for i, rest in enumerate(((low_a_ref, high_a_ref), (low_b_ref, high_b_ref))):
        first, second = grads[6 * i : 6 * i + 3], grads[6 * i + 3 : 6 * i + 6]
        together = jnp.concatenate(
            [r[...] for pair in zip(first, second) for r in pair], axis=1
        )
        part = to_two(together, *rest)
        g_normed = part if g_normed is None else g_normed + part
    offset = patch + cdim - 128
    gain_ref[offset : offset + 1, :] += jnp.sum(g_normed * unit, axis=0, keepdims=True)
    g_in = (gm_ref[...] + norm_pull(g_normed, unit, inverse, gain)).astype(bf16)
    gin_t_ref[:, rows] = g_in.T
    looked = looked_ref[...].astype(f32)
    entered_ref[rows, :] = jnp.where(encoder, patches_ref[...].astype(f32), looked).astype(bf16)

    start = patch // 128 * 128
    before, later = patch - start, 128 - (patch - start) - cdim
    pieces = [jnp.zeros((before, tokens), f32)] if before else []
    pieces.append(latent_ref[...])
    pieces += [jnp.zeros((later, tokens), f32)] if later else []
    latent = jnp.concatenate(pieces, axis=0).T
    latent = jnp.concatenate([jnp.zeros((tokens, start), f32), latent], axis=1)
    lane = lanes(tokens, 256)
    is_code = (lane >= patch) & (lane < patch + cdim)
    count = gains_ref[3:4, 0:1]
    g_looked = (
        by_two(g_in, thin_low_ref, thin_high_ref)
        + (2.0 * commit_weight) * (looked - latent) / count
    )
    g_looked = jnp.where(encoder, 0.0, jnp.where(is_code, g_looked, 0.0)).astype(bf16)
    row = lax.broadcasted_iota(jnp.int32, (256, 128), 0)
    tiled = jnp.where(lanes(256, 128) % cdim + patch == row, 1.0, 0.0).astype(bf16)
    copies = mm(g_looked, tiled)
    per = 128 // cdim
    away = code_ref[...] // LO - lanes(tokens, 128) // cdim
    spread = jnp.concatenate(
        [
            jnp.where(away == i * per, copies, 0.0).astype(bf16)
            for i in range(sum_ref.shape[1] // 128)
        ],
        axis=1,
    )
    low_row = code_row_ref[...] & (LO - 1)
    onehot = jnp.where(
        lax.broadcasted_iota(jnp.int32, (LO, tokens), 0) == low_row, 1.0, 0.0
    ).astype(bf16)
    sum_ref[...] += mm(onehot, spread)

    @pl.when(step == pl.num_programs(0) - 1)
    def _():
        gain_ref[offset + 1 : offset + 3, :] = stat_ref[1:3, :]
        thin = head_ref[...] + mm(gin_t_ref[...], entered_ref[...])
        ends = gain_ref[...].T
        split = keep_ref.shape[0]
        for i, ref in enumerate((keep_ref, sent_ref)):
            here = slice(i * split, (i + 1) * split)
            ref[:, :128] = thin[here, :128].astype(bf16)
            ref[:, 128:256] = (thin[here, 128:] + ends[here, :]).astype(bf16)
            if aligned:
                blocks = split // aligned
                for b in range(blocks):
                    at = (i * blocks + b) * 128
                    for j in range(LO // aligned):
                        ref[b * aligned : (b + 1) * aligned, 256 + j * 128 : 384 + j * 128] = sum_ref[
                            j * aligned : (j + 1) * aligned, at : at + 128
                        ].astype(bf16)
        if not aligned:
            book_ref[...] = sum_ref[...].astype(bf16)


def leave(side, code, code_row, grads, hidden, gm, patches, looked, latent, a, b, gains, head, stat, aligned, patch, cdim, codes, block=256):
    width = hidden.shape[1]
    wide = b[0].shape[1]
    table = (LO, codes // LO * cdim)
    columns = 256 + (LO // aligned * 128 if aligned else 0)
    thin_spec = pl.BlockSpec((width // 2, 256), lambda i: (0, wide // 256))
    wide_spec = pl.BlockSpec((width // 2, wide), lambda i: (0, 0))
    return call(
        functools.partial(leave_kernel, patch, cdim, aligned),
        "leave",
        [((width // 2, columns), bf16)] * 2 + ([] if aligned else [(table, bf16)]),
        flops=8 << 30,
        nbytes=12 << 20,
        limit=32 << 20,
        grid=(SEQ // block,),
        in_specs=[SCALAR, rows_of(block, 128), columns_of(1, block)]
        + [rows_of(block, 2 * HD)] * 12
        + [rows_of(block, width)] * 2
        + [rows_of(block, 256)] * 2
        + [columns_of(cdim, block)]
        + [wide_spec] * 4
        + [thin_spec] * 2
        + [whole()] * 3,
        out_specs=[whole()] * (2 if aligned else 3),
        scratch_shapes=[
            pltpu.VMEM((width, SEQ), bf16),
            pltpu.VMEM((SEQ, 256), bf16),
            pltpu.VMEM((128, width), f32),
            pltpu.VMEM(table, f32),
        ],
    )(side, code, code_row, *grads, hidden, gm, patches, looked, latent, *a, *b, *a, gains, head, stat)


def untangle(block, per, cdim):
    rows = block.shape[0]
    step = per * cdim
    tall = jnp.concatenate([block[:, j * step : (j + 1) * step] for j in range(LO // rows)], axis=0)
    if step < 128:
        tall = jnp.concatenate([tall, jnp.zeros((LO, 128 - step), f32)], axis=1)
    turned = tall.T
    return jnp.concatenate([turned[i * cdim : (i + 1) * cdim, :] for i in range(per)], axis=1)


def settle_kernel(own_ref, sent_ref, qkv_own_ref, qkv_sent_ref, thin_ref, book_ref, stat_ref, thin_out_ref, book_out_ref, total_ref):
    cdim, codes_here = book_ref.shape
    book = book_ref[...].astype(bf16).astype(f32)
    shrink = lax.rsqrt(jnp.sum(book * book, axis=0, keepdims=True) + 1.0)
    unit = book * shrink
    grad = untangle(thin_ref[:, 256:], codes_here // LO, cdim)
    grad = shrink * (grad - unit * jnp.sum(grad * unit, axis=0, keepdims=True))
    book_out_ref[...] = grad
    small = thin_ref[:, :256]
    thin_out_ref[...] = small

    def total(value):
        return jnp.sum(jnp.sum(value * value, axis=0, keepdims=True), axis=1, keepdims=True)

    squares = total(grad) + total(small)
    for ref in (own_ref, sent_ref, qkv_own_ref, qkv_sent_ref):
        squares += total(ref[...])
    loss = jnp.sum(stat_ref[3:4, :], axis=1, keepdims=True)
    row = lax.broadcasted_iota(jnp.int32, (8, 128), 0)
    total_ref[...] = jnp.where(row == 0, squares, jnp.where(row == 1, loss, 0.0))


def settle(rest_own, rest_sent, qkv_own, qkv_sent, thin, book_t, stat):
    return call(
        settle_kernel,
        "settle",
        [((thin.shape[0], 256), f32), (book_t.shape, f32), ((8, 128), f32)],
        nbytes=1 << 20,
        limit=12 << 20,
        in_specs=[whole()] * 7,
        out_specs=[whole()] * 3,
    )(rest_own, rest_sent, qkv_own, qkv_sent, thin, book_t, stat)


def adam(master, moment, square, clipped, rate):
    moment_new = first_decay * moment + (1.0 - first_decay) * clipped
    square_new = second_decay * square + (1.0 - second_decay) * clipped * clipped
    moment_hat = moment_new / (1.0 - first_decay**STEP)
    square_hat = square_new / (1.0 - second_decay**STEP)
    updated = master - rate * (
        moment_hat / (jnp.sqrt(square_hat) + adam_epsilon) + weight_decay * master
    )
    return updated, moment_new, square_new


def update_kernel(side_ref, *refs):
    grads, weights, outs = refs[:9], refs[9:27], refs[27:45]
    norm_ref, turn_ref = refs[45:]
    total_ref, own_ref, got_ref, qkv_own_ref, qkv_got_ref, small_own_ref, small_got_ref, book_own_ref, book_got_ref = grads
    side = side_ref[0]
    encoder = side == 0
    norm = jnp.sqrt(total_ref[0:1, 0:1])
    norm_ref[...] = jnp.broadcast_to(norm, norm_ref.shape)
    factor = clip_norm / jnp.maximum(norm, clip_norm)

    def apply(which, index, grad):
        three = [weights[3 * which + i][index] for i in range(3)]
        for i, value in enumerate(adam(*three, grad * factor, learn_rates[which])):
            outs[3 * which + i][index] = value

    half = weights[0].shape[3]
    units = weights[3].shape[3]
    rows = own_ref.shape[0]
    patch = weights[6].shape[2]
    cdim = weights[9].shape[1]
    gains = []
    for at, rest, qkv, small in (
        (side, own_ref, qkv_own_ref, small_own_ref),
        (1 - side, got_ref, qkv_got_ref, small_got_ref),
    ):
        for j in range(3):
            apply(0, (at, j), qkv[:, j * half : (j + 1) * half])
        apply(0, (at, 3), rest[:, :half])
        for j in range(2):
            apply(1, (at, j), rest[:, half + j * units : half + (j + 1) * units])
        apply(2, (at,), small[:, :patch])
        turn_ref[0:rows, :] = small[:, 128:256]
        turned = turn_ref[...].T[:, :rows]
        first = patch - 128
        apply(3, (at,), turned[first : first + cdim])
        gains.append(turned[first + cdim : first + cdim + 3])
    apply(4, (slice(None),), jnp.where(encoder, book_got_ref[...], book_own_ref[...]))
    apply(5, (slice(0, 3),), jnp.where(encoder, gains[0], gains[1]))
    apply(5, (slice(3, 6),), jnp.where(encoder, gains[1], gains[0]))


def update(side, grads, weights):
    out = [(w.shape, f32) for w in weights] + [((8, 128), f32)]
    return pl.pallas_call(
        update_kernel,
        name="update",
        out_shape=[jax.ShapeDtypeStruct(s, d) for s, d in out],
        in_specs=[SCALAR] + [whole()] * (len(grads) + len(weights)),
        out_specs=[whole()] * len(out),
        scratch_shapes=[pltpu.VMEM((128, 128), f32)],
        compiler_params=pltpu.CompilerParams(vmem_limit_bytes=24 << 20),
        cost_estimate=pl.CostEstimate(flops=1 << 22, bytes_accessed=10 << 20, transcendentals=0),
    )(side, *grads, *weights)


def body(
    pixels,
    valid_mask,
    code_index,
    attention_weight,
    attention_moment,
    attention_square,
    feedforward_weight,
    feedforward_moment,
    feedforward_square,
    pixel_weight,
    pixel_moment,
    pixel_square,
    code_weight,
    code_moment,
    code_square,
    codebook,
    codebook_moment,
    codebook_square,
    norm_gains,
    gains_moment,
    gains_square,
):
    side = lax.axis_index("mp")
    place = lax.axis_index("dp")
    parts = lax.axis_size("dp")
    bits = bits_of(parts)
    encoder = side == 0
    flag = side.astype(jnp.int32).reshape(1)
    rows = attention_weight.shape[2]
    half = attention_weight.shape[3]
    units = feedforward_weight.shape[3]
    patch = pixel_weight.shape[1]
    cdim = code_weight.shape[1]
    codes_here = codebook.shape[0]
    codes = codes_here * parts
    per = codes_here // LO
    wide = 3 * half
    aligned = rows if per * cdim == 128 and rows % 16 == 0 else 0

    pixels_t, valid_t = pixels.T, valid_mask.T
    own_a, sent_b = pack_first(
        flag, attention_weight, pixel_weight.transpose(0, 2, 1), code_weight, codebook.T,
        norm_gains, valid_t,
    )
    held_a = widen(own_a, 0)
    got_b = swap_mp(sent_b)

    turned = place_of((code_index // codes_here) ^ place, place & 1, bits)
    code_row = (turned * codes_here + code_index % codes_here)[None, :]
    rest_own, rest_sent, patches, valid, code_column = pack_rest(
        flag, attention_weight, feedforward_weight, pixels_t, after(valid_t, sent_b), code_row
    )
    held_a, held_b, rest_sent = together(held_a, got_b, rest_sent)
    rest_got = swap_mp(rest_sent)
    held_a, held_b = widen(held_a, 1), widen(held_b, 0)
    held_a, held_b, rest_got = together(held_a, held_b, rest_got)
    rest = widen(jnp.concatenate([rest_own, rest_got], axis=1), 0)
    held_b = widen(held_b, 1)
    for step in range(2, bits - 1):
        held_a, held_b = widen(held_a, step), after(held_b, held_a) if step > 2 else held_b
        if step > 2:
            held_b = widen(held_b, step - 1)
    a = (held_a, swap_core(held_a))
    held_b = widen(held_b, bits - 2)
    b = (held_b, swap_core(held_b))

    book = None
    if not aligned:
        book = jnp.concatenate(a)[:, wide + 256 :].reshape(parts, rows, LO // rows, per * cdim)
        book = book.transpose(2, 1, 0, 3).reshape(LO, -1)
    hidden, looked, qkv_a, qkv_b, normed_t, gains = enter(
        flag, code_column, patches, a, b, book, aligned, patch, cdim, codes
    )
    rest = widen(after(rest, *a, *b), 1)
    qkv_a, rest = together(qkv_a, rest)
    mixed_a, log_a = attend(qkv_a)
    for step in range(2, bits - 1):
        rest = widen(rest, step)
    mixed_b, log_b = attend(after(qkv_b, mixed_a))
    rest = after(rest, mixed_b)
    rest = (rest, swap_core(rest))

    go_a, go_b, g_middle, latent, keep_r, sent_r, g_head, stat = middle(
        flag, (mixed_a, mixed_b), hidden, patches, looked, valid, rest, a, gains, wide, patch, cdim
    )
    grads_a0 = attend_back(qkv_a, mixed_a, go_a, log_a, 0)
    latent_there = swap_mp(after(latent, *grads_a0))
    rest = halves(fold((keep_r, sent_r), None, grads_a0))
    grads_a1 = attend_back(after(qkv_a, *rest), mixed_a, go_a, log_a, 1)
    keep_a, sent_a = project_grad(normed_t, grads_a0, grads_a1)
    last = bits - 2
    rest = halves(fold(rest, last, (keep_a,)))
    grads_b0 = attend_back(after(qkv_b, keep_a, *rest), mixed_b, go_b, log_b, 0)
    part_a = halves(fold((keep_a, sent_a), None, grads_b0))
    rest = together(*rest, *grads_b0)[:2]
    grads_b1 = attend_back(after(qkv_b, *part_a), mixed_b, go_b, log_b, 1)
    keep_b, sent_b = project_grad(normed_t, grads_b0, grads_b1)
    for step in range(last - 1, 0, -1):
        rest = halves(fold(rest, step, (keep_b,)))
    part_a = halves(fold(part_a, last, (keep_b,)))
    keep_s, sent_s, *g_book = leave(
        flag, code_column, code_row, grads_a0 + grads_a1 + grads_b0 + grads_b1,
        after(hidden, *rest, *part_a), g_middle, patches, looked, latent_there,
        a, b, gains, g_head, stat, aligned, patch, cdim, codes,
    )
    rest = fold(rest, 0, (keep_s,))
    part_a = halves(fold(part_a, last - 1, (keep_s,)))
    part_b = fold((keep_b, sent_b), None, (keep_s,))
    if not aligned:
        g_book = g_book[0].reshape(LO // rows, rows, parts, per * cdim)
        g_book = g_book.transpose(2, 1, 0, 3).reshape(2, parts * rows // 2, -1)
        keep_s = jnp.concatenate([keep_s, g_book[0]], axis=1)
        sent_s = jnp.concatenate([sent_s, g_book[1]], axis=1)
    thin = fold((keep_s, sent_s), None)
    rest_own, rest_sent = rest[:, : rest.shape[1] // 2], rest[:, rest.shape[1] // 2 :]
    rest_got = swap_mp(rest_sent)
    part_b = after(jnp.concatenate([part_b, thin], axis=1), rest, *part_a)
    for step in range(last, -1, -1):
        part_b = fold(halves(part_b), step)
    for step in range(last - 2, -1, -1):
        part_a = fold(part_a, step)
        if step:
            part_a = halves(part_a)
    qkv_own, qkv_sent, thin = part_a, part_b[:, :wide], part_b[:, wide:]
    qkv_got = swap_mp(qkv_sent)
    small_own, book_own, totals = settle(
        rest_own, rest_sent, qkv_own, qkv_sent, thin, codebook.T, stat
    )
    small_got, book_got = swap_mp(small_own), swap_mp(book_own)
    totals = all_sum(totals)
    thin_view = (0, 2, 1)
    weights = (
        attention_weight,
        attention_moment,
        attention_square,
        feedforward_weight,
        feedforward_moment,
        feedforward_square,
        pixel_weight.transpose(thin_view),
        pixel_moment.transpose(thin_view),
        pixel_square.transpose(thin_view),
        code_weight,
        code_moment,
        code_square,
        codebook.T,
        codebook_moment.T,
        codebook_square.T,
        norm_gains,
        gains_moment,
        gains_square,
    )
    grads = (
        totals, rest_own, rest_got, qkv_own, qkv_got, small_own, small_got, book_own, book_got
    )
    *new, norm_total = update(flag, grads, weights)
    new[6:9] = [x.transpose(thin_view) for x in new[6:9]]
    new[12:15] = [x.T for x in new[12:15]]
    return tuple(new) + (totals[1, 0], gains[3, 0], norm_total[0, 0])


def solution(mesh):
    wide = P(None, None, "dp", "mp")
    thin = P(None, None, "dp")
    rows = P("dp", None)
    gain = P(None, "dp")
    weights = (wide,) * 6 + (thin,) * 6 + (rows,) * 3 + (gain,) * 3
    return jax.shard_map(
        body,
        mesh=mesh,
        in_specs=(rows, rows, P("dp")) + weights,
        out_specs=weights + (P(), P(), P()),
        check_vma=False,
    )
```

```python
import functools

import jax
import jax.numpy as jnp
from jax import lax
from jax.experimental import pallas as pl
from jax.experimental.pallas import tpu as pltpu
from jax.sharding import PartitionSpec as P

HD = 64
SEQ = 1024
STEP = 10

norm_epsilon = 1e-05
commit_weight = 0.25
clip_norm = 0.003
learn_rates = (0.2, 0.02, 0.04, 0.5, 0.5, 0.6)
first_decay = 0.9
second_decay = 0.999
weight_decay = 0.01
adam_epsilon = 1e-08

bf16 = jnp.bfloat16
f32 = jnp.float32


def swap_mp(value):
    return lax.ppermute(value, "mp", [(0, 1), (1, 0)])


def bits_of(size):
    return size.bit_length() - 1


def step_orders(bits):
    high = list(range(bits - 1, 1, -1))
    return (high + [1], [1] + high)


def swap_step(value, step):
    size = lax.axis_size("dp")
    orders = step_orders(bits_of(size))
    return lax.ppermute(value, "dp", [(i, i ^ (1 << orders[i & 1][step])) for i in range(size)])


def swap_core(value):
    return lax.ppermute(value, "dp", [(i, i ^ 1) for i in range(lax.axis_size("dp"))])


def place_of(mask, core, bits):
    places = [
        sum(((mask >> bit) & 1) << step for step, bit in enumerate(order))
        for order in step_orders(bits)
    ]
    same = mask & 1 == 0
    return jnp.where(same == (core == 0), places[0], places[1]) + jnp.where(same, 0, 1 << (bits - 1))


def after(value, *others):
    return lax.optimization_barrier((value,) + others)[0]


def together(*arrays):
    return lax.optimization_barrier(arrays)


def widen(held, step, later=()):
    got = swap_step(held, step)
    if later:
        held = after(held, *later)
    return jnp.concatenate([held, got], axis=0)


def fold(pair, step, later=()):
    keep, sent = pair
    got = swap_core(sent) if step is None else swap_step(sent, step)
    if later:
        keep = after(keep, *later)
    return keep, got


def added(pair):
    return pair[0].astype(f32) + pair[1].astype(f32)


def halves(pair):
    split = pair[0].shape[0] // 2
    keep = added([x[:split] for x in pair])
    return together(keep, added([x[split:] for x in pair]).astype(bf16))


def all_sum(value):
    size = lax.axis_size("dp")
    for bit in range(bits_of(size)):
        value = value + lax.ppermute(value, "dp", [(i, i ^ (1 << bit)) for i in range(size)])
    return value + swap_mp(value)


NN = (((1,), (0,)), ((), ()))
NT = (((1,), (1,)), ((), ()))
VMEM_LIMIT = 48 << 20
LO = 128


def mm(a, b, dims=NN):
    return lax.dot_general(a, b, dims, preferred_element_type=f32)


def whole():
    return pl.BlockSpec(memory_space=pltpu.VMEM)


def rows_of(block, width):
    return pl.BlockSpec((block, width), lambda i: (i, 0))


def columns_of(height, block):
    return pl.BlockSpec((height, block), lambda i: (0, i))


def call(kernel, name, out, flops=0, nbytes=0, exps=0, limit=VMEM_LIMIT, **kw):
    return pl.pallas_call(
        kernel,
        name=name,
        out_shape=[jax.ShapeDtypeStruct(s, d) for s, d in out],
        compiler_params=pltpu.CompilerParams(vmem_limit_bytes=limit),
        cost_estimate=pl.CostEstimate(flops=flops, bytes_accessed=nbytes, transcendentals=exps),
        **kw,
    )


SCALAR = pl.BlockSpec(memory_space=pltpu.SMEM)


def attend_kernel(q_ref, k_ref, v_ref, o_ref, log_ref, vt_ref):
    vt_ref[...] = v_ref[...].T
    keys = k_ref[...]
    q = q_ref[...] * jnp.asarray(HD**-0.5, bf16)
    low = lax.broadcasted_iota(jnp.int32, q.shape, 1) < HD
    zero = jnp.zeros_like(q)
    mixed = []
    for head in range(2):
        own = jnp.where(low if head == 0 else ~low, q, zero)
        s = mm(keys, own, NT)
        peak = jnp.max(s, axis=0, keepdims=True)
        e = jnp.exp(s - peak)
        total = jnp.sum(e, axis=0, keepdims=True)
        part = mm(vt_ref[head * HD : (head + 1) * HD, :], e.astype(bf16))
        mixed.append(part * (1.0 / total))
        log_ref[0, head : head + 1, :] = peak + jnp.log(total)
    o_ref[...] = jnp.concatenate(mixed, axis=0).T.astype(bf16)


def column_block(at):
    return pl.BlockSpec((SEQ, 2 * HD), lambda i: (0, at + i))


def attend(qkv):
    width = qkv.shape[1] // 3
    pairs = width // (2 * HD)
    return call(
        attend_kernel,
        "attend",
        [((SEQ, width), bf16), ((pairs, 2, SEQ), f32)],
        flops=pairs * 8 * SEQ * SEQ * 256,
        nbytes=8 * SEQ * width,
        limit=28 << 20,
        grid=(pairs,),
        in_specs=[column_block(0), column_block(pairs), column_block(2 * pairs)],
        out_specs=[column_block(0), pl.BlockSpec((1, 2, SEQ), lambda i: (i, 0, 0))],
        scratch_shapes=[pltpu.VMEM((2 * HD, SEQ), bf16)],
    )(qkv, qkv, qkv)


def attend_back_kernel(
    chunk, q_ref, k_ref, v_ref, o_ref, go_ref, log_ref, gq_ref, gk_ref, gv_ref, kt_ref, sk_ref, sv_ref
):
    kt_ref[...] = k_ref[...].T
    keys = k_ref[...]
    values = v_ref[...]
    low = lax.broadcasted_iota(jnp.int32, (chunk, 2 * HD), 1) < HD
    scale = HD**-0.5
    for start in range(0, SEQ, chunk):
        rows = pl.ds(start, chunk)
        q = q_ref[rows, :] * jnp.asarray(scale, bf16)
        go = go_ref[rows, :]
        product = (go.astype(f32) * o_ref[rows, :].astype(f32)).T
        zero = jnp.zeros_like(q)
        grads = []
        sums = None
        for head in range(2):
            here = low if head == 0 else ~low
            own = jnp.where(here, q, zero)
            own_go = jnp.where(here, go, zero)
            inner = jnp.sum(product[head * HD : (head + 1) * HD, :], axis=0, keepdims=True)
            p = jnp.exp(mm(keys, own, NT) - log_ref[0, head : head + 1, rows])
            gp = mm(values, own_go, NT)
            gs = (p * (gp - inner)).astype(bf16)
            gk = mm(gs, own)
            gv = mm(p.astype(bf16), own_go)
            sums = (gk, gv) if head == 0 else (sums[0] + gk, sums[1] + gv)
            grads.append(mm(kt_ref[head * HD : (head + 1) * HD, :], gs))
        gq_ref[rows, :] = (jnp.concatenate(grads, axis=0).T * scale).astype(bf16)
        if start == 0:
            sk_ref[...] = sums[0]
            sv_ref[...] = sums[1]
        elif start + chunk < SEQ:
            sk_ref[...] += sums[0]
            sv_ref[...] += sums[1]
        else:
            gk_ref[...] = (sk_ref[...] + sums[0]).astype(bf16)
            gv_ref[...] = (sv_ref[...] + sums[1]).astype(bf16)


def attend_back(qkv, o, go, log_total, pair, chunk=512):
    pairs = o.shape[1] // (2 * HD)
    return call(
        functools.partial(attend_back_kernel, chunk),
        "attend_back",
        [((SEQ, 2 * HD), bf16)] * 3,
        flops=20 * SEQ * SEQ * 256,
        nbytes=16 * SEQ * 128,
        limit=20 << 20,
        grid=(1,),
        in_specs=[
            column_block(pair),
            column_block(pairs + pair),
            column_block(2 * pairs + pair),
            column_block(pair),
            column_block(pair),
            pl.BlockSpec((1, 2, SEQ), lambda i: (pair, 0, 0)),
        ],
        out_specs=[column_block(0)] * 3,
        scratch_shapes=[
            pltpu.VMEM((2 * HD, SEQ), bf16),
            pltpu.VMEM((SEQ, 2 * HD), f32),
            pltpu.VMEM((SEQ, 2 * HD), f32),
        ],
    )(qkv, qkv, qkv, o, go, log_total)


def lanes(rows, columns):
    return lax.broadcasted_iota(jnp.int32, (rows, columns), 1)


def normed_of(hidden):
    centred = hidden - jnp.mean(hidden, axis=-1, keepdims=True)
    spread = jnp.mean(centred * centred, axis=-1, keepdims=True)
    inverse = lax.rsqrt(spread + norm_epsilon)
    return centred * inverse, inverse


def norm_pull(grad, unit, inverse, gain):
    scaled = grad * gain
    return inverse * (
        scaled
        - jnp.mean(scaled, axis=-1, keepdims=True)
        - unit * jnp.mean(scaled * unit, axis=-1, keepdims=True)
    )


def by_two(value, low_ref, high_ref, columns=slice(None)):
    split = low_ref.shape[0]
    return mm(value[:, :split], low_ref[:, columns]) + mm(value[:, split:], high_ref[:, columns])


def to_two(value, low_ref, high_ref, columns=slice(None)):
    return jnp.concatenate(
        [mm(value, low_ref[:, columns], NT), mm(value, high_ref[:, columns], NT)], axis=1
    )


def pack_first_kernel(
    side_ref, attention_ref, pixel_ref, code_ref, book_ref, gains_ref, valid_ref,
    own_ref, sent_ref, turn_ref,
):
    side = side_ref[0]
    rows, half = attention_ref.shape[2], attention_ref.shape[3]
    patch, cdim = pixel_ref.shape[2], code_ref.shape[1]
    for j in range(3):
        own_ref[:, j * half : (j + 1) * half] = attention_ref[side, j].astype(bf16)
        sent_ref[:, j * half : (j + 1) * half] = attention_ref[1 - side, j].astype(bf16)
    count = jnp.sum(valid_ref[...], axis=0, keepdims=True)
    count = jnp.sum(count.astype(f32), axis=1, keepdims=True).astype(jnp.int32)
    at = 3 * half
    first = patch - 128
    turn_ref[...] = jnp.zeros_like(turn_ref)
    turn_ref[first : first + cdim, 0:rows] = code_ref[side]
    first += cdim
    turn_ref[first : first + 3, 0:rows] = jnp.where(side == 0, gains_ref[0:3, :], gains_ref[3:6, :])
    digits = (count & 255, (count >> 8) & 255, count >> 16)
    for i, digit in enumerate(digits):
        turn_ref[first + 3 + i : first + 4 + i, 0:1] = digit.astype(f32)
    own_ref[:, at + 128 : at + 256] = turn_ref[...].T[0:rows, :].astype(bf16)
    own_ref[:, at : at + patch] = pixel_ref[side].astype(bf16)
    at += 256
    book = book_ref[...].astype(bf16).astype(f32)
    unit = book * lax.rsqrt(jnp.sum(book * book, axis=0, keepdims=True) + 1.0)
    per = book.shape[1] // LO
    tall = jnp.concatenate([unit[:, i * LO : (i + 1) * LO] for i in range(per)], axis=0)
    if per * cdim < 128:
        tall = jnp.concatenate([tall, jnp.zeros((128 - per * cdim, LO), f32)], axis=0)
    wide = tall.T
    step = per * cdim
    for j in range(LO // rows):
        own_ref[:, at + j * step : at + (j + 1) * step] = wide[
            j * rows : (j + 1) * rows, :step
        ].astype(bf16)


def pack_first(side, attention, pixel_t, code, book_t, gains, valid_t):
    _, _, rows, half = attention.shape
    cdim, codes = book_t.shape
    return call(
        pack_first_kernel,
        "pack_first",
        [((rows, 3 * half + 256 + cdim * codes // rows), bf16), ((rows, 3 * half), bf16)],
        nbytes=2 << 20,
        limit=60 << 20,
        in_specs=[SCALAR] + [whole()] * 6,
        out_specs=[whole()] * 2,
        scratch_shapes=[pltpu.VMEM((128, 128), f32)],
    )(side, attention, pixel_t, code, book_t, gains, valid_t)


def pack_rest_kernel(
    side_ref, attention_ref, feedforward_ref, pixels_ref, valid_ref, code_ref,
    own_ref, sent_ref, patches_ref, mask_ref, column_ref,
):
    side = side_ref[0]
    half, units = attention_ref.shape[3], feedforward_ref.shape[3]
    for ref, which in ((own_ref, side), (sent_ref, 1 - side)):
        ref[:, :half] = attention_ref[which, 3].astype(bf16)
        ref[:, half : half + units] = feedforward_ref[which, 0].astype(bf16)
        ref[:, half + units :] = feedforward_ref[which, 1].astype(bf16)
    patch, tokens = pixels_ref.shape
    zeros = jnp.zeros((256 - patch, tokens), f32)
    patches_ref[...] = jnp.concatenate([pixels_ref[...].astype(f32), zeros], axis=0).T.astype(bf16)
    mask_ref[...] = jnp.concatenate([valid_ref[...].astype(f32), zeros], axis=0).T.astype(bf16)
    column_ref[...] = jnp.broadcast_to(code_ref[...].astype(f32), (128, tokens)).T.astype(jnp.int32)


def pack_rest(side, attention, feedforward, pixels_t, valid_t, code_row):
    rows, half = attention.shape[2:]
    units = feedforward.shape[3]
    return call(
        pack_rest_kernel,
        "pack_rest",
        [((rows, half + 2 * units), bf16)] * 2
        + [((SEQ, 256), bf16)] * 2
        + [((SEQ, 128), jnp.int32)],
        nbytes=5 << 20,
        limit=60 << 20,
        in_specs=[SCALAR] + [whole()] * 5,
        out_specs=[whole()] * 5,
    )(side, attention, feedforward, pixels_t, valid_t, code_row)


def enter_kernel(
    patch, cdim, aligned, side_ref, code_ref, patches_ref, low_a_ref, high_a_ref, *refs,
):
    if aligned:
        hidden_ref, looked_ref, qkv_ref, normed_ref, normed_t_ref, gains_ref, book_ref = refs
    else:
        book_ref, hidden_ref, looked_ref, qkv_ref, normed_ref, normed_t_ref, gains_ref = refs
    step = pl.program_id(0)
    tokens = code_ref.shape[0]
    wide = qkv_ref.shape[1]
    split = low_a_ref.shape[0]
    thin = slice(wide, wide + 256)

    @pl.when(step == 0)
    def _():
        first = patch + cdim - 128
        gains_ref[...] = jnp.zeros_like(gains_ref)
        digits = 0.0
        for i, ref in enumerate((low_a_ref, high_a_ref)):
            turned = ref[:, wide + 128 : wide + 256].astype(f32).T
            gains_ref[0:3, i * split : (i + 1) * split] = turned[first : first + 3, :]
            digits += jnp.sum(turned, axis=1, keepdims=True)
        count = (
            digits[first + 3 : first + 4]
            + 256.0 * digits[first + 4 : first + 5]
            + 65536.0 * digits[first + 5 : first + 6]
        )
        gains_ref[3:4, :] = jnp.broadcast_to(count, (1, gains_ref.shape[1]))
        if aligned:
            rows = aligned
            for i, ref in enumerate((low_a_ref, high_a_ref)):
                blocks = split // rows
                for b in range(blocks):
                    at = (i * blocks + b) * 128
                    for j in range(LO // rows):
                        column = wide + 256 + j * 128
                        book_ref[j * rows : (j + 1) * rows, at : at + 128] = ref[
                            b * rows : (b + 1) * rows, column : column + 128
                        ]

    code = code_ref[...]
    low, high = code & (LO - 1), code // LO
    lane = lanes(tokens, 128)
    onehot = jnp.where(lane == low, 1.0, 0.0).astype(bf16)
    spread = mm(onehot, book_ref[...])
    group = lane // cdim
    per = 128 // cdim
    away = high - group
    picked = jnp.zeros((tokens, 128), f32)
    for i in range(spread.shape[1] // 128):
        picked += jnp.where(away == i * per, spread[:, i * 128 : (i + 1) * 128], 0.0)
    lane_out = lanes(128, 256)
    fold_in = (
        lax.broadcasted_iota(jnp.int32, (128, 256), 0) % cdim + patch == lane_out
    ) & (lane_out < patch + cdim)
    looked = mm(picked.astype(bf16), jnp.where(fold_in, 1.0, 0.0).astype(bf16)).astype(bf16)
    looked_ref[...] = looked
    encoder = side_ref[0] == 0
    entered = jnp.where(encoder, patches_ref[...].astype(f32), looked.astype(f32)).astype(bf16)
    hidden = to_two(entered, low_a_ref, high_a_ref, thin)
    hidden_ref[...] = hidden
    unit, _ = normed_of(hidden)
    normed = (unit * gains_ref[0:1, :]).astype(bf16)
    normed_t_ref[...] = normed.T
    normed_ref[...] = normed
    qkv_ref[...] = by_two(normed, low_a_ref, high_a_ref, slice(0, wide)).astype(bf16)


def enter(side, code, patches, a, book, aligned, wide, patch, cdim, codes, block=256):
    width = 2 * a[0].shape[0]
    table = (LO, codes // LO * cdim)
    return call(
        functools.partial(enter_kernel, patch, cdim, aligned),
        "enter",
        [
            ((SEQ, width), f32),
            ((SEQ, 256), bf16),
            ((SEQ, wide), bf16),
            ((SEQ, width), bf16),
            ((width, SEQ), bf16),
            ((8, width), f32),
        ],
        flops=8 << 30,
        nbytes=12 << 20,
        limit=28 << 20,
        grid=(SEQ // block,),
        in_specs=[SCALAR, rows_of(block, 128), rows_of(block, 256)]
        + [whole()] * (2 if aligned else 3),
        out_specs=[
            rows_of(block, width),
            rows_of(block, 256),
            rows_of(block, wide),
            rows_of(block, width),
            columns_of(width, block),
            pl.BlockSpec((8, width), lambda i: (0, 0)),
        ],
        scratch_shapes=[pltpu.VMEM(table, bf16)] if aligned else [],
    )(side, code, patches, *a, *([] if aligned else [book]))


def project_kernel(normed_ref, low_ref, high_ref, qkv_ref):
    qkv_ref[...] = by_two(normed_ref[...], low_ref, high_ref).astype(bf16)


def project(normed, b, block=512):
    wide = b[0].shape[1]
    return call(
        project_kernel,
        "project",
        [((SEQ, wide), bf16)],
        flops=2 << 30,
        nbytes=4 << 20,
        limit=16 << 20,
        grid=(SEQ // block,),
        in_specs=[rows_of(block, normed.shape[1]), whole(), whole()],
        out_specs=[rows_of(block, wide)],
    )(normed, *b)[0]


GELU_A, GELU_B = 0.7978845608028654, 0.044715


def middle_kernel(
    patch, cdim, side_ref, mixed_a_ref, mixed_b_ref, hidden_ref, patches_ref, looked_ref, valid_ref,
    low_ref, high_ref, thin_low_ref, thin_high_ref, gains_ref,
    go_a_ref, go_b_ref, gm_ref, latent_ref, keep_ref, sent_ref,
    head_grad_ref, stat_ref,
    active_ref, gbefore_ref, low_t_ref, two_t_ref, branch_t_ref, final_t_ref, head_ref,
    full_a_ref, full_b_ref, thin_ref, copy_sem,
):
    step = pl.program_id(0)
    tokens = hidden_ref.shape[0]
    half = mixed_a_ref.shape[1]
    units = (low_ref.shape[1] // 2 - half) // 2
    rows = pl.ds(pl.multiple_of(step * tokens, tokens), tokens)
    encoder = side_ref[0] == 0
    rests = (full_a_ref, full_b_ref)
    mixeds = (mixed_a_ref, mixed_b_ref)
    out, up, down = slice(0, half), slice(half, half + units), slice(half + units, half + 2 * units)

    @pl.when(step == 0)
    def _():
        stat_ref[...] = jnp.zeros_like(stat_ref)
        split = low_ref.shape[0]
        each = half + 2 * units
        copies = [
            pltpu.make_async_copy(
                piece.at[:, pl.ds(i * each, each)],
                rests[i].at[pl.ds(j * split, split), :],
                copy_sem.at[2 * i + j],
            )
            for i in range(2)
            for j, piece in enumerate((low_ref, high_ref))
        ]
        for copy in copies:
            copy.start()
        thin_ref[:split, :] = thin_low_ref[...]
        thin_ref[split:, :] = thin_high_ref[...]
        for copy in copies:
            copy.wait()

    gain_two, gain_final = gains_ref[1:2, :], gains_ref[2:3, :]
    middle = hidden_ref[...]
    for ref, rest in zip(mixeds, rests):
        middle += mm(ref[rows, :], rest[:, out], NT)
    unit_two, inverse_two = normed_of(middle)
    two = (unit_two * gain_two).astype(bf16)
    two_t_ref[:, rows] = two.T
    slopes = []
    for i, rest in enumerate(rests):
        before = mm(two, rest[:, up])
        square = before * before
        bent = jnp.tanh(GELU_A * before * (1.0 + GELU_B * square))
        active_ref[rows, i * units : (i + 1) * units] = (0.5 * before * (1.0 + bent)).astype(bf16)
        slopes.append(
            0.5 * (1.0 + bent)
            + (0.5 * GELU_A) * before * (1.0 - bent * bent) * (1.0 + 3.0 * GELU_B * square)
        )

    @pl.when(step >= 0)
    def _():
        total = middle
        for i, rest in enumerate(rests):
            total += mm(active_ref[rows, i * units : (i + 1) * units], rest[:, down], NT)
        gm_ref[...] = total

    result = gm_ref[...]
    unit, inverse = normed_of(result)
    final = (unit * gain_final).astype(bf16)
    final_t_ref[:, rows] = final.T
    seen = mm(final, thin_ref[...])
    lane = lanes(tokens, 256)
    is_code = (lane >= patch) & (lane < patch + cdim)
    count = gains_ref[3:4, 0:1]
    patches = patches_ref[...].astype(f32)
    looked = looked_ref[...].astype(f32)
    valid = valid_ref[...].astype(f32)
    gap = jnp.where(lane < patch, seen - patches, 0.0)
    root = jnp.sqrt(gap * gap + 1.0)
    g_out = valid * (2.0 * gap + gap / root) / count
    raw = jnp.where(is_code, seen, 0.0)
    shrink = lax.rsqrt(jnp.sum(raw * raw, axis=-1, keepdims=True) + 1.0)
    latent = raw * shrink
    away = latent - looked
    g_latent = (2.0 * commit_weight) * away / count
    g_raw = shrink * (g_latent - latent * jnp.sum(g_latent * latent, axis=-1, keepdims=True))
    losses = jnp.where(encoder, commit_weight * away * away, valid * (gap * gap + root - 1.0))
    stat_ref[3:4, 0:256] += jnp.sum(losses, axis=0, keepdims=True)
    start = patch // 128 * 128
    latent_ref[...] = latent[:, start : start + 128].T[patch - start : patch - start + cdim, :]
    g_head = jnp.where(
        encoder, jnp.where(is_code, g_raw, 0.0), jnp.where(lane < patch, g_out, 0.0)
    ).astype(bf16)
    head_ref[rows, :] = g_head
    g_final = mm(g_head, thin_ref[...], NT)
    stat_ref[2:3, :] += jnp.sum(g_final * unit, axis=0, keepdims=True)
    g_result = norm_pull(g_final, unit, inverse, gain_final)

    low = g_result.astype(bf16)
    low_t_ref[:, rows] = low.T
    g_two = None
    for i, rest in enumerate(rests):
        g_before = (mm(low, rest[:, down]) * slopes[i]).astype(bf16)
        gbefore_ref[rows, i * units : (i + 1) * units] = g_before
        part = mm(g_before, rest[:, up], NT)
        g_two = part if g_two is None else g_two + part
    stat_ref[1:2, :] += jnp.sum(g_two * unit_two, axis=0, keepdims=True)
    g_middle = g_result + norm_pull(g_two, unit_two, inverse_two, gain_two)
    gm_ref[...] = g_middle
    branch = g_middle.astype(bf16)
    branch_t_ref[:, rows] = branch.T
    for ref, rest in zip((go_a_ref, go_b_ref), rests):
        ref[...] = mm(branch, rest[:, out]).astype(bf16)

    @pl.when(step == pl.num_programs(0) - 1)
    def _():
        head_grad_ref[...] = mm(final_t_ref[...], head_ref[...])
        split = keep_ref.shape[0]
        for i in range(2):
            first = i * (half + 2 * units)
            for ref, part in ((keep_ref, slice(0, split)), (sent_ref, slice(split, 2 * split))):
                ref[:, first : first + half] = mm(branch_t_ref[part, :], mixeds[i][...]).astype(bf16)
                for at in range(0, units, 512):
                    columns = slice(i * units + at, i * units + at + 512)
                    here = first + half + at
                    ref[:, here : here + 512] = mm(two_t_ref[part, :], gbefore_ref[:, columns]).astype(bf16)
                    here += units
                    ref[:, here : here + 512] = mm(low_t_ref[part, :], active_ref[:, columns]).astype(bf16)


def middle(side, mixed, hidden, patches, looked, valid, rest, thin, gains, at, patch, cdim, block=512):
    width = hidden.shape[1]
    half = mixed[0].shape[1]
    each = rest[0].shape[1] // 2
    hiddens = each - half
    thin_spec = pl.BlockSpec((width // 2, 256), lambda i: (0, at // 256))
    return call(
        functools.partial(middle_kernel, patch, cdim),
        "middle",
        [((SEQ, half), bf16)] * 2
        + [((SEQ, width), f32), ((cdim, SEQ), f32)]
        + [(rest[0].shape, bf16)] * 2
        + [((width, 256), f32), ((8, width), f32)],
        flops=16 << 30,
        nbytes=20 << 20,
        limit=40 << 20,
        grid=(SEQ // block,),
        in_specs=[SCALAR]
        + [whole()] * 2
        + [rows_of(block, width)]
        + [rows_of(block, 256)] * 3
        + [pl.BlockSpec(memory_space=pl.ANY)] * 2
        + [thin_spec] * 2
        + [whole()],
        out_specs=[rows_of(block, half)] * 2
        + [rows_of(block, width), columns_of(cdim, block)]
        + [whole()] * 4,
        scratch_shapes=[
            pltpu.VMEM((SEQ, hiddens), bf16),
            pltpu.VMEM((SEQ, hiddens), bf16),
            pltpu.VMEM((width, SEQ), bf16),
            pltpu.VMEM((width, SEQ), bf16),
            pltpu.VMEM((width, SEQ), bf16),
            pltpu.VMEM((width, SEQ), bf16),
            pltpu.VMEM((SEQ, 256), bf16),
            pltpu.VMEM((width, each), bf16),
            pltpu.VMEM((width, each), bf16),
            pltpu.VMEM((width, 256), bf16),
            pltpu.SemaphoreType.DMA((4,)),
        ],
    )(side, *mixed, hidden, patches, looked, valid, *rest, *thin, gains)


def project_grad_kernel(normed_t_ref, *refs):
    grads, outs = refs[:6], refs[6:]
    split = outs[0].shape[0]
    for i, ref in enumerate(outs):
        normed_t = normed_t_ref[i * split : (i + 1) * split, :]
        for j in range(3):
            both = jnp.concatenate([grads[j][...], grads[3 + j][...]], axis=1)
            width = both.shape[1]
            ref[:, j * width : (j + 1) * width] = mm(normed_t, both).astype(bf16)


def project_grad(normed_t, first, second):
    width = normed_t.shape[0]
    return call(
        project_grad_kernel,
        "project_grad",
        [((width // 2, 12 * HD), bf16)] * 2,
        flops=2 << 30,
        nbytes=5 << 20,
        limit=16 << 20,
        in_specs=[whole()] * 7,
        out_specs=[whole()] * 2,
    )(normed_t, *first, *second)


def leave_kernel(*refs):
    grads = refs[:12]
    (
        hidden_ref, gm_ref, low_a_ref, high_a_ref, low_b_ref, high_b_ref, gains_ref,
        gin_ref, gin_t_ref, gain_ref,
    ) = refs[12:]

    @pl.when(pl.program_id(0) == 0)
    def _():
        gain_ref[...] = jnp.zeros_like(gain_ref)

    gain = gains_ref[0:1, :]
    unit, inverse = normed_of(hidden_ref[...])
    g_normed = None
    for i, rest in enumerate(((low_a_ref, high_a_ref), (low_b_ref, high_b_ref))):
        first, second = grads[6 * i : 6 * i + 3], grads[6 * i + 3 : 6 * i + 6]
        side_by_side = jnp.concatenate(
            [r[...] for pair in zip(first, second) for r in pair], axis=1
        )
        part = to_two(side_by_side, *rest)
        g_normed = part if g_normed is None else g_normed + part
    gain_ref[0:1, :] += jnp.sum(g_normed * unit, axis=0, keepdims=True)
    g_in = (gm_ref[...] + norm_pull(g_normed, unit, inverse, gain)).astype(bf16)
    gin_ref[...] = g_in
    gin_t_ref[...] = g_in.T


def leave(grads, hidden, gm, a, b, gains, block=256):
    width = hidden.shape[1]
    wide = b[0].shape[1]
    wide_spec = pl.BlockSpec((width // 2, wide), lambda i: (0, 0))
    return call(
        leave_kernel,
        "leave",
        [((SEQ, width), bf16), ((width, SEQ), bf16), ((8, width), f32)],
        flops=4 << 30,
        nbytes=8 << 20,
        limit=24 << 20,
        grid=(SEQ // block,),
        in_specs=[rows_of(block, 2 * HD)] * 12
        + [rows_of(block, width)] * 2
        + [wide_spec] * 4
        + [whole()],
        out_specs=[
            rows_of(block, width),
            columns_of(width, block),
            pl.BlockSpec((8, width), lambda i: (0, 0)),
        ],
    )(*grads, hidden, gm, *a, *b, gains)


def finish_kernel(
    patch, cdim, aligned, side_ref, code_ref, code_row_ref, gin_ref, patches_ref, looked_ref, latent_ref,
    thin_low_ref, thin_high_ref, gains_ref, gin_t_ref, head_ref, stat_ref, gain_one_ref, keep_ref, sent_ref, *more,
):
    if aligned:
        entered_ref, gain_ref, sum_ref = more
    else:
        book_ref, entered_ref, gain_ref, sum_ref = more
    step = pl.program_id(0)
    tokens = gin_ref.shape[0]
    rows = pl.ds(pl.multiple_of(step * tokens, tokens), tokens)
    encoder = side_ref[0] == 0
    g_in = gin_ref[...]
    looked = looked_ref[...].astype(f32)
    entered_ref[rows, :] = jnp.where(encoder, patches_ref[...].astype(f32), looked).astype(bf16)

    @pl.when(step == 0)
    def _():
        sum_ref[...] = jnp.zeros_like(sum_ref)

    start = patch // 128 * 128
    before, later = patch - start, 128 - (patch - start) - cdim
    pieces = [jnp.zeros((before, tokens), f32)] if before else []
    pieces.append(latent_ref[...])
    pieces += [jnp.zeros((later, tokens), f32)] if later else []
    latent = jnp.concatenate(pieces, axis=0).T
    latent = jnp.concatenate([jnp.zeros((tokens, start), f32), latent], axis=1)
    lane = lanes(tokens, 256)
    is_code = (lane >= patch) & (lane < patch + cdim)
    count = gains_ref[3:4, 0:1]
    g_looked = (
        by_two(g_in, thin_low_ref, thin_high_ref)
        + (2.0 * commit_weight) * (looked - latent) / count
    )
    g_looked = jnp.where(encoder, 0.0, jnp.where(is_code, g_looked, 0.0)).astype(bf16)
    row = lax.broadcasted_iota(jnp.int32, (256, 128), 0)
    tiled = jnp.where(lanes(256, 128) % cdim + patch == row, 1.0, 0.0).astype(bf16)
    copies = mm(g_looked, tiled)
    per = 128 // cdim
    away = code_ref[...] // LO - lanes(tokens, 128) // cdim
    spread = jnp.concatenate(
        [
            jnp.where(away == i * per, copies, 0.0).astype(bf16)
            for i in range(sum_ref.shape[1] // 128)
        ],
        axis=1,
    )
    low_row = code_row_ref[...] & (LO - 1)
    onehot = jnp.where(
        lax.broadcasted_iota(jnp.int32, (LO, tokens), 0) == low_row, 1.0, 0.0
    ).astype(bf16)
    sum_ref[...] += mm(onehot, spread)

    @pl.when(step == pl.num_programs(0) - 1)
    def _():
        offset = patch + cdim - 128
        gain_ref[...] = jnp.zeros_like(gain_ref)
        gain_ref[offset : offset + 1, :] = gain_one_ref[0:1, :]
        gain_ref[offset + 1 : offset + 3, :] = stat_ref[1:3, :]
        thin = head_ref[...] + mm(gin_t_ref[...], entered_ref[...])
        ends = gain_ref[...].T
        split = keep_ref.shape[0]
        for i, ref in enumerate((keep_ref, sent_ref)):
            here = slice(i * split, (i + 1) * split)
            ref[:, :128] = thin[here, :128].astype(bf16)
            ref[:, 128:256] = (thin[here, 128:] + ends[here, :]).astype(bf16)
            if aligned:
                blocks = split // aligned
                for b in range(blocks):
                    at = (i * blocks + b) * 128
                    for j in range(LO // aligned):
                        ref[b * aligned : (b + 1) * aligned, 256 + j * 128 : 384 + j * 128] = sum_ref[
                            j * aligned : (j + 1) * aligned, at : at + 128
                        ].astype(bf16)
        if not aligned:
            book_ref[...] = sum_ref[...].astype(bf16)


def finish(side, code, code_row, gin, patches, looked, latent, a, gains, gin_t, head, stat, gain_one, wide, aligned, patch, cdim, codes, block=256):
    width = gin.shape[1]
    table = (LO, codes // LO * cdim)
    columns = 256 + (LO // aligned * 128 if aligned else 0)
    thin_spec = pl.BlockSpec((width // 2, 256), lambda i: (0, wide // 256))
    return call(
        functools.partial(finish_kernel, patch, cdim, aligned),
        "finish",
        [((width // 2, columns), bf16)] * 2 + ([] if aligned else [(table, bf16)]),
        flops=4 << 30,
        nbytes=8 << 20,
        limit=24 << 20,
        grid=(SEQ // block,),
        in_specs=[SCALAR, rows_of(block, 128), columns_of(1, block), rows_of(block, width)]
        + [rows_of(block, 256)] * 2
        + [columns_of(cdim, block)]
        + [thin_spec] * 2
        + [whole()] * 5,
        out_specs=[whole()] * (2 if aligned else 3),
        scratch_shapes=[
            pltpu.VMEM((SEQ, 256), bf16),
            pltpu.VMEM((128, width), f32),
            pltpu.VMEM(table, f32),
        ],
    )(side, code, code_row, gin, patches, looked, latent, *a, gains, gin_t, head, stat, gain_one)


def untangle(block, per, cdim):
    rows = block.shape[0]
    step = per * cdim
    tall = jnp.concatenate([block[:, j * step : (j + 1) * step] for j in range(LO // rows)], axis=0)
    if step < 128:
        tall = jnp.concatenate([tall, jnp.zeros((LO, 128 - step), f32)], axis=1)
    turned = tall.T
    return jnp.concatenate([turned[i * cdim : (i + 1) * cdim, :] for i in range(per)], axis=1)


def settle_kernel(own_ref, sent_ref, qkv_own_ref, qkv_sent_ref, thin_ref, book_ref, stat_ref, thin_out_ref, book_out_ref, total_ref):
    cdim, codes_here = book_ref.shape
    book = book_ref[...].astype(bf16).astype(f32)
    shrink = lax.rsqrt(jnp.sum(book * book, axis=0, keepdims=True) + 1.0)
    unit = book * shrink
    grad = untangle(thin_ref[:, 256:], codes_here // LO, cdim)
    grad = shrink * (grad - unit * jnp.sum(grad * unit, axis=0, keepdims=True))
    book_out_ref[...] = grad
    small = thin_ref[:, :256]
    thin_out_ref[...] = small

    def total(value):
        return jnp.sum(jnp.sum(value * value, axis=0, keepdims=True), axis=1, keepdims=True)

    squares = total(grad) + total(small)
    for ref in (own_ref, sent_ref, qkv_own_ref, qkv_sent_ref):
        squares += total(ref[...])
    loss = jnp.sum(stat_ref[3:4, :], axis=1, keepdims=True)
    row = lax.broadcasted_iota(jnp.int32, (8, 128), 0)
    total_ref[...] = jnp.where(row == 0, squares, jnp.where(row == 1, loss, 0.0))


def settle(rest_own, rest_sent, qkv_own, qkv_sent, thin, book_t, stat):
    return call(
        settle_kernel,
        "settle",
        [((thin.shape[0], 256), f32), (book_t.shape, f32), ((8, 128), f32)],
        nbytes=1 << 20,
        limit=12 << 20,
        in_specs=[whole()] * 7,
        out_specs=[whole()] * 3,
    )(rest_own, rest_sent, qkv_own, qkv_sent, thin, book_t, stat)


def adam(master, moment, square, clipped, rate):
    moment_new = first_decay * moment + (1.0 - first_decay) * clipped
    square_new = second_decay * square + (1.0 - second_decay) * clipped * clipped
    moment_hat = moment_new / (1.0 - first_decay**STEP)
    square_hat = square_new / (1.0 - second_decay**STEP)
    updated = master - rate * (
        moment_hat / (jnp.sqrt(square_hat) + adam_epsilon) + weight_decay * master
    )
    return updated, moment_new, square_new


def update_kernel(side_ref, *refs):
    grads, weights, outs = refs[:9], refs[9:27], refs[27:45]
    norm_ref, turn_ref = refs[45:]
    total_ref, own_ref, got_ref, qkv_own_ref, qkv_got_ref, small_own_ref, small_got_ref, book_own_ref, book_got_ref = grads
    side = side_ref[0]
    encoder = side == 0
    norm = jnp.sqrt(total_ref[0:1, 0:1])
    norm_ref[...] = jnp.broadcast_to(norm, norm_ref.shape)
    factor = clip_norm / jnp.maximum(norm, clip_norm)

    def apply(which, index, grad):
        three = [weights[3 * which + i][index] for i in range(3)]
        for i, value in enumerate(adam(*three, grad * factor, learn_rates[which])):
            outs[3 * which + i][index] = value

    half = weights[0].shape[3]
    units = weights[3].shape[3]
    rows = own_ref.shape[0]
    patch = weights[6].shape[2]
    cdim = weights[9].shape[1]
    gains = []
    for at, rest, qkv, small in (
        (side, own_ref, qkv_own_ref, small_own_ref),
        (1 - side, got_ref, qkv_got_ref, small_got_ref),
    ):
        for j in range(3):
            apply(0, (at, j), qkv[:, j * half : (j + 1) * half])
        apply(0, (at, 3), rest[:, :half])
        for j in range(2):
            apply(1, (at, j), rest[:, half + j * units : half + (j + 1) * units])
        apply(2, (at,), small[:, :patch])
        turn_ref[0:rows, :] = small[:, 128:256]
        turned = turn_ref[...].T[:, :rows]
        first = patch - 128
        apply(3, (at,), turned[first : first + cdim])
        gains.append(turned[first + cdim : first + cdim + 3])
    apply(4, (slice(None),), jnp.where(encoder, book_got_ref[...], book_own_ref[...]))
    apply(5, (slice(0, 3),), jnp.where(encoder, gains[0], gains[1]))
    apply(5, (slice(3, 6),), jnp.where(encoder, gains[1], gains[0]))


def update(side, grads, weights):
    out = [(w.shape, f32) for w in weights] + [((8, 128), f32)]
    return pl.pallas_call(
        update_kernel,
        name="update",
        out_shape=[jax.ShapeDtypeStruct(s, d) for s, d in out],
        in_specs=[SCALAR] + [whole()] * (len(grads) + len(weights)),
        out_specs=[whole()] * len(out),
        scratch_shapes=[pltpu.VMEM((128, 128), f32)],
        compiler_params=pltpu.CompilerParams(vmem_limit_bytes=24 << 20),
        cost_estimate=pl.CostEstimate(flops=1 << 22, bytes_accessed=10 << 20, transcendentals=0),
    )(side, *grads, *weights)


def body(
    pixels,
    valid_mask,
    code_index,
    attention_weight,
    attention_moment,
    attention_square,
    feedforward_weight,
    feedforward_moment,
    feedforward_square,
    pixel_weight,
    pixel_moment,
    pixel_square,
    code_weight,
    code_moment,
    code_square,
    codebook,
    codebook_moment,
    codebook_square,
    norm_gains,
    gains_moment,
    gains_square,
):
    side = lax.axis_index("mp")
    place = lax.axis_index("dp")
    parts = lax.axis_size("dp")
    bits = bits_of(parts)
    encoder = side == 0
    flag = side.astype(jnp.int32).reshape(1)
    rows = attention_weight.shape[2]
    half = attention_weight.shape[3]
    units = feedforward_weight.shape[3]
    patch = pixel_weight.shape[1]
    cdim = code_weight.shape[1]
    codes_here = codebook.shape[0]
    codes = codes_here * parts
    per = codes_here // LO
    wide = 3 * half
    aligned = rows if per * cdim == 128 and rows % 16 == 0 else 0

    pixels_t, valid_t = pixels.T, valid_mask.T
    own_a, sent_b = pack_first(
        flag, attention_weight, pixel_weight.transpose(0, 2, 1), code_weight, codebook.T,
        norm_gains, valid_t,
    )
    held_a = widen(own_a, 0)
    got_b = swap_mp(sent_b)

    turned = place_of((code_index // codes_here) ^ place, place & 1, bits)
    code_row = (turned * codes_here + code_index % codes_here)[None, :]
    rest_own, rest_sent, patches, valid, code_column = pack_rest(
        flag, attention_weight, feedforward_weight, pixels_t, after(valid_t, sent_b), code_row
    )
    held_a, rest_sent = together(held_a, rest_sent)
    rest_got = swap_mp(rest_sent)
    held_b = widen(after(got_b, held_a), 0)
    held_a = widen(held_a, 1)
    early = widen(after(jnp.concatenate([rest_own, rest_got], axis=1), held_a), 0)
    held_b = widen(after(held_b, held_a), 1)
    for step in range(2, bits - 1):
        held_a = widen(held_a, step)
    a = (held_a, swap_core(held_a))
    early = after(early, held_a)
    for step in range(2, bits - 1):
        held_b = widen(after(held_b, held_a), step)

    book = None
    if not aligned:
        book = jnp.concatenate(a)[:, wide + 256 :].reshape(parts, rows, LO // rows, per * cdim)
        book = book.transpose(2, 1, 0, 3).reshape(LO, -1)
    hidden, looked, qkv_a, normed, normed_t, gains = enter(
        flag, code_column, patches, a, book, aligned, wide, patch, cdim, codes
    )
    qkv_a, held_b = together(qkv_a, held_b)
    b = (held_b, swap_core(held_b))
    mixed_a, log_a = attend(qkv_a)
    rest = widen(early, 1, (mixed_a,))
    rest, normed = together(rest, normed, mixed_a)[:2]
    for step in range(2, bits - 1):
        rest = widen(rest, step, (mixed_a,))
    qkv_b = project(normed, b)
    mixed_b, log_b = attend(qkv_b)
    rest = after(rest, mixed_b)
    rest = (rest, swap_core(rest))

    go_a, go_b, g_middle, latent, keep_r, sent_r, g_head, stat = middle(
        flag, (mixed_a, mixed_b), hidden, patches, looked, valid, rest, a, gains, wide, patch, cdim
    )
    last = bits - 2
    grads_a0 = attend_back(qkv_a, mixed_a, go_a, log_a, 0)
    latent_there = swap_mp(after(latent, *grads_a0))
    rest = halves(fold((keep_r, sent_r), None, grads_a0))
    grads_a1 = attend_back(after(qkv_a, *rest), mixed_a, go_a, log_a, 1)
    keep_a, sent_a = project_grad(normed_t, grads_a0, grads_a1)
    grads_b0 = attend_back(after(qkv_b, keep_a), mixed_b, go_b, log_b, 0)
    rest = halves(fold(rest, last, grads_b0))
    part_a = halves(fold((keep_a, sent_a), None, grads_b0))
    grads_b1 = attend_back(after(qkv_b, *part_a, *rest), mixed_b, go_b, log_b, 1)
    keep_b, sent_b = project_grad(normed_t, grads_b0, grads_b1)
    part_a = halves(fold(part_a, last, (keep_b,)))
    g_in, gin_t, gain_one = leave(
        grads_a0 + grads_a1 + grads_b0 + grads_b1, after(hidden, *part_a), g_middle, a, b, gains
    )
    part_b = halves(fold((keep_b, sent_b), None, (gin_t,)))
    keep_s, sent_s, *g_book = finish(
        flag, code_column, code_row, after(g_in, *part_b), patches, looked, latent_there,
        a, gains, gin_t, g_head, stat, gain_one, wide, aligned, patch, cdim, codes,
    )
    for step in range(last - 1, 0, -1):
        rest = halves(fold(rest, step, (gin_t,)))
    if not aligned:
        g_book = g_book[0].reshape(LO // rows, rows, parts, per * cdim)
        g_book = g_book.transpose(2, 1, 0, 3).reshape(2, parts * rows // 2, -1)
        keep_s = jnp.concatenate([keep_s, g_book[0]], axis=1)
        sent_s = jnp.concatenate([sent_s, g_book[1]], axis=1)
    keep_s, sent_s, *rest = together(keep_s, sent_s, *rest)
    thin = fold((keep_s, sent_s), None)
    part_a, part_b = fold(part_a, last - 1, (keep_s,)), fold(part_b, last, (keep_s,))
    for step in range(last, -1, -1):
        thin = fold(halves(thin), step)
        if step > 0:
            part_b = fold(halves(part_b), step - 1)
        if step > 1:
            part_a = fold(halves(part_a), step - 2)
        if step == last:
            rest = added(fold(rest, 0, (thin[0],)))
            rest_got = swap_mp(rest[:, rest.shape[1] // 2 :])
    thin, part_a, part_b = added(thin), added(part_a), added(part_b)
    qkv_own, qkv_sent = part_a, part_b
    rest_own, rest_sent = rest[:, : rest.shape[1] // 2], rest[:, rest.shape[1] // 2 :]
    qkv_got = swap_mp(qkv_sent)
    small_own, book_own, totals = settle(
        rest_own, rest_sent, qkv_own, qkv_sent, thin, codebook.T, stat
    )
    small_got, book_got = swap_mp(small_own), swap_mp(book_own)
    totals = all_sum(totals)
    thin_view = (0, 2, 1)
    weights = (
        attention_weight,
        attention_moment,
        attention_square,
        feedforward_weight,
        feedforward_moment,
        feedforward_square,
        pixel_weight.transpose(thin_view),
        pixel_moment.transpose(thin_view),
        pixel_square.transpose(thin_view),
        code_weight,
        code_moment,
        code_square,
        codebook.T,
        codebook_moment.T,
        codebook_square.T,
        norm_gains,
        gains_moment,
        gains_square,
    )
    grads = (
        totals, rest_own, rest_got, qkv_own, qkv_got, small_own, small_got, book_own, book_got
    )
    *new, norm_total = update(flag, grads, weights)
    new[6:9] = [x.transpose(thin_view) for x in new[6:9]]
    new[12:15] = [x.T for x in new[12:15]]
    return tuple(new) + (totals[1, 0], gains[3, 0], norm_total[0, 0])


def solution(mesh):
    wide = P(None, None, "dp", "mp")
    thin = P(None, None, "dp")
    rows = P("dp", None)
    gain = P(None, "dp")
    weights = (wide,) * 6 + (thin,) * 6 + (rows,) * 3 + (gain,) * 3
    return jax.shard_map(
        body,
        mesh=mesh,
        in_specs=(rows, rows, P("dp")) + weights,
        out_specs=weights + (P(), P(), P()),
        check_vma=False,
    )
```

```python
import functools

import jax
import jax.numpy as jnp
from jax import lax
from jax.experimental import pallas as pl
from jax.experimental.pallas import tpu as pltpu
from jax.sharding import PartitionSpec as P

HD = 64
SEQ = 1024
STEP = 10

norm_epsilon = 1e-05
commit_weight = 0.25
clip_norm = 0.003
learn_rates = (0.2, 0.02, 0.04, 0.5, 0.5, 0.6)
first_decay = 0.9
second_decay = 0.999
weight_decay = 0.01
adam_epsilon = 1e-08

bf16 = jnp.bfloat16
f32 = jnp.float32


def swap_mp(value):
    return lax.ppermute(value, "mp", [(0, 1), (1, 0)])


def bits_of(size):
    return size.bit_length() - 1


def step_orders(bits):
    high = list(range(bits - 1, 1, -1))
    return (high + [1], [1] + high)


def swap_step(value, step):
    size = lax.axis_size("dp")
    orders = step_orders(bits_of(size))
    return lax.ppermute(value, "dp", [(i, i ^ (1 << orders[i & 1][step])) for i in range(size)])


def swap_core(value):
    return lax.ppermute(value, "dp", [(i, i ^ 1) for i in range(lax.axis_size("dp"))])


def place_of(mask, core, bits):
    places = [
        sum(((mask >> bit) & 1) << step for step, bit in enumerate(order))
        for order in step_orders(bits)
    ]
    same = mask & 1 == 0
    return jnp.where(same == (core == 0), places[0], places[1]) + jnp.where(same, 0, 1 << (bits - 1))


def after(value, *others):
    return lax.optimization_barrier((value,) + others)[0]


def together(*arrays):
    return lax.optimization_barrier(arrays)


def widen(held, step, later=()):
    got = swap_step(held, step)
    if later:
        held = after(held, *later)
    return jnp.concatenate([held, got], axis=0)


def fold(pair, step, later=()):
    keep, sent = pair
    got = swap_core(sent) if step is None else swap_step(sent, step)
    if later:
        keep = after(keep, *later)
    return keep, got


def added(pair):
    return pair[0].astype(f32) + pair[1].astype(f32)


def halves(pair):
    split = pair[0].shape[0] // 2
    keep = added([x[:split] for x in pair])
    return together(keep, added([x[split:] for x in pair]).astype(bf16))


def all_sum(value):
    size = lax.axis_size("dp")
    for bit in range(1, bits_of(size)):
        value = value + lax.ppermute(value, "dp", [(i, i ^ (1 << bit)) for i in range(size)])
    return value + swap_mp(value)


NN = (((1,), (0,)), ((), ()))
NT = (((1,), (1,)), ((), ()))
VMEM_LIMIT = 48 << 20
LO = 128


def mm(a, b, dims=NN):
    return lax.dot_general(a, b, dims, preferred_element_type=f32)


def whole():
    return pl.BlockSpec(memory_space=pltpu.VMEM)


def rows_of(block, width):
    return pl.BlockSpec((block, width), lambda i: (i, 0))


def columns_of(height, block):
    return pl.BlockSpec((height, block), lambda i: (0, i))


def call(kernel, name, out, flops=0, nbytes=0, exps=0, limit=VMEM_LIMIT, **kw):
    return pl.pallas_call(
        kernel,
        name=name,
        out_shape=[jax.ShapeDtypeStruct(s, d) for s, d in out],
        compiler_params=pltpu.CompilerParams(vmem_limit_bytes=limit),
        cost_estimate=pl.CostEstimate(flops=flops, bytes_accessed=nbytes, transcendentals=exps),
        **kw,
    )


SCALAR = pl.BlockSpec(memory_space=pltpu.SMEM)


def attend_kernel(q_ref, k_ref, v_ref, o_ref, log_ref, vt_ref):
    vt_ref[...] = v_ref[...].T
    keys = k_ref[...]
    q = q_ref[...] * jnp.asarray(HD**-0.5, bf16)
    low = lax.broadcasted_iota(jnp.int32, q.shape, 1) < HD
    zero = jnp.zeros_like(q)
    mixed = []
    for head in range(2):
        own = jnp.where(low if head == 0 else ~low, q, zero)
        s = mm(keys, own, NT)
        peak = jnp.max(s, axis=0, keepdims=True)
        e = jnp.exp(s - peak)
        total = jnp.sum(e, axis=0, keepdims=True)
        part = mm(vt_ref[head * HD : (head + 1) * HD, :], e.astype(bf16))
        mixed.append(part * (1.0 / total))
        log_ref[0, head : head + 1, :] = peak + jnp.log(total)
    o_ref[...] = jnp.concatenate(mixed, axis=0).T.astype(bf16)


def column_block(at):
    return pl.BlockSpec((SEQ, 2 * HD), lambda i: (0, at + i))


def attend(qkv, first, count):
    pairs = qkv.shape[1] // (6 * HD)
    return call(
        attend_kernel,
        "attend",
        [((SEQ, 2 * HD * count), bf16), ((count, 2, SEQ), f32)],
        flops=count * 8 * SEQ * SEQ * 256,
        nbytes=16 * SEQ * HD * count,
        limit=28 << 20,
        grid=(count,),
        in_specs=[column_block(first), column_block(pairs + first), column_block(2 * pairs + first)],
        out_specs=[column_block(0), pl.BlockSpec((1, 2, SEQ), lambda i: (i, 0, 0))],
        scratch_shapes=[pltpu.VMEM((2 * HD, SEQ), bf16)],
    )(qkv, qkv, qkv)


def attend_back_kernel(
    chunk, q_ref, k_ref, v_ref, o_ref, go_ref, log_ref, gq_ref, gk_ref, gv_ref, kt_ref, sk_ref, sv_ref
):
    kt_ref[...] = k_ref[...].T
    keys = k_ref[...]
    values = v_ref[...]
    low = lax.broadcasted_iota(jnp.int32, (chunk, 2 * HD), 1) < HD
    scale = HD**-0.5
    for start in range(0, SEQ, chunk):
        rows = pl.ds(start, chunk)
        q = q_ref[rows, :] * jnp.asarray(scale, bf16)
        go = go_ref[rows, :]
        product = (go.astype(f32) * o_ref[rows, :].astype(f32)).T
        zero = jnp.zeros_like(q)
        grads = []
        sums = None
        for head in range(2):
            here = low if head == 0 else ~low
            own = jnp.where(here, q, zero)
            own_go = jnp.where(here, go, zero)
            inner = jnp.sum(product[head * HD : (head + 1) * HD, :], axis=0, keepdims=True)
            p = jnp.exp(mm(keys, own, NT) - log_ref[0, head : head + 1, rows])
            gp = mm(values, own_go, NT)
            gs = (p * (gp - inner)).astype(bf16)
            gk = mm(gs, own)
            gv = mm(p.astype(bf16), own_go)
            sums = (gk, gv) if head == 0 else (sums[0] + gk, sums[1] + gv)
            grads.append(mm(kt_ref[head * HD : (head + 1) * HD, :], gs))
        gq_ref[rows, :] = (jnp.concatenate(grads, axis=0).T * scale).astype(bf16)
        if start == 0:
            sk_ref[...] = sums[0]
            sv_ref[...] = sums[1]
        elif start + chunk < SEQ:
            sk_ref[...] += sums[0]
            sv_ref[...] += sums[1]
        else:
            gk_ref[...] = (sk_ref[...] + sums[0]).astype(bf16)
            gv_ref[...] = (sv_ref[...] + sums[1]).astype(bf16)


def attend_back(qkv, o, go, log_total, pair, at, chunk=512):
    pairs = go.shape[1] // (2 * HD)
    return call(
        functools.partial(attend_back_kernel, chunk),
        "attend_back",
        [((SEQ, 2 * HD), bf16)] * 3,
        flops=20 * SEQ * SEQ * 256,
        nbytes=16 * SEQ * 128,
        limit=20 << 20,
        grid=(1,),
        in_specs=[
            column_block(pair),
            column_block(pairs + pair),
            column_block(2 * pairs + pair),
            column_block(at),
            column_block(pair),
            pl.BlockSpec((1, 2, SEQ), lambda i: (at, 0, 0)),
        ],
        out_specs=[column_block(0)] * 3,
        scratch_shapes=[
            pltpu.VMEM((2 * HD, SEQ), bf16),
            pltpu.VMEM((SEQ, 2 * HD), f32),
            pltpu.VMEM((SEQ, 2 * HD), f32),
        ],
    )(qkv, qkv, qkv, o, go, log_total)


def lanes(rows, columns):
    return lax.broadcasted_iota(jnp.int32, (rows, columns), 1)


def normed_of(hidden):
    centred = hidden - jnp.mean(hidden, axis=-1, keepdims=True)
    spread = jnp.mean(centred * centred, axis=-1, keepdims=True)
    inverse = lax.rsqrt(spread + norm_epsilon)
    return centred * inverse, inverse


def norm_pull(grad, unit, inverse, gain):
    scaled = grad * gain
    return inverse * (
        scaled
        - jnp.mean(scaled, axis=-1, keepdims=True)
        - unit * jnp.mean(scaled * unit, axis=-1, keepdims=True)
    )


def by_two(value, low_ref, high_ref, columns=slice(None)):
    split = low_ref.shape[0]
    return mm(value[:, :split], low_ref[:, columns]) + mm(value[:, split:], high_ref[:, columns])


def to_two(value, low_ref, high_ref, columns=slice(None)):
    return jnp.concatenate(
        [mm(value, low_ref[:, columns], NT), mm(value, high_ref[:, columns], NT)], axis=1
    )


def pack_kernel(
    side_ref, attention_ref, feedforward_ref, pixel_ref, code_ref, book_ref, gains_ref, valid_ref,
    own_ref, rest_ref, sent_ref, turn_ref,
):
    side = side_ref[0]
    rows, half = attention_ref.shape[2], attention_ref.shape[3]
    units = feedforward_ref.shape[3]
    patch, cdim = pixel_ref.shape[2], code_ref.shape[1]
    at = 3 * half
    for j in range(3):
        own_ref[:, j * half : (j + 1) * half] = attention_ref[side, j].astype(bf16)
        sent_ref[:, j * half : (j + 1) * half] = attention_ref[1 - side, j].astype(bf16)
    for ref, which, first in ((rest_ref, side, 0), (sent_ref, 1 - side, at)):
        ref[:, first : first + half] = attention_ref[which, 3].astype(bf16)
        for j in range(2):
            here = first + half + j * units
            ref[:, here : here + units] = feedforward_ref[which, j].astype(bf16)
    count = jnp.sum(valid_ref[...], axis=0, keepdims=True)
    count = jnp.sum(count.astype(f32), axis=1, keepdims=True).astype(jnp.int32)
    first = patch - 128
    turn_ref[...] = jnp.zeros_like(turn_ref)
    turn_ref[first : first + cdim, 0:rows] = code_ref[side]
    first += cdim
    turn_ref[first : first + 3, 0:rows] = jnp.where(side == 0, gains_ref[0:3, :], gains_ref[3:6, :])
    digits = (count & 255, (count >> 8) & 255, count >> 16)
    for i, digit in enumerate(digits):
        turn_ref[first + 3 + i : first + 4 + i, 0:1] = digit.astype(f32)
    own_ref[:, at + 128 : at + 256] = turn_ref[...].T[0:rows, :].astype(bf16)
    own_ref[:, at : at + patch] = pixel_ref[side].astype(bf16)
    at += 256
    book = book_ref[...].astype(bf16).astype(f32)
    unit = book * lax.rsqrt(jnp.sum(book * book, axis=0, keepdims=True) + 1.0)
    per = book.shape[1] // LO
    tall = jnp.concatenate([unit[:, i * LO : (i + 1) * LO] for i in range(per)], axis=0)
    if per * cdim < 128:
        tall = jnp.concatenate([tall, jnp.zeros((128 - per * cdim, LO), f32)], axis=0)
    wide = tall.T
    step = per * cdim
    for j in range(LO // rows):
        own_ref[:, at + j * step : at + (j + 1) * step] = wide[
            j * rows : (j + 1) * rows, :step
        ].astype(bf16)


def pack(side, attention, feedforward, pixel_t, code, book_t, gains, valid_t):
    _, _, rows, half = attention.shape
    units = feedforward.shape[3]
    cdim, codes = book_t.shape
    rest = half + 2 * units
    return call(
        pack_kernel,
        "pack",
        [
            ((rows, 3 * half + 256 + cdim * codes // rows), bf16),
            ((rows, rest), bf16),
            ((rows, 3 * half + rest), bf16),
        ],
        nbytes=4 << 20,
        limit=60 << 20,
        in_specs=[SCALAR] + [whole()] * 7,
        out_specs=[whole()] * 3,
        scratch_shapes=[pltpu.VMEM((128, 128), f32)],
    )(side, attention, feedforward, pixel_t, code, book_t, gains, valid_t)


def inputs_kernel(core_ref, pixels_ref, valid_ref, code_ref, patches_ref, mask_ref, column_ref, row_ref, *, bits, codes_here):
    patch, tokens = pixels_ref.shape
    zeros = jnp.zeros((256 - patch, tokens), f32)
    patches_ref[...] = jnp.concatenate([pixels_ref[...].astype(f32), zeros], axis=0).T.astype(bf16)
    mask_ref[...] = jnp.concatenate([valid_ref[...].astype(f32), zeros], axis=0).T.astype(bf16)
    code = jnp.broadcast_to(code_ref[...], (8, tokens))
    place = core_ref[0]
    turned = place_of((code // codes_here) ^ place, place & 1, bits) * codes_here + code % codes_here
    row_ref[...] = turned[0:1, :]
    column_ref[...] = jnp.broadcast_to(turned[0:1, :].astype(f32), (128, tokens)).T.astype(jnp.int32)


def inputs(place, pixels_t, valid_t, code, bits, codes_here):
    return call(
        functools.partial(inputs_kernel, bits=bits, codes_here=codes_here),
        "inputs",
        [((SEQ, 256), bf16)] * 2 + [((SEQ, 128), jnp.int32), ((1, SEQ), jnp.int32)],
        nbytes=3 << 20,
        limit=60 << 20,
        in_specs=[SCALAR] + [whole()] * 3,
        out_specs=[whole()] * 4,
    )(place, pixels_t, valid_t, code)


def enter_kernel(
    patch, cdim, aligned, side_ref, code_ref, patches_ref, low_a_ref, high_a_ref, *refs,
):
    if aligned:
        hidden_ref, looked_ref, qkv_ref, normed_ref, normed_t_ref, gains_ref, book_ref = refs
    else:
        book_ref, hidden_ref, looked_ref, qkv_ref, normed_ref, normed_t_ref, gains_ref = refs
    step = pl.program_id(0)
    tokens = code_ref.shape[0]
    wide = qkv_ref.shape[1]
    split = low_a_ref.shape[0]
    thin = slice(wide, wide + 256)

    @pl.when(step == 0)
    def _():
        first = patch + cdim - 128
        gains_ref[...] = jnp.zeros_like(gains_ref)
        digits = 0.0
        for i, ref in enumerate((low_a_ref, high_a_ref)):
            turned = ref[:, wide + 128 : wide + 256].astype(f32).T
            gains_ref[0:3, i * split : (i + 1) * split] = turned[first : first + 3, :]
            digits += jnp.sum(turned, axis=1, keepdims=True)
        count = (
            digits[first + 3 : first + 4]
            + 256.0 * digits[first + 4 : first + 5]
            + 65536.0 * digits[first + 5 : first + 6]
        )
        gains_ref[3:4, :] = jnp.broadcast_to(count, (1, gains_ref.shape[1]))
        if aligned:
            rows = aligned
            for i, ref in enumerate((low_a_ref, high_a_ref)):
                blocks = split // rows
                for b in range(blocks):
                    at = (i * blocks + b) * 128
                    for j in range(LO // rows):
                        column = wide + 256 + j * 128
                        book_ref[j * rows : (j + 1) * rows, at : at + 128] = ref[
                            b * rows : (b + 1) * rows, column : column + 128
                        ]

    code = code_ref[...]
    low, high = code & (LO - 1), code // LO
    lane = lanes(tokens, 128)
    onehot = jnp.where(lane == low, 1.0, 0.0).astype(bf16)
    spread = mm(onehot, book_ref[...])
    group = lane // cdim
    per = 128 // cdim
    away = high - group
    picked = jnp.zeros((tokens, 128), f32)
    for i in range(spread.shape[1] // 128):
        picked += jnp.where(away == i * per, spread[:, i * 128 : (i + 1) * 128], 0.0)
    lane_out = lanes(128, 256)
    fold_in = (
        lax.broadcasted_iota(jnp.int32, (128, 256), 0) % cdim + patch == lane_out
    ) & (lane_out < patch + cdim)
    looked = mm(picked.astype(bf16), jnp.where(fold_in, 1.0, 0.0).astype(bf16)).astype(bf16)
    looked_ref[...] = looked
    encoder = side_ref[0] == 0
    entered = jnp.where(encoder, patches_ref[...].astype(f32), looked.astype(f32)).astype(bf16)
    hidden = to_two(entered, low_a_ref, high_a_ref, thin)
    hidden_ref[...] = hidden
    unit, _ = normed_of(hidden)
    normed = (unit * gains_ref[0:1, :]).astype(bf16)
    normed_t_ref[...] = normed.T
    normed_ref[...] = normed
    qkv_ref[...] = by_two(normed, low_a_ref, high_a_ref, slice(0, wide)).astype(bf16)


def enter(side, code, patches, a, book, aligned, wide, patch, cdim, codes, block=256):
    width = 2 * a[0].shape[0]
    table = (LO, codes // LO * cdim)
    return call(
        functools.partial(enter_kernel, patch, cdim, aligned),
        "enter",
        [
            ((SEQ, width), f32),
            ((SEQ, 256), bf16),
            ((SEQ, wide), bf16),
            ((SEQ, width), bf16),
            ((width, SEQ), bf16),
            ((8, width), f32),
        ],
        flops=8 << 30,
        nbytes=12 << 20,
        limit=28 << 20,
        grid=(SEQ // block,),
        in_specs=[SCALAR, rows_of(block, 128), rows_of(block, 256)]
        + [whole()] * (2 if aligned else 3),
        out_specs=[
            rows_of(block, width),
            rows_of(block, 256),
            rows_of(block, wide),
            rows_of(block, width),
            columns_of(width, block),
            pl.BlockSpec((8, width), lambda i: (0, 0)),
        ],
        scratch_shapes=[pltpu.VMEM(table, bf16)] if aligned else [],
    )(side, code, patches, *a, *([] if aligned else [book]))


def project_kernel(normed_ref, low_ref, high_ref, qkv_ref):
    qkv_ref[...] = by_two(normed_ref[...], low_ref, high_ref).astype(bf16)


def project(normed, b, block=512):
    wide = b[0].shape[1]
    return call(
        project_kernel,
        "project",
        [((SEQ, wide), bf16)],
        flops=2 << 30,
        nbytes=4 << 20,
        limit=16 << 20,
        grid=(SEQ // block,),
        in_specs=[rows_of(block, normed.shape[1]), whole(), whole()],
        out_specs=[rows_of(block, wide)],
    )(normed, *b)[0]


GELU_A, GELU_B = 0.7978845608028654, 0.044715


def middle_kernel(
    patch, cdim, runs, side_ref, *refs,
):
    mixed_refs, refs = refs[:runs], refs[runs:]
    (
    hidden_ref, patches_ref, looked_ref, valid_ref,
    low_ref, high_ref, thin_low_ref, thin_high_ref, gains_ref,
    go_a_ref, go_b_ref, gm_ref, latent_ref, keep_ref, sent_ref,
    head_grad_ref, stat_ref,
    active_ref, gbefore_ref, low_t_ref, two_t_ref, branch_t_ref, final_t_ref, head_ref,
    full_a_ref, full_b_ref, thin_ref, copy_sem,
    ) = refs
    step = pl.program_id(0)
    tokens = hidden_ref.shape[0]
    half = go_a_ref.shape[1]
    units = (low_ref.shape[1] // 2 - half) // 2
    rows = pl.ds(pl.multiple_of(step * tokens, tokens), tokens)
    encoder = side_ref[0] == 0
    rests = (full_a_ref, full_b_ref)
    out, up, down = slice(0, half), slice(half, half + units), slice(half + units, half + 2 * units)

    @pl.when(step == 0)
    def _():
        stat_ref[...] = jnp.zeros_like(stat_ref)
        split = low_ref.shape[0]
        each = half + 2 * units
        copies = [
            pltpu.make_async_copy(
                piece.at[:, pl.ds(i * each, each)],
                rests[i].at[pl.ds(j * split, split), :],
                copy_sem.at[2 * i + j],
            )
            for i in range(2)
            for j, piece in enumerate((low_ref, high_ref))
        ]
        for copy in copies:
            copy.start()
        thin_ref[:split, :] = thin_low_ref[...]
        thin_ref[split:, :] = thin_high_ref[...]
        for copy in copies:
            copy.wait()

    gain_two, gain_final = gains_ref[1:2, :], gains_ref[2:3, :]
    middle = hidden_ref[...]
    mixed = jnp.concatenate([ref[rows, :] for ref in mixed_refs], axis=1)
    for i, rest in enumerate(rests):
        middle += mm(mixed[:, i * half : (i + 1) * half], rest[:, out], NT)
    unit_two, inverse_two = normed_of(middle)
    two = (unit_two * gain_two).astype(bf16)
    two_t_ref[:, rows] = two.T
    slopes = []
    for i, rest in enumerate(rests):
        before = mm(two, rest[:, up])
        square = before * before
        bent = jnp.tanh(GELU_A * before * (1.0 + GELU_B * square))
        active_ref[rows, i * units : (i + 1) * units] = (0.5 * before * (1.0 + bent)).astype(bf16)
        slopes.append(
            0.5 * (1.0 + bent)
            + (0.5 * GELU_A) * before * (1.0 - bent * bent) * (1.0 + 3.0 * GELU_B * square)
        )

    @pl.when(step >= 0)
    def _():
        total = middle
        for i, rest in enumerate(rests):
            total += mm(active_ref[rows, i * units : (i + 1) * units], rest[:, down], NT)
        gm_ref[...] = total

    result = gm_ref[...]
    unit, inverse = normed_of(result)
    final = (unit * gain_final).astype(bf16)
    final_t_ref[:, rows] = final.T
    seen = mm(final, thin_ref[...])
    lane = lanes(tokens, 256)
    is_code = (lane >= patch) & (lane < patch + cdim)
    count = gains_ref[3:4, 0:1]
    patches = patches_ref[...].astype(f32)
    looked = looked_ref[...].astype(f32)
    valid = valid_ref[...].astype(f32)
    gap = jnp.where(lane < patch, seen - patches, 0.0)
    root = jnp.sqrt(gap * gap + 1.0)
    g_out = valid * (2.0 * gap + gap / root) / count
    raw = jnp.where(is_code, seen, 0.0)
    shrink = lax.rsqrt(jnp.sum(raw * raw, axis=-1, keepdims=True) + 1.0)
    latent = raw * shrink
    away = latent - looked
    g_latent = (2.0 * commit_weight) * away / count
    g_raw = shrink * (g_latent - latent * jnp.sum(g_latent * latent, axis=-1, keepdims=True))
    losses = jnp.where(encoder, commit_weight * away * away, valid * (gap * gap + root - 1.0))
    stat_ref[3:4, 0:256] += jnp.sum(losses, axis=0, keepdims=True)
    start = patch // 128 * 128
    latent_ref[...] = latent[:, start : start + 128].T[patch - start : patch - start + cdim, :]
    g_head = jnp.where(
        encoder, jnp.where(is_code, g_raw, 0.0), jnp.where(lane < patch, g_out, 0.0)
    ).astype(bf16)
    head_ref[rows, :] = g_head
    g_final = mm(g_head, thin_ref[...], NT)
    stat_ref[2:3, :] += jnp.sum(g_final * unit, axis=0, keepdims=True)
    g_result = norm_pull(g_final, unit, inverse, gain_final)

    low = g_result.astype(bf16)
    low_t_ref[:, rows] = low.T
    g_two = None
    for i, rest in enumerate(rests):
        g_before = (mm(low, rest[:, down]) * slopes[i]).astype(bf16)
        gbefore_ref[rows, i * units : (i + 1) * units] = g_before
        part = mm(g_before, rest[:, up], NT)
        g_two = part if g_two is None else g_two + part
    stat_ref[1:2, :] += jnp.sum(g_two * unit_two, axis=0, keepdims=True)
    g_middle = g_result + norm_pull(g_two, unit_two, inverse_two, gain_two)
    gm_ref[...] = g_middle
    branch = g_middle.astype(bf16)
    branch_t_ref[:, rows] = branch.T
    for ref, rest in zip((go_a_ref, go_b_ref), rests):
        ref[...] = mm(branch, rest[:, out]).astype(bf16)

    @pl.when(step == pl.num_programs(0) - 1)
    def _():
        head_grad_ref[...] = mm(final_t_ref[...], head_ref[...])
        split = keep_ref.shape[0]
        for i in range(2):
            first = i * (half + 2 * units)
            for ref, part in ((keep_ref, slice(0, split)), (sent_ref, slice(split, 2 * split))):
                at = 0
                for mixed_ref in mixed_refs:
                    here = at - i * half
                    at += mixed_ref.shape[1]
                    if 0 <= here < half:
                        ref[:, first + here : first + at - i * half] = mm(
                            branch_t_ref[part, :], mixed_ref[...]
                        ).astype(bf16)
                for at in range(0, units, 512):
                    columns = slice(i * units + at, i * units + at + 512)
                    here = first + half + at
                    ref[:, here : here + 512] = mm(two_t_ref[part, :], gbefore_ref[:, columns]).astype(bf16)
                    here += units
                    ref[:, here : here + 512] = mm(low_t_ref[part, :], active_ref[:, columns]).astype(bf16)


def middle(side, mixed, hidden, patches, looked, valid, rest, thin, gains, at, patch, cdim, block=512):
    width = hidden.shape[1]
    half = sum(m.shape[1] for m in mixed) // 2
    each = rest[0].shape[1] // 2
    hiddens = each - half
    thin_spec = pl.BlockSpec((width // 2, 256), lambda i: (0, at // 256))
    return call(
        functools.partial(middle_kernel, patch, cdim, len(mixed)),
        "middle",
        [((SEQ, half), bf16)] * 2
        + [((SEQ, width), f32), ((cdim, SEQ), f32)]
        + [(rest[0].shape, bf16)] * 2
        + [((width, 256), f32), ((8, width), f32)],
        flops=16 << 30,
        nbytes=20 << 20,
        limit=32 << 20,
        grid=(SEQ // block,),
        in_specs=[SCALAR]
        + [whole()] * len(mixed)
        + [rows_of(block, width)]
        + [rows_of(block, 256)] * 3
        + [whole()] * 2
        + [thin_spec] * 2
        + [whole()],
        out_specs=[rows_of(block, half)] * 2
        + [rows_of(block, width), columns_of(cdim, block)]
        + [whole()] * 4,
        scratch_shapes=[
            pltpu.VMEM((SEQ, hiddens), bf16),
            pltpu.VMEM((SEQ, hiddens), bf16),
            pltpu.VMEM((width, SEQ), bf16),
            pltpu.VMEM((width, SEQ), bf16),
            pltpu.VMEM((width, SEQ), bf16),
            pltpu.VMEM((width, SEQ), bf16),
            pltpu.VMEM((SEQ, 256), bf16),
            pltpu.VMEM((width, each), bf16),
            pltpu.VMEM((width, each), bf16),
            pltpu.VMEM((width, 256), bf16),
            pltpu.SemaphoreType.DMA((4,)),
        ],
    )(side, *mixed, hidden, patches, looked, valid, *rest, *thin, gains)


def project_grad_kernel(normed_t_ref, *refs):
    grads, outs = refs[:12], refs[12:]
    split = outs[0].shape[0]
    for i, ref in enumerate(outs):
        normed_t = normed_t_ref[i * split : (i + 1) * split, :]
        for side in range(2):
            for j in range(3):
                first, second = grads[6 * side + j], grads[6 * side + 3 + j]
                both = jnp.concatenate([first[...], second[...]], axis=1)
                width = both.shape[1]
                at = (3 * side + j) * width
                ref[:, at : at + width] = mm(normed_t, both).astype(bf16)


def project_grad(normed_t, grads):
    width = normed_t.shape[0]
    return call(
        project_grad_kernel,
        "project_grad",
        [((width // 2, 24 * HD), bf16)] * 2,
        flops=4 << 30,
        nbytes=8 << 20,
        limit=20 << 20,
        in_specs=[whole()] * 13,
        out_specs=[whole()] * 2,
    )(normed_t, *grads)


def leave_kernel(*refs):
    grads = refs[:12]
    (
        hidden_ref, gm_ref, low_a_ref, high_a_ref, low_b_ref, high_b_ref, gains_ref,
        gin_ref, gin_t_ref, gain_ref,
    ) = refs[12:]

    @pl.when(pl.program_id(0) == 0)
    def _():
        gain_ref[...] = jnp.zeros_like(gain_ref)

    gain = gains_ref[0:1, :]
    unit, inverse = normed_of(hidden_ref[...])
    g_normed = None
    for i, rest in enumerate(((low_a_ref, high_a_ref), (low_b_ref, high_b_ref))):
        first, second = grads[6 * i : 6 * i + 3], grads[6 * i + 3 : 6 * i + 6]
        side_by_side = jnp.concatenate(
            [r[...] for pair in zip(first, second) for r in pair], axis=1
        )
        part = to_two(side_by_side, *rest)
        g_normed = part if g_normed is None else g_normed + part
    gain_ref[0:1, :] += jnp.sum(g_normed * unit, axis=0, keepdims=True)
    g_in = (gm_ref[...] + norm_pull(g_normed, unit, inverse, gain)).astype(bf16)
    gin_ref[...] = g_in
    gin_t_ref[...] = g_in.T


def leave(grads, hidden, gm, a, b, gains, block=256):
    width = hidden.shape[1]
    wide = b[0].shape[1]
    wide_spec = pl.BlockSpec((width // 2, wide), lambda i: (0, 0))
    return call(
        leave_kernel,
        "leave",
        [((SEQ, width), bf16), ((width, SEQ), bf16), ((8, width), f32)],
        flops=4 << 30,
        nbytes=8 << 20,
        limit=24 << 20,
        grid=(SEQ // block,),
        in_specs=[rows_of(block, 2 * HD)] * 12
        + [rows_of(block, width)] * 2
        + [wide_spec] * 4
        + [whole()],
        out_specs=[
            rows_of(block, width),
            columns_of(width, block),
            pl.BlockSpec((8, width), lambda i: (0, 0)),
        ],
    )(*grads, hidden, gm, *a, *b, gains)


def finish_kernel(
    patch, cdim, aligned, side_ref, code_ref, code_row_ref, gin_ref, patches_ref, looked_ref, latent_ref,
    thin_low_ref, thin_high_ref, gains_ref, gin_t_ref, head_ref, stat_ref, gain_one_ref, keep_ref, sent_ref, *more,
):
    if aligned:
        entered_ref, gain_ref, sum_ref = more
    else:
        book_ref, entered_ref, gain_ref, sum_ref = more
    step = pl.program_id(0)
    tokens = gin_ref.shape[0]
    rows = pl.ds(pl.multiple_of(step * tokens, tokens), tokens)
    encoder = side_ref[0] == 0
    g_in = gin_ref[...]
    looked = looked_ref[...].astype(f32)
    entered_ref[rows, :] = jnp.where(encoder, patches_ref[...].astype(f32), looked).astype(bf16)

    @pl.when(step == 0)
    def _():
        sum_ref[...] = jnp.zeros_like(sum_ref)

    start = patch // 128 * 128
    before, later = patch - start, 128 - (patch - start) - cdim
    pieces = [jnp.zeros((before, tokens), f32)] if before else []
    pieces.append(latent_ref[...])
    pieces += [jnp.zeros((later, tokens), f32)] if later else []
    latent = jnp.concatenate(pieces, axis=0).T
    latent = jnp.concatenate([jnp.zeros((tokens, start), f32), latent], axis=1)
    lane = lanes(tokens, 256)
    is_code = (lane >= patch) & (lane < patch + cdim)
    count = gains_ref[3:4, 0:1]
    g_looked = (
        by_two(g_in, thin_low_ref, thin_high_ref)
        + (2.0 * commit_weight) * (looked - latent) / count
    )
    g_looked = jnp.where(encoder, 0.0, jnp.where(is_code, g_looked, 0.0)).astype(bf16)
    row = lax.broadcasted_iota(jnp.int32, (256, 128), 0)
    tiled = jnp.where(lanes(256, 128) % cdim + patch == row, 1.0, 0.0).astype(bf16)
    copies = mm(g_looked, tiled)
    per = 128 // cdim
    away = code_ref[...] // LO - lanes(tokens, 128) // cdim
    spread = jnp.concatenate(
        [
            jnp.where(away == i * per, copies, 0.0).astype(bf16)
            for i in range(sum_ref.shape[1] // 128)
        ],
        axis=1,
    )
    low_row = code_row_ref[...] & (LO - 1)
    onehot = jnp.where(
        lax.broadcasted_iota(jnp.int32, (LO, tokens), 0) == low_row, 1.0, 0.0
    ).astype(bf16)
    sum_ref[...] += mm(onehot, spread)

    @pl.when(step == pl.num_programs(0) - 1)
    def _():
        offset = patch + cdim - 128
        gain_ref[...] = jnp.zeros_like(gain_ref)
        gain_ref[offset : offset + 1, :] = gain_one_ref[0:1, :]
        gain_ref[offset + 1 : offset + 3, :] = stat_ref[1:3, :]
        thin = head_ref[...] + mm(gin_t_ref[...], entered_ref[...])
        ends = gain_ref[...].T
        split = keep_ref.shape[0]
        for i, ref in enumerate((keep_ref, sent_ref)):
            here = slice(i * split, (i + 1) * split)
            ref[:, :128] = thin[here, :128].astype(bf16)
            ref[:, 128:256] = (thin[here, 128:] + ends[here, :]).astype(bf16)
            if aligned:
                blocks = split // aligned
                for b in range(blocks):
                    at = (i * blocks + b) * 128
                    for j in range(LO // aligned):
                        ref[b * aligned : (b + 1) * aligned, 256 + j * 128 : 384 + j * 128] = sum_ref[
                            j * aligned : (j + 1) * aligned, at : at + 128
                        ].astype(bf16)
        if not aligned:
            book_ref[...] = sum_ref[...].astype(bf16)


def finish(side, code, code_row, gin, patches, looked, latent, a, gains, gin_t, head, stat, gain_one, wide, aligned, patch, cdim, codes, block=256):
    width = gin.shape[1]
    table = (LO, codes // LO * cdim)
    columns = 256 + (LO // aligned * 128 if aligned else 0)
    thin_spec = pl.BlockSpec((width // 2, 256), lambda i: (0, wide // 256))
    return call(
        functools.partial(finish_kernel, patch, cdim, aligned),
        "finish",
        [((width // 2, columns), bf16)] * 2 + ([] if aligned else [(table, bf16)]),
        flops=4 << 30,
        nbytes=8 << 20,
        limit=24 << 20,
        grid=(SEQ // block,),
        in_specs=[SCALAR, rows_of(block, 128), columns_of(1, block), rows_of(block, width)]
        + [rows_of(block, 256)] * 2
        + [columns_of(cdim, block)]
        + [thin_spec] * 2
        + [whole()] * 5,
        out_specs=[whole()] * (2 if aligned else 3),
        scratch_shapes=[
            pltpu.VMEM((SEQ, 256), bf16),
            pltpu.VMEM((128, width), f32),
            pltpu.VMEM(table, f32),
        ],
    )(side, code, code_row, gin, patches, looked, latent, *a, gains, gin_t, head, stat, gain_one)


def untangle(block, per, cdim):
    rows = block.shape[0]
    step = per * cdim
    tall = jnp.concatenate([block[:, j * step : (j + 1) * step] for j in range(LO // rows)], axis=0)
    if step < 128:
        tall = jnp.concatenate([tall, jnp.zeros((LO, 128 - step), f32)], axis=1)
    turned = tall.T
    return jnp.concatenate([turned[i * cdim : (i + 1) * cdim, :] for i in range(per)], axis=1)


def settle_kernel(own_ref, sent_ref, qkv_own_ref, qkv_sent_ref, thin_ref, book_ref, stat_ref, thin_out_ref, total_ref):
    cdim, codes_here = book_ref.shape
    book = book_ref[...].astype(bf16).astype(f32)
    shrink = lax.rsqrt(jnp.sum(book * book, axis=0, keepdims=True) + 1.0)
    unit = book * shrink
    grad = untangle(thin_ref[:, 256:], codes_here // LO, cdim)
    grad = shrink * (grad - unit * jnp.sum(grad * unit, axis=0, keepdims=True))
    small = thin_ref[:, :256]
    rows, wide = qkv_sent_ref.shape
    thin_out_ref[:, :wide] = qkv_sent_ref[...]
    thin_out_ref[:, wide : wide + 256] = small
    for i in range(cdim // rows):
        first = wide + 256 + i * codes_here
        thin_out_ref[:, first : first + codes_here] = grad[i * rows : (i + 1) * rows, :]

    def total(value):
        return jnp.sum(jnp.sum(value * value, axis=0, keepdims=True), axis=1, keepdims=True)

    squares = total(grad) + total(small)
    for ref in (own_ref, sent_ref, qkv_own_ref, qkv_sent_ref):
        squares += total(ref[...])
    loss = jnp.sum(stat_ref[3:4, :], axis=1, keepdims=True)
    row = lax.broadcasted_iota(jnp.int32, (8, 128), 0)
    total_ref[...] = jnp.where(row == 0, squares, jnp.where(row == 1, loss, 0.0))


def settle(rest_own, rest_sent, qkv_own, qkv_sent, thin, book_t, stat):
    return call(
        settle_kernel,
        "settle",
        [((thin.shape[0], qkv_sent.shape[1] + 256 + book_t.shape[0] // thin.shape[0] * book_t.shape[1]), f32), ((8, 128), f32)],
        nbytes=1 << 20,
        limit=12 << 20,
        in_specs=[whole()] * 7,
        out_specs=[whole()] * 2,
    )(rest_own, rest_sent, qkv_own, qkv_sent, thin, book_t, stat)


def adam(master, moment, square, clipped, rate):
    moment_new = first_decay * moment + (1.0 - first_decay) * clipped
    square_new = second_decay * square + (1.0 - second_decay) * clipped * clipped
    moment_hat = moment_new / (1.0 - first_decay**STEP)
    square_hat = square_new / (1.0 - second_decay**STEP)
    updated = master - rate * (
        moment_hat / (jnp.sqrt(square_hat) + adam_epsilon) + weight_decay * master
    )
    return updated, moment_new, square_new


def update_kernel(side_ref, *refs):
    grads, weights, outs = refs[:7], refs[7:25], refs[25:43]
    loss_ref, count_ref, norm_ref, turn_ref = refs[43:]
    total_ref, all_ref, own_ref, got_ref, qkv_own_ref, last_own_ref, last_got_ref = grads
    wide = qkv_own_ref.shape[1]
    side = side_ref[0]
    encoder = side == 0
    norm = jnp.sqrt(total_ref[0:1, 0:1])
    norm_ref[...] = norm
    loss_ref[...] = total_ref[1:2, 0:1]
    count_ref[...] = all_ref[3:4, 0:1]
    factor = clip_norm / jnp.maximum(norm, clip_norm)

    def apply(which, index, grad):
        three = [weights[3 * which + i][index] for i in range(3)]
        for i, value in enumerate(adam(*three, grad * factor, learn_rates[which])):
            outs[3 * which + i][index] = value

    half = weights[0].shape[3]
    units = weights[3].shape[3]
    rows = own_ref.shape[0]
    patch = weights[6].shape[2]
    cdim = weights[9].shape[1]
    gains = []
    for at, rest, qkv, small in (
        (side, own_ref, qkv_own_ref, last_own_ref),
        (1 - side, got_ref, last_got_ref, last_got_ref),
    ):
        for j in range(3):
            apply(0, (at, j), qkv[:, j * half : (j + 1) * half])
        apply(0, (at, 3), rest[:, :half])
        for j in range(2):
            apply(1, (at, j), rest[:, half + j * units : half + (j + 1) * units])
        apply(2, (at,), small[:, wide : wide + patch])
        turn_ref[0:rows, :] = small[:, wide + 128 : wide + 256]
        turned = turn_ref[...].T[:, :rows]
        first = patch - 128
        apply(3, (at,), turned[first : first + cdim])
        gains.append(turned[first + cdim : first + cdim + 3])
    codes_here = weights[12].shape[1]
    for i in range(cdim // rows):
        here = slice(wide + 256 + i * codes_here, wide + 256 + (i + 1) * codes_here)
        apply(4, (slice(i * rows, (i + 1) * rows),), jnp.where(encoder, last_got_ref[:, here], last_own_ref[:, here]))
    apply(5, (slice(0, 3),), jnp.where(encoder, gains[0], gains[1]))
    apply(5, (slice(3, 6),), jnp.where(encoder, gains[1], gains[0]))


def update(side, grads, weights):
    out = [(w.shape, f32) for w in weights] + [((1, 1), f32)] * 3
    return pl.pallas_call(
        update_kernel,
        name="update",
        out_shape=[jax.ShapeDtypeStruct(s, d) for s, d in out],
        in_specs=[SCALAR] + [whole()] * (len(grads) + len(weights)),
        out_specs=[whole()] * len(out),
        scratch_shapes=[pltpu.VMEM((128, 128), f32)],
        compiler_params=pltpu.CompilerParams(vmem_limit_bytes=24 << 20),
        cost_estimate=pl.CostEstimate(flops=1 << 22, bytes_accessed=10 << 20, transcendentals=0),
    )(side, *grads, *weights)


def body(
    pixels,
    valid_mask,
    code_index,
    attention_weight,
    attention_moment,
    attention_square,
    feedforward_weight,
    feedforward_moment,
    feedforward_square,
    pixel_weight,
    pixel_moment,
    pixel_square,
    code_weight,
    code_moment,
    code_square,
    codebook,
    codebook_moment,
    codebook_square,
    norm_gains,
    gains_moment,
    gains_square,
):
    side = lax.axis_index("mp")
    place = lax.axis_index("dp")
    parts = lax.axis_size("dp")
    bits = bits_of(parts)
    encoder = side == 0
    flag = side.astype(jnp.int32).reshape(1)
    rows = attention_weight.shape[2]
    half = attention_weight.shape[3]
    units = feedforward_weight.shape[3]
    patch = pixel_weight.shape[1]
    cdim = code_weight.shape[1]
    codes_here = codebook.shape[0]
    codes = codes_here * parts
    per = codes_here // LO
    wide = 3 * half
    aligned = rows if per * cdim == 128 and rows % 16 == 0 else 0

    pixels_t, valid_t = pixels.T, valid_mask.T
    own_a, rest_own, sent = pack(
        flag, attention_weight, feedforward_weight, pixel_weight.transpose(0, 2, 1), code_weight,
        codebook.T, norm_gains, valid_t,
    )
    got = swap_mp(sent)
    held_a = widen(own_a, 0)
    patches, valid, code_column, code_row = inputs(
        place.astype(jnp.int32).reshape(1), pixels_t, after(valid_t, own_a), code_index[None, :],
        bits, codes_here,
    )
    held_a = widen(after(held_a, valid), 1)
    held_b, rest_got = widen(got[:, :wide], 0), widen(got[:, wide:], 0)
    rest_own = widen(rest_own, 0, (rest_got,))
    early = jnp.concatenate(together(rest_own, rest_got), axis=1)
    held_b = widen(after(held_b, held_a), 1)
    for step in range(2, bits - 1):
        held_a = widen(held_a, step)
    a = (held_a, swap_core(held_a))
    held_b = after(held_b, held_a)
    for step in range(2, bits - 2):
        held_b = widen(held_b, step)

    book = None
    if not aligned:
        book = jnp.concatenate(a)[:, wide + 256 :].reshape(parts, rows, LO // rows, per * cdim)
        book = book.transpose(2, 1, 0, 3).reshape(LO, -1)
    hidden, looked, qkv_a, normed, normed_t, gains = enter(
        flag, code_column, patches, a, book, aligned, wide, patch, cdim, codes
    )
    mixed_0, log_0 = attend(qkv_a, 0, 1)
    held_b = widen(held_b, bits - 2, (mixed_0,))
    rest = widen(early, 1, (mixed_0,))
    qkv_a, rest, held_b = together(qkv_a, rest, held_b, mixed_0)[:3]
    b = (held_b, swap_core(held_b))
    mixed_1, log_1 = attend(qkv_a, 1, 1)
    for step in range(2, bits - 1):
        rest = widen(rest, step, (mixed_1,))
    qkv_b = project(after(normed, mixed_1), b)
    mixed_2, log_2 = attend(qkv_b, 0, 2)
    rest = after(rest, mixed_2)
    rest = (rest, swap_core(rest))

    go_a, go_b, g_middle, latent, keep_r, sent_r, g_head, stat = middle(
        flag, (mixed_0, mixed_1, mixed_2), hidden, patches, looked, valid, rest, a, gains, wide, patch, cdim
    )
    last = bits - 2
    grads_a0 = attend_back(qkv_a, mixed_0, go_a, log_0, 0, 0)
    latent_there = swap_mp(after(latent, *grads_a0))
    rest = halves(fold((keep_r, sent_r), None, grads_a0))
    grads_a1 = attend_back(after(qkv_a, *rest), mixed_1, go_a, log_1, 1, 0)
    grads_b0 = attend_back(after(qkv_b, *grads_a1), mixed_2, go_b, log_2, 0, 0)
    rest = halves(fold(rest, last, grads_b0))
    grads_b1 = attend_back(after(qkv_b, *rest), mixed_2, go_b, log_2, 1, 1)
    grads = grads_a0 + grads_a1 + grads_b0 + grads_b1
    keep_q, sent_q = project_grad(normed_t, grads)
    g_in, gin_t, gain_one = leave(grads, after(hidden, keep_q), g_middle, a, b, gains)
    part = halves(fold((keep_q, sent_q), None, (gin_t,)))
    for step in range(last - 1, 0, -1):
        rest = halves(fold(rest, step, (gin_t,)))
    keep_s, sent_s, *g_book = finish(
        flag, code_column, code_row, after(g_in, *part, *rest), patches, looked, latent_there,
        a, gains, gin_t, g_head, stat, gain_one, wide, aligned, patch, cdim, codes,
    )
    if not aligned:
        g_book = g_book[0].reshape(LO // rows, rows, parts, per * cdim)
        g_book = g_book.transpose(2, 1, 0, 3).reshape(2, parts * rows // 2, -1)
        keep_s = jnp.concatenate([keep_s, g_book[0]], axis=1)
        sent_s = jnp.concatenate([sent_s, g_book[1]], axis=1)
    thin = fold((keep_s, sent_s), None)
    part = fold(part, last, (keep_s,))
    for step in range(last, -1, -1):
        thin = fold(halves(thin), step)
        if step > 0:
            part = fold(halves(part), step - 1)
        if step == max(last - 1, 0):
            rest = added(fold(rest, 0, (thin[0],)))
            rest_got = swap_mp(rest[:, rest.shape[1] // 2 :])
    thin, part = added(thin), added(part)
    qkv_own, qkv_sent = part[:, :wide], part[:, wide:]
    rest_own, rest_sent = rest[:, : rest.shape[1] // 2], rest[:, rest.shape[1] // 2 :]
    last_own, totals = settle(rest_own, rest_sent, qkv_own, qkv_sent, thin, codebook.T, stat)
    totals = totals + swap_core(totals)
    last_got = swap_mp(after(last_own, totals))
    totals = all_sum(totals)
    thin_view = (0, 2, 1)
    weights = (
        attention_weight,
        attention_moment,
        attention_square,
        feedforward_weight,
        feedforward_moment,
        feedforward_square,
        pixel_weight.transpose(thin_view),
        pixel_moment.transpose(thin_view),
        pixel_square.transpose(thin_view),
        code_weight,
        code_moment,
        code_square,
        codebook.T,
        codebook_moment.T,
        codebook_square.T,
        norm_gains,
        gains_moment,
        gains_square,
    )
    grads = (
        totals, gains, rest_own, rest_got, qkv_own, last_own, last_got
    )
    *new, loss, count, norm = update(flag, grads, weights)
    new[6:9] = [x.transpose(thin_view) for x in new[6:9]]
    new[12:15] = [x.T for x in new[12:15]]
    return tuple(new) + tuple(x.reshape(()) for x in (loss, count, norm))


def solution(mesh):
    wide = P(None, None, "dp", "mp")
    thin = P(None, None, "dp")
    rows = P("dp", None)
    gain = P(None, "dp")
    weights = (wide,) * 6 + (thin,) * 6 + (rows,) * 3 + (gain,) * 3
    return jax.shard_map(
        body,
        mesh=mesh,
        in_specs=(rows, rows, P("dp")) + weights,
        out_specs=weights + (P(), P(), P()),
        check_vma=False,
    )
```

```python
import functools

import jax
import jax.numpy as jnp
from jax import lax
from jax.experimental import pallas as pl
from jax.experimental.pallas import tpu as pltpu
from jax.sharding import PartitionSpec as P

HD = 64
SEQ = 1024
STEP = 10

norm_epsilon = 1e-05
commit_weight = 0.25
clip_norm = 0.003
learn_rates = (0.2, 0.02, 0.04, 0.5, 0.5, 0.6)
first_decay = 0.9
second_decay = 0.999
weight_decay = 0.01
adam_epsilon = 1e-08

bf16 = jnp.bfloat16
f32 = jnp.float32


def swap_mp(value):
    return lax.ppermute(value, "mp", [(0, 1), (1, 0)])


def bits_of(size):
    return size.bit_length() - 1


def step_orders(bits):
    high = list(range(bits - 1, 1, -1))
    return (high + [1], high[:1] + [1] + high[1:])


def swap_step(value, step):
    size = lax.axis_size("dp")
    orders = step_orders(bits_of(size))
    return lax.ppermute(value, "dp", [(i, i ^ (1 << orders[i & 1][step])) for i in range(size)])


def swap_core(value):
    return lax.ppermute(value, "dp", [(i, i ^ 1) for i in range(lax.axis_size("dp"))])


def place_of(mask, core, bits):
    places = [
        sum(((mask >> bit) & 1) << step for step, bit in enumerate(order))
        for order in step_orders(bits)
    ]
    same = mask & 1 == 0
    return jnp.where(same == (core == 0), places[0], places[1]) + jnp.where(same, 0, 1 << (bits - 1))


def after(value, *others):
    return lax.optimization_barrier((value,) + others)[0]


def together(*arrays):
    return lax.optimization_barrier(arrays)


def widen(held, step, later=()):
    got = swap_step(held, step)
    if later:
        held = after(held, *later)
    return jnp.concatenate([held, got], axis=0)


def fold(pair, step, later=()):
    keep, sent = pair
    got = swap_core(sent) if step is None else swap_step(sent, step)
    if later:
        keep = after(keep, *later)
    return keep, got


def added(pair):
    return pair[0].astype(f32) + pair[1].astype(f32)


def halves(pair):
    split = pair[0].shape[0] // 2
    keep = added([x[:split] for x in pair])
    return together(keep, added([x[split:] for x in pair]).astype(bf16))


def all_sum(value):
    size = lax.axis_size("dp")
    for bit in range(1, bits_of(size)):
        value = value + lax.ppermute(value, "dp", [(i, i ^ (1 << bit)) for i in range(size)])
    return value + swap_mp(value)


NN = (((1,), (0,)), ((), ()))
NT = (((1,), (1,)), ((), ()))
VMEM_LIMIT = 48 << 20
LO = 128


def mm(a, b, dims=NN):
    return lax.dot_general(a, b, dims, preferred_element_type=f32)


def whole():
    return pl.BlockSpec(memory_space=pltpu.VMEM)


def rows_of(block, width):
    return pl.BlockSpec((block, width), lambda i: (i, 0))


def columns_of(height, block):
    return pl.BlockSpec((height, block), lambda i: (0, i))


def call(kernel, name, out, flops=0, nbytes=0, exps=0, limit=VMEM_LIMIT, **kw):
    return pl.pallas_call(
        kernel,
        name=name,
        out_shape=[jax.ShapeDtypeStruct(s, d) for s, d in out],
        compiler_params=pltpu.CompilerParams(vmem_limit_bytes=limit),
        cost_estimate=pl.CostEstimate(flops=flops, bytes_accessed=nbytes, transcendentals=exps),
        **kw,
    )


SCALAR = pl.BlockSpec(memory_space=pltpu.SMEM)


def attend_kernel(q_ref, k_ref, v_ref, o_ref, log_ref, vt_ref):
    vt_ref[...] = v_ref[...].T
    keys = k_ref[...]
    q = q_ref[...] * jnp.asarray(HD**-0.5, bf16)
    low = lax.broadcasted_iota(jnp.int32, q.shape, 1) < HD
    zero = jnp.zeros_like(q)
    mixed = []
    for head in range(2):
        own = jnp.where(low if head == 0 else ~low, q, zero)
        s = mm(keys, own, NT)
        peak = jnp.max(s, axis=0, keepdims=True)
        e = jnp.exp(s - peak)
        total = jnp.sum(e, axis=0, keepdims=True)
        part = mm(vt_ref[head * HD : (head + 1) * HD, :], e.astype(bf16))
        mixed.append(part * (1.0 / total))
        log_ref[0, head : head + 1, :] = peak + jnp.log(total)
    o_ref[...] = jnp.concatenate(mixed, axis=0).T.astype(bf16)


def column_block(at):
    return pl.BlockSpec((SEQ, 2 * HD), lambda i: (0, at + i))


def attend(qkv, first, count):
    pairs = qkv.shape[1] // (6 * HD)
    return call(
        attend_kernel,
        "attend",
        [((SEQ, 2 * HD * count), bf16), ((count, 2, SEQ), f32)],
        flops=count * 8 * SEQ * SEQ * 256,
        nbytes=16 * SEQ * HD * count,
        limit=28 << 20,
        grid=(count,),
        in_specs=[column_block(first), column_block(pairs + first), column_block(2 * pairs + first)],
        out_specs=[column_block(0), pl.BlockSpec((1, 2, SEQ), lambda i: (i, 0, 0))],
        scratch_shapes=[pltpu.VMEM((2 * HD, SEQ), bf16)],
    )(qkv, qkv, qkv)


def attend_back_kernel(
    chunk, q_ref, k_ref, v_ref, o_ref, go_ref, log_ref, gq_ref, gk_ref, gv_ref, kt_ref, sk_ref, sv_ref
):
    kt_ref[...] = k_ref[...].T
    keys = k_ref[...]
    values = v_ref[...]
    low = lax.broadcasted_iota(jnp.int32, (chunk, 2 * HD), 1) < HD
    scale = HD**-0.5
    for start in range(0, SEQ, chunk):
        rows = pl.ds(start, chunk)
        q = q_ref[rows, :] * jnp.asarray(scale, bf16)
        go = go_ref[rows, :]
        product = (go.astype(f32) * o_ref[rows, :].astype(f32)).T
        zero = jnp.zeros_like(q)
        grads = []
        sums = None
        for head in range(2):
            here = low if head == 0 else ~low
            own = jnp.where(here, q, zero)
            own_go = jnp.where(here, go, zero)
            inner = jnp.sum(product[head * HD : (head + 1) * HD, :], axis=0, keepdims=True)
            p = jnp.exp(mm(keys, own, NT) - log_ref[0, head : head + 1, rows])
            gp = mm(values, own_go, NT)
            gs = (p * (gp - inner)).astype(bf16)
            gk = mm(gs, own)
            gv = mm(p.astype(bf16), own_go)
            sums = (gk, gv) if head == 0 else (sums[0] + gk, sums[1] + gv)
            grads.append(mm(kt_ref[head * HD : (head + 1) * HD, :], gs))
        gq_ref[rows, :] = (jnp.concatenate(grads, axis=0).T * scale).astype(bf16)
        if start == 0:
            sk_ref[...] = sums[0]
            sv_ref[...] = sums[1]
        elif start + chunk < SEQ:
            sk_ref[...] += sums[0]
            sv_ref[...] += sums[1]
        else:
            gk_ref[...] = (sk_ref[...] + sums[0]).astype(bf16)
            gv_ref[...] = (sv_ref[...] + sums[1]).astype(bf16)


def attend_back(qkv, o, go, log_total, pair, at, chunk=512):
    pairs = go.shape[1] // (2 * HD)
    return call(
        functools.partial(attend_back_kernel, chunk),
        "attend_back",
        [((SEQ, 2 * HD), bf16)] * 3,
        flops=20 * SEQ * SEQ * 256,
        nbytes=16 * SEQ * 128,
        limit=20 << 20,
        grid=(1,),
        in_specs=[
            column_block(pair),
            column_block(pairs + pair),
            column_block(2 * pairs + pair),
            column_block(at),
            column_block(pair),
            pl.BlockSpec((1, 2, SEQ), lambda i: (at, 0, 0)),
        ],
        out_specs=[column_block(0)] * 3,
        scratch_shapes=[
            pltpu.VMEM((2 * HD, SEQ), bf16),
            pltpu.VMEM((SEQ, 2 * HD), f32),
            pltpu.VMEM((SEQ, 2 * HD), f32),
        ],
    )(qkv, qkv, qkv, o, go, log_total)


def lanes(rows, columns):
    return lax.broadcasted_iota(jnp.int32, (rows, columns), 1)


def normed_of(hidden):
    centred = hidden - jnp.mean(hidden, axis=-1, keepdims=True)
    spread = jnp.mean(centred * centred, axis=-1, keepdims=True)
    inverse = lax.rsqrt(spread + norm_epsilon)
    return centred * inverse, inverse


def norm_pull(grad, unit, inverse, gain):
    scaled = grad * gain
    return inverse * (
        scaled
        - jnp.mean(scaled, axis=-1, keepdims=True)
        - unit * jnp.mean(scaled * unit, axis=-1, keepdims=True)
    )


def by_two(value, low_ref, high_ref, columns=slice(None)):
    split = low_ref.shape[0]
    return mm(value[:, :split], low_ref[:, columns]) + mm(value[:, split:], high_ref[:, columns])


def to_two(value, low_ref, high_ref, columns=slice(None)):
    return jnp.concatenate(
        [mm(value, low_ref[:, columns], NT), mm(value, high_ref[:, columns], NT)], axis=1
    )


def pack_kernel(
    side_ref, attention_ref, feedforward_ref, pixel_ref, code_ref, book_ref, gains_ref, valid_ref,
    own_ref, rest_ref, sent_ref, turn_ref,
):
    side = side_ref[0]
    rows, half = attention_ref.shape[2], attention_ref.shape[3]
    units = feedforward_ref.shape[3]
    patch, cdim = pixel_ref.shape[2], code_ref.shape[1]
    at = 3 * half
    for j in range(3):
        own_ref[:, j * half : (j + 1) * half] = attention_ref[side, j].astype(bf16)
        sent_ref[:, j * half : (j + 1) * half] = attention_ref[1 - side, j].astype(bf16)
    for ref, which, first in ((rest_ref, side, 0), (sent_ref, 1 - side, at)):
        ref[:, first : first + half] = attention_ref[which, 3].astype(bf16)
        for j in range(2):
            here = first + half + j * units
            ref[:, here : here + units] = feedforward_ref[which, j].astype(bf16)
    count = jnp.sum(valid_ref[...], axis=0, keepdims=True)
    count = jnp.sum(count.astype(f32), axis=1, keepdims=True).astype(jnp.int32)
    first = patch - 128
    turn_ref[...] = jnp.zeros_like(turn_ref)
    turn_ref[first : first + cdim, 0:rows] = code_ref[side]
    first += cdim
    turn_ref[first : first + 3, 0:rows] = jnp.where(side == 0, gains_ref[0:3, :], gains_ref[3:6, :])
    digits = (count & 255, (count >> 8) & 255, count >> 16)
    for i, digit in enumerate(digits):
        turn_ref[first + 3 + i : first + 4 + i, 0:1] = digit.astype(f32)
    own_ref[:, at + 128 : at + 256] = turn_ref[...].T[0:rows, :].astype(bf16)
    own_ref[:, at : at + patch] = pixel_ref[side].astype(bf16)
    at += 256
    book = book_ref[...].astype(bf16).astype(f32)
    unit = book * lax.rsqrt(jnp.sum(book * book, axis=0, keepdims=True) + 1.0)
    per = book.shape[1] // LO
    tall = jnp.concatenate([unit[:, i * LO : (i + 1) * LO] for i in range(per)], axis=0)
    if per * cdim < 128:
        tall = jnp.concatenate([tall, jnp.zeros((128 - per * cdim, LO), f32)], axis=0)
    wide = tall.T
    step = per * cdim
    for j in range(LO // rows):
        own_ref[:, at + j * step : at + (j + 1) * step] = wide[
            j * rows : (j + 1) * rows, :step
        ].astype(bf16)


def pack(side, attention, feedforward, pixel_t, code, book_t, gains, valid_t):
    _, _, rows, half = attention.shape
    units = feedforward.shape[3]
    cdim, codes = book_t.shape
    rest = half + 2 * units
    return call(
        pack_kernel,
        "pack",
        [
            ((rows, 3 * half + 256 + cdim * codes // rows), bf16),
            ((rows, rest), bf16),
            ((rows, 3 * half + rest), bf16),
        ],
        nbytes=4 << 20,
        limit=60 << 20,
        in_specs=[SCALAR] + [whole()] * 7,
        out_specs=[whole()] * 3,
        scratch_shapes=[pltpu.VMEM((128, 128), f32)],
    )(side, attention, feedforward, pixel_t, code, book_t, gains, valid_t)


def inputs_kernel(core_ref, pixels_ref, valid_ref, code_ref, patches_ref, mask_ref, column_ref, row_ref, *, bits, codes_here):
    patch, tokens = pixels_ref.shape
    zeros = jnp.zeros((256 - patch, tokens), f32)
    patches_ref[...] = jnp.concatenate([pixels_ref[...].astype(f32), zeros], axis=0).T.astype(bf16)
    mask_ref[...] = jnp.concatenate([valid_ref[...].astype(f32), zeros], axis=0).T.astype(bf16)
    code = jnp.broadcast_to(code_ref[...], (8, tokens))
    place = core_ref[0]
    turned = place_of((code // codes_here) ^ place, place & 1, bits) * codes_here + code % codes_here
    row_ref[...] = turned[0:1, :]
    column_ref[...] = jnp.broadcast_to(turned[0:1, :].astype(f32), (128, tokens)).T.astype(jnp.int32)


def inputs(place, pixels_t, valid_t, code, bits, codes_here):
    return call(
        functools.partial(inputs_kernel, bits=bits, codes_here=codes_here),
        "inputs",
        [((SEQ, 256), bf16)] * 2 + [((SEQ, 128), jnp.int32), ((1, SEQ), jnp.int32)],
        nbytes=3 << 20,
        limit=60 << 20,
        in_specs=[SCALAR] + [whole()] * 3,
        out_specs=[whole()] * 4,
    )(place, pixels_t, valid_t, code)


def enter_kernel(
    patch, cdim, aligned, side_ref, code_ref, patches_ref, low_a_ref, high_a_ref, *refs,
):
    if aligned:
        hidden_ref, looked_ref, qkv_ref, normed_ref, normed_t_ref, gains_ref, book_ref = refs
    else:
        book_ref, hidden_ref, looked_ref, qkv_ref, normed_ref, normed_t_ref, gains_ref = refs
    step = pl.program_id(0)
    tokens = code_ref.shape[0]
    wide = qkv_ref.shape[1]
    split = low_a_ref.shape[0]
    thin = slice(wide, wide + 256)

    @pl.when(step == 0)
    def _():
        first = patch + cdim - 128
        gains_ref[...] = jnp.zeros_like(gains_ref)
        digits = 0.0
        for i, ref in enumerate((low_a_ref, high_a_ref)):
            turned = ref[:, wide + 128 : wide + 256].astype(f32).T
            gains_ref[0:3, i * split : (i + 1) * split] = turned[first : first + 3, :]
            digits += jnp.sum(turned, axis=1, keepdims=True)
        count = (
            digits[first + 3 : first + 4]
            + 256.0 * digits[first + 4 : first + 5]
            + 65536.0 * digits[first + 5 : first + 6]
        )
        gains_ref[3:4, :] = jnp.broadcast_to(count, (1, gains_ref.shape[1]))
        if aligned:
            rows = aligned
            for i, ref in enumerate((low_a_ref, high_a_ref)):
                blocks = split // rows
                for b in range(blocks):
                    at = (i * blocks + b) * 128
                    for j in range(LO // rows):
                        column = wide + 256 + j * 128
                        book_ref[j * rows : (j + 1) * rows, at : at + 128] = ref[
                            b * rows : (b + 1) * rows, column : column + 128
                        ]

    code = code_ref[...]
    low, high = code & (LO - 1), code // LO
    lane = lanes(tokens, 128)
    onehot = jnp.where(lane == low, 1.0, 0.0).astype(bf16)
    spread = mm(onehot, book_ref[...])
    group = lane // cdim
    per = 128 // cdim
    away = high - group
    picked = jnp.zeros((tokens, 128), f32)
    for i in range(spread.shape[1] // 128):
        picked += jnp.where(away == i * per, spread[:, i * 128 : (i + 1) * 128], 0.0)
    lane_out = lanes(128, 256)
    fold_in = (
        lax.broadcasted_iota(jnp.int32, (128, 256), 0) % cdim + patch == lane_out
    ) & (lane_out < patch + cdim)
    looked = mm(picked.astype(bf16), jnp.where(fold_in, 1.0, 0.0).astype(bf16)).astype(bf16)
    looked_ref[...] = looked
    encoder = side_ref[0] == 0
    entered = jnp.where(encoder, patches_ref[...].astype(f32), looked.astype(f32)).astype(bf16)
    hidden = to_two(entered, low_a_ref, high_a_ref, thin)
    hidden_ref[...] = hidden
    unit, _ = normed_of(hidden)
    normed = (unit * gains_ref[0:1, :]).astype(bf16)
    normed_t_ref[...] = normed.T
    normed_ref[...] = normed
    qkv_ref[...] = by_two(normed, low_a_ref, high_a_ref, slice(0, wide)).astype(bf16)


def enter(side, code, patches, a, book, aligned, wide, patch, cdim, codes, block=512):
    width = 2 * a[0].shape[0]
    table = (LO, codes // LO * cdim)
    return call(
        functools.partial(enter_kernel, patch, cdim, aligned),
        "enter",
        [
            ((SEQ, width), f32),
            ((SEQ, 256), bf16),
            ((SEQ, wide), bf16),
            ((SEQ, width), bf16),
            ((width, SEQ), bf16),
            ((8, width), f32),
        ],
        flops=8 << 30,
        nbytes=12 << 20,
        limit=28 << 20,
        grid=(SEQ // block,),
        in_specs=[SCALAR, rows_of(block, 128), rows_of(block, 256)]
        + [whole()] * (2 if aligned else 3),
        out_specs=[
            rows_of(block, width),
            rows_of(block, 256),
            rows_of(block, wide),
            rows_of(block, width),
            columns_of(width, block),
            pl.BlockSpec((8, width), lambda i: (0, 0)),
        ],
        scratch_shapes=[pltpu.VMEM(table, bf16)] if aligned else [],
    )(side, code, patches, *a, *([] if aligned else [book]))


def project_kernel(normed_ref, low_ref, high_ref, qkv_ref):
    qkv_ref[...] = by_two(normed_ref[...], low_ref, high_ref).astype(bf16)


def project(normed, b, block=512):
    wide = b[0].shape[1]
    return call(
        project_kernel,
        "project",
        [((SEQ, wide), bf16)],
        flops=2 << 30,
        nbytes=4 << 20,
        limit=16 << 20,
        grid=(SEQ // block,),
        in_specs=[rows_of(block, normed.shape[1]), whole(), whole()],
        out_specs=[rows_of(block, wide)],
    )(normed, *b)[0]


GELU_A, GELU_B = 0.7978845608028654, 0.044715


def middle_kernel(
    patch, cdim, runs, side_ref, *refs,
):
    mixed_refs, refs = refs[:runs], refs[runs:]
    (
    hidden_ref, patches_ref, looked_ref, valid_ref,
    low_ref, high_ref, thin_low_ref, thin_high_ref, gains_ref,
    go_a_ref, go_b_ref, gm_ref, latent_ref, keep_ref, sent_ref,
    head_grad_ref, stat_ref,
    active_ref, gbefore_ref, low_t_ref, two_t_ref, branch_t_ref, final_t_ref, head_ref,
    full_a_ref, full_b_ref, thin_ref, copy_sem,
    ) = refs
    step = pl.program_id(0)
    tokens = hidden_ref.shape[0]
    half = go_a_ref.shape[1]
    units = (low_ref.shape[1] // 2 - half) // 2
    rows = pl.ds(pl.multiple_of(step * tokens, tokens), tokens)
    encoder = side_ref[0] == 0
    rests = (full_a_ref, full_b_ref)
    out, up, down = slice(0, half), slice(half, half + units), slice(half + units, half + 2 * units)

    @pl.when(step == 0)
    def _():
        stat_ref[...] = jnp.zeros_like(stat_ref)
        split = low_ref.shape[0]
        each = half + 2 * units
        copies = [
            pltpu.make_async_copy(
                piece.at[:, pl.ds(i * each, each)],
                rests[i].at[pl.ds(j * split, split), :],
                copy_sem.at[2 * i + j],
            )
            for i in range(2)
            for j, piece in enumerate((low_ref, high_ref))
        ]
        for copy in copies:
            copy.start()
        thin_ref[:split, :] = thin_low_ref[...]
        thin_ref[split:, :] = thin_high_ref[...]
        for copy in copies:
            copy.wait()

    gain_two, gain_final = gains_ref[1:2, :], gains_ref[2:3, :]
    middle = hidden_ref[...]
    mixed = jnp.concatenate([ref[rows, :] for ref in mixed_refs], axis=1)
    for i, rest in enumerate(rests):
        middle += mm(mixed[:, i * half : (i + 1) * half], rest[:, out], NT)
    unit_two, inverse_two = normed_of(middle)
    two = (unit_two * gain_two).astype(bf16)
    two_t_ref[:, rows] = two.T
    slopes = []
    for i, rest in enumerate(rests):
        before = mm(two, rest[:, up])
        square = before * before
        bent = jnp.tanh(GELU_A * before * (1.0 + GELU_B * square))
        active_ref[rows, i * units : (i + 1) * units] = (0.5 * before * (1.0 + bent)).astype(bf16)
        slopes.append(
            0.5 * (1.0 + bent)
            + (0.5 * GELU_A) * before * (1.0 - bent * bent) * (1.0 + 3.0 * GELU_B * square)
        )

    @pl.when(step >= 0)
    def _():
        total = middle
        for i, rest in enumerate(rests):
            total += mm(active_ref[rows, i * units : (i + 1) * units], rest[:, down], NT)
        gm_ref[...] = total

    result = gm_ref[...]
    unit, inverse = normed_of(result)
    final = (unit * gain_final).astype(bf16)
    final_t_ref[:, rows] = final.T
    seen = mm(final, thin_ref[...])
    lane = lanes(tokens, 256)
    is_code = (lane >= patch) & (lane < patch + cdim)
    count = gains_ref[3:4, 0:1]
    patches = patches_ref[...].astype(f32)
    looked = looked_ref[...].astype(f32)
    valid = valid_ref[...].astype(f32)
    gap = jnp.where(lane < patch, seen - patches, 0.0)
    root = jnp.sqrt(gap * gap + 1.0)
    g_out = valid * (2.0 * gap + gap / root) / count
    raw = jnp.where(is_code, seen, 0.0)
    shrink = lax.rsqrt(jnp.sum(raw * raw, axis=-1, keepdims=True) + 1.0)
    latent = raw * shrink
    away = latent - looked
    g_latent = (2.0 * commit_weight) * away / count
    g_raw = shrink * (g_latent - latent * jnp.sum(g_latent * latent, axis=-1, keepdims=True))
    losses = jnp.where(encoder, commit_weight * away * away, valid * (gap * gap + root - 1.0))
    stat_ref[3:4, 0:256] += jnp.sum(losses, axis=0, keepdims=True)
    start = patch // 128 * 128
    latent_ref[...] = latent[:, start : start + 128].T[patch - start : patch - start + cdim, :]
    g_head = jnp.where(
        encoder, jnp.where(is_code, g_raw, 0.0), jnp.where(lane < patch, g_out, 0.0)
    ).astype(bf16)
    head_ref[rows, :] = g_head
    g_final = mm(g_head, thin_ref[...], NT)
    stat_ref[2:3, :] += jnp.sum(g_final * unit, axis=0, keepdims=True)
    g_result = norm_pull(g_final, unit, inverse, gain_final)

    low = g_result.astype(bf16)
    low_t_ref[:, rows] = low.T
    g_two = None
    for i, rest in enumerate(rests):
        g_before = (mm(low, rest[:, down]) * slopes[i]).astype(bf16)
        gbefore_ref[rows, i * units : (i + 1) * units] = g_before
        part = mm(g_before, rest[:, up], NT)
        g_two = part if g_two is None else g_two + part
    stat_ref[1:2, :] += jnp.sum(g_two * unit_two, axis=0, keepdims=True)
    g_middle = g_result + norm_pull(g_two, unit_two, inverse_two, gain_two)
    gm_ref[...] = g_middle
    branch = g_middle.astype(bf16)
    branch_t_ref[:, rows] = branch.T
    for ref, rest in zip((go_a_ref, go_b_ref), rests):
        ref[...] = mm(branch, rest[:, out]).astype(bf16)

    @pl.when(step == pl.num_programs(0) - 1)
    def _():
        head_grad_ref[...] = mm(final_t_ref[...], head_ref[...])
        split = keep_ref.shape[0]
        for i in range(2):
            first = i * (half + 2 * units)
            for ref, part in ((keep_ref, slice(0, split)), (sent_ref, slice(split, 2 * split))):
                at = 0
                for mixed_ref in mixed_refs:
                    here = at - i * half
                    at += mixed_ref.shape[1]
                    if 0 <= here < half:
                        ref[:, first + here : first + at - i * half] = mm(
                            branch_t_ref[part, :], mixed_ref[...]
                        ).astype(bf16)
                for at in range(0, units, 512):
                    columns = slice(i * units + at, i * units + at + 512)
                    here = first + half + at
                    ref[:, here : here + 512] = mm(two_t_ref[part, :], gbefore_ref[:, columns]).astype(bf16)
                    here += units
                    ref[:, here : here + 512] = mm(low_t_ref[part, :], active_ref[:, columns]).astype(bf16)


def middle(side, mixed, hidden, patches, looked, valid, rest, thin, gains, at, patch, cdim, block=512):
    width = hidden.shape[1]
    half = sum(m.shape[1] for m in mixed) // 2
    each = rest[0].shape[1] // 2
    hiddens = each - half
    thin_spec = pl.BlockSpec((width // 2, 256), lambda i: (0, at // 256))
    return call(
        functools.partial(middle_kernel, patch, cdim, len(mixed)),
        "middle",
        [((SEQ, half), bf16)] * 2
        + [((SEQ, width), f32), ((cdim, SEQ), f32)]
        + [(rest[0].shape, bf16)] * 2
        + [((width, 256), f32), ((8, width), f32)],
        flops=16 << 30,
        nbytes=20 << 20,
        limit=32 << 20,
        grid=(SEQ // block,),
        in_specs=[SCALAR]
        + [whole()] * len(mixed)
        + [rows_of(block, width)]
        + [rows_of(block, 256)] * 3
        + [whole()] * 2
        + [thin_spec] * 2
        + [whole()],
        out_specs=[rows_of(block, half)] * 2
        + [rows_of(block, width), columns_of(cdim, block)]
        + [whole()] * 4,
        scratch_shapes=[
            pltpu.VMEM((SEQ, hiddens), bf16),
            pltpu.VMEM((SEQ, hiddens), bf16),
            pltpu.VMEM((width, SEQ), bf16),
            pltpu.VMEM((width, SEQ), bf16),
            pltpu.VMEM((width, SEQ), bf16),
            pltpu.VMEM((width, SEQ), bf16),
            pltpu.VMEM((SEQ, 256), bf16),
            pltpu.VMEM((width, each), bf16),
            pltpu.VMEM((width, each), bf16),
            pltpu.VMEM((width, 256), bf16),
            pltpu.SemaphoreType.DMA((4,)),
        ],
    )(side, *mixed, hidden, patches, looked, valid, *rest, *thin, gains)


def project_grad_kernel(normed_t_ref, *refs):
    grads, outs = refs[:12], refs[12:]
    split = outs[0].shape[0]
    for i, ref in enumerate(outs):
        normed_t = normed_t_ref[i * split : (i + 1) * split, :]
        for side in range(2):
            for j in range(3):
                first, second = grads[6 * side + j], grads[6 * side + 3 + j]
                both = jnp.concatenate([first[...], second[...]], axis=1)
                width = both.shape[1]
                at = (3 * side + j) * width
                ref[:, at : at + width] = mm(normed_t, both).astype(bf16)


def project_grad(normed_t, grads):
    width = normed_t.shape[0]
    return call(
        project_grad_kernel,
        "project_grad",
        [((width // 2, 24 * HD), bf16)] * 2,
        flops=4 << 30,
        nbytes=8 << 20,
        limit=20 << 20,
        in_specs=[whole()] * 13,
        out_specs=[whole()] * 2,
    )(normed_t, *grads)


def leave_kernel(*refs):
    grads = refs[:12]
    (
        hidden_ref, gm_ref, low_a_ref, high_a_ref, low_b_ref, high_b_ref, gains_ref,
        gin_ref, gin_t_ref, gain_ref,
    ) = refs[12:]

    @pl.when(pl.program_id(0) == 0)
    def _():
        gain_ref[...] = jnp.zeros_like(gain_ref)

    gain = gains_ref[0:1, :]
    unit, inverse = normed_of(hidden_ref[...])
    g_normed = None
    for i, rest in enumerate(((low_a_ref, high_a_ref), (low_b_ref, high_b_ref))):
        first, second = grads[6 * i : 6 * i + 3], grads[6 * i + 3 : 6 * i + 6]
        side_by_side = jnp.concatenate(
            [r[...] for pair in zip(first, second) for r in pair], axis=1
        )
        part = to_two(side_by_side, *rest)
        g_normed = part if g_normed is None else g_normed + part
    gain_ref[0:1, :] += jnp.sum(g_normed * unit, axis=0, keepdims=True)
    g_in = (gm_ref[...] + norm_pull(g_normed, unit, inverse, gain)).astype(bf16)
    gin_ref[...] = g_in
    gin_t_ref[...] = g_in.T


def leave(grads, hidden, gm, a, b, gains, block=512):
    width = hidden.shape[1]
    wide = b[0].shape[1]
    wide_spec = pl.BlockSpec((width // 2, wide), lambda i: (0, 0))
    return call(
        leave_kernel,
        "leave",
        [((SEQ, width), bf16), ((width, SEQ), bf16), ((8, width), f32)],
        flops=4 << 30,
        nbytes=8 << 20,
        limit=24 << 20,
        grid=(SEQ // block,),
        in_specs=[rows_of(block, 2 * HD)] * 12
        + [rows_of(block, width)] * 2
        + [wide_spec] * 4
        + [whole()],
        out_specs=[
            rows_of(block, width),
            columns_of(width, block),
            pl.BlockSpec((8, width), lambda i: (0, 0)),
        ],
    )(*grads, hidden, gm, *a, *b, gains)


def finish_kernel(
    patch, cdim, aligned, side_ref, code_ref, code_row_ref, gin_ref, patches_ref, looked_ref, latent_ref,
    thin_low_ref, thin_high_ref, gains_ref, gin_t_ref, head_ref, stat_ref, gain_one_ref, keep_ref, sent_ref, *more,
):
    if aligned:
        entered_ref, gain_ref, sum_ref = more
    else:
        book_ref, entered_ref, gain_ref, sum_ref = more
    step = pl.program_id(0)
    tokens = gin_ref.shape[0]
    rows = pl.ds(pl.multiple_of(step * tokens, tokens), tokens)
    encoder = side_ref[0] == 0
    g_in = gin_ref[...]
    looked = looked_ref[...].astype(f32)
    entered_ref[rows, :] = jnp.where(encoder, patches_ref[...].astype(f32), looked).astype(bf16)

    @pl.when(step == 0)
    def _():
        sum_ref[...] = jnp.zeros_like(sum_ref)

    start = patch // 128 * 128
    before, later = patch - start, 128 - (patch - start) - cdim
    pieces = [jnp.zeros((before, tokens), f32)] if before else []
    pieces.append(latent_ref[...])
    pieces += [jnp.zeros((later, tokens), f32)] if later else []
    latent = jnp.concatenate(pieces, axis=0).T
    latent = jnp.concatenate([jnp.zeros((tokens, start), f32), latent], axis=1)
    lane = lanes(tokens, 256)
    is_code = (lane >= patch) & (lane < patch + cdim)
    count = gains_ref[3:4, 0:1]
    g_looked = (
        by_two(g_in, thin_low_ref, thin_high_ref)
        + (2.0 * commit_weight) * (looked - latent) / count
    )
    g_looked = jnp.where(encoder, 0.0, jnp.where(is_code, g_looked, 0.0)).astype(bf16)
    row = lax.broadcasted_iota(jnp.int32, (256, 128), 0)
    tiled = jnp.where(lanes(256, 128) % cdim + patch == row, 1.0, 0.0).astype(bf16)
    copies = mm(g_looked, tiled)
    per = 128 // cdim
    away = code_ref[...] // LO - lanes(tokens, 128) // cdim
    spread = jnp.concatenate(
        [
            jnp.where(away == i * per, copies, 0.0).astype(bf16)
            for i in range(sum_ref.shape[1] // 128)
        ],
        axis=1,
    )
    low_row = code_row_ref[...] & (LO - 1)
    onehot = jnp.where(
        lax.broadcasted_iota(jnp.int32, (LO, tokens), 0) == low_row, 1.0, 0.0
    ).astype(bf16)
    sum_ref[...] += mm(onehot, spread)

    @pl.when(step == pl.num_programs(0) - 1)
    def _():
        offset = patch + cdim - 128
        gain_ref[...] = jnp.zeros_like(gain_ref)
        gain_ref[offset : offset + 1, :] = gain_one_ref[0:1, :]
        gain_ref[offset + 1 : offset + 3, :] = stat_ref[1:3, :]
        thin = head_ref[...] + mm(gin_t_ref[...], entered_ref[...])
        ends = gain_ref[...].T
        split = keep_ref.shape[0]
        for i, ref in enumerate((keep_ref, sent_ref)):
            here = slice(i * split, (i + 1) * split)
            ref[:, :128] = thin[here, :128].astype(bf16)
            ref[:, 128:256] = (thin[here, 128:] + ends[here, :]).astype(bf16)
            if aligned:
                blocks = split // aligned
                for b in range(blocks):
                    at = (i * blocks + b) * 128
                    for j in range(LO // aligned):
                        ref[b * aligned : (b + 1) * aligned, 256 + j * 128 : 384 + j * 128] = sum_ref[
                            j * aligned : (j + 1) * aligned, at : at + 128
                        ].astype(bf16)
        if not aligned:
            book_ref[...] = sum_ref[...].astype(bf16)


def finish(side, code, code_row, gin, patches, looked, latent, a, gains, gin_t, head, stat, gain_one, wide, aligned, patch, cdim, codes, block=512):
    width = gin.shape[1]
    table = (LO, codes // LO * cdim)
    columns = 256 + (LO // aligned * 128 if aligned else 0)
    thin_spec = pl.BlockSpec((width // 2, 256), lambda i: (0, wide // 256))
    return call(
        functools.partial(finish_kernel, patch, cdim, aligned),
        "finish",
        [((width // 2, columns), bf16)] * 2 + ([] if aligned else [(table, bf16)]),
        flops=4 << 30,
        nbytes=8 << 20,
        limit=24 << 20,
        grid=(SEQ // block,),
        in_specs=[SCALAR, rows_of(block, 128), columns_of(1, block), rows_of(block, width)]
        + [rows_of(block, 256)] * 2
        + [columns_of(cdim, block)]
        + [thin_spec] * 2
        + [whole()] * 5,
        out_specs=[whole()] * (2 if aligned else 3),
        scratch_shapes=[
            pltpu.VMEM((SEQ, 256), bf16),
            pltpu.VMEM((128, width), f32),
            pltpu.VMEM(table, f32),
        ],
    )(side, code, code_row, gin, patches, looked, latent, *a, gains, gin_t, head, stat, gain_one)


def untangle(block, per, cdim):
    rows = block.shape[0]
    step = per * cdim
    tall = jnp.concatenate([block[:, j * step : (j + 1) * step] for j in range(LO // rows)], axis=0)
    if step < 128:
        tall = jnp.concatenate([tall, jnp.zeros((LO, 128 - step), f32)], axis=1)
    turned = tall.T
    return jnp.concatenate([turned[i * cdim : (i + 1) * cdim, :] for i in range(per)], axis=1)


def settle_kernel(own_ref, sent_ref, qkv_own_ref, qkv_sent_ref, thin_ref, book_ref, stat_ref, thin_out_ref, total_ref):
    cdim, codes_here = book_ref.shape
    book = book_ref[...].astype(bf16).astype(f32)
    shrink = lax.rsqrt(jnp.sum(book * book, axis=0, keepdims=True) + 1.0)
    unit = book * shrink
    grad = untangle(thin_ref[:, 256:], codes_here // LO, cdim)
    grad = shrink * (grad - unit * jnp.sum(grad * unit, axis=0, keepdims=True))
    small = thin_ref[:, :256]
    rows, wide = qkv_sent_ref.shape
    thin_out_ref[:, :wide] = qkv_sent_ref[...]
    thin_out_ref[:, wide : wide + 256] = small
    for i in range(cdim // rows):
        first = wide + 256 + i * codes_here
        thin_out_ref[:, first : first + codes_here] = grad[i * rows : (i + 1) * rows, :]

    def total(value):
        return jnp.sum(jnp.sum(value * value, axis=0, keepdims=True), axis=1, keepdims=True)

    squares = total(grad) + total(small)
    for ref in (own_ref, sent_ref, qkv_own_ref, qkv_sent_ref):
        squares += total(ref[...])
    loss = jnp.sum(stat_ref[3:4, :], axis=1, keepdims=True)
    row = lax.broadcasted_iota(jnp.int32, (8, 128), 0)
    total_ref[...] = jnp.where(row == 0, squares, jnp.where(row == 1, loss, 0.0))


def settle(rest_own, rest_sent, qkv_own, qkv_sent, thin, book_t, stat):
    return call(
        settle_kernel,
        "settle",
        [((thin.shape[0], qkv_sent.shape[1] + 256 + book_t.shape[0] // thin.shape[0] * book_t.shape[1]), f32), ((8, 128), f32)],
        nbytes=1 << 20,
        limit=12 << 20,
        in_specs=[whole()] * 7,
        out_specs=[whole()] * 2,
    )(rest_own, rest_sent, qkv_own, qkv_sent, thin, book_t, stat)


def adam(master, moment, square, clipped, rate):
    moment_new = first_decay * moment + (1.0 - first_decay) * clipped
    square_new = second_decay * square + (1.0 - second_decay) * clipped * clipped
    moment_hat = moment_new / (1.0 - first_decay**STEP)
    square_hat = square_new / (1.0 - second_decay**STEP)
    updated = master - rate * (
        moment_hat / (jnp.sqrt(square_hat) + adam_epsilon) + weight_decay * master
    )
    return updated, moment_new, square_new


def update_kernel(side_ref, *refs):
    grads, weights, outs = refs[:7], refs[7:25], refs[25:43]
    loss_ref, count_ref, norm_ref, turn_ref = refs[43:]
    total_ref, all_ref, own_ref, got_ref, qkv_own_ref, last_own_ref, last_got_ref = grads
    wide = qkv_own_ref.shape[1]
    side = side_ref[0]
    encoder = side == 0
    norm = jnp.sqrt(total_ref[0:1, 0:1])
    norm_ref[...] = norm
    loss_ref[...] = total_ref[1:2, 0:1]
    count_ref[...] = all_ref[3:4, 0:1]
    factor = clip_norm / jnp.maximum(norm, clip_norm)

    def apply(which, index, grad):
        three = [weights[3 * which + i][index] for i in range(3)]
        for i, value in enumerate(adam(*three, grad * factor, learn_rates[which])):
            outs[3 * which + i][index] = value

    half = weights[0].shape[3]
    units = weights[3].shape[3]
    rows = own_ref.shape[0]
    patch = weights[6].shape[2]
    cdim = weights[9].shape[1]
    gains = []
    for at, rest, qkv, small in (
        (side, own_ref, qkv_own_ref, last_own_ref),
        (1 - side, got_ref, last_got_ref, last_got_ref),
    ):
        for j in range(3):
            apply(0, (at, j), qkv[:, j * half : (j + 1) * half])
        apply(0, (at, 3), rest[:, :half])
        for j in range(2):
            apply(1, (at, j), rest[:, half + j * units : half + (j + 1) * units])
        apply(2, (at,), small[:, wide : wide + patch])
        turn_ref[0:rows, :] = small[:, wide + 128 : wide + 256]
        turned = turn_ref[...].T[:, :rows]
        first = patch - 128
        apply(3, (at,), turned[first : first + cdim])
        gains.append(turned[first + cdim : first + cdim + 3])
    codes_here = weights[12].shape[1]
    for i in range(cdim // rows):
        here = slice(wide + 256 + i * codes_here, wide + 256 + (i + 1) * codes_here)
        apply(4, (slice(i * rows, (i + 1) * rows),), jnp.where(encoder, last_got_ref[:, here], last_own_ref[:, here]))
    apply(5, (slice(0, 3),), jnp.where(encoder, gains[0], gains[1]))
    apply(5, (slice(3, 6),), jnp.where(encoder, gains[1], gains[0]))


def update(side, grads, weights):
    out = [(w.shape, f32) for w in weights] + [((1, 1), f32)] * 3
    return pl.pallas_call(
        update_kernel,
        name="update",
        out_shape=[jax.ShapeDtypeStruct(s, d) for s, d in out],
        in_specs=[SCALAR] + [whole()] * (len(grads) + len(weights)),
        out_specs=[whole()] * len(out),
        scratch_shapes=[pltpu.VMEM((128, 128), f32)],
        compiler_params=pltpu.CompilerParams(vmem_limit_bytes=24 << 20),
        cost_estimate=pl.CostEstimate(flops=1 << 22, bytes_accessed=10 << 20, transcendentals=0),
    )(side, *grads, *weights)


def body(
    pixels,
    valid_mask,
    code_index,
    attention_weight,
    attention_moment,
    attention_square,
    feedforward_weight,
    feedforward_moment,
    feedforward_square,
    pixel_weight,
    pixel_moment,
    pixel_square,
    code_weight,
    code_moment,
    code_square,
    codebook,
    codebook_moment,
    codebook_square,
    norm_gains,
    gains_moment,
    gains_square,
):
    side = lax.axis_index("mp")
    place = lax.axis_index("dp")
    parts = lax.axis_size("dp")
    bits = bits_of(parts)
    encoder = side == 0
    flag = side.astype(jnp.int32).reshape(1)
    rows = attention_weight.shape[2]
    half = attention_weight.shape[3]
    units = feedforward_weight.shape[3]
    patch = pixel_weight.shape[1]
    cdim = code_weight.shape[1]
    codes_here = codebook.shape[0]
    codes = codes_here * parts
    per = codes_here // LO
    wide = 3 * half
    aligned = rows if per * cdim == 128 and rows % 16 == 0 else 0

    pixels_t, valid_t = pixels.T, valid_mask.T
    own_a, rest_own, sent = pack(
        flag, attention_weight, feedforward_weight, pixel_weight.transpose(0, 2, 1), code_weight,
        codebook.T, norm_gains, valid_t,
    )
    got = swap_mp(sent)
    held_a = widen(own_a, 0)
    patches, valid, code_column, code_row = inputs(
        place.astype(jnp.int32).reshape(1), pixels_t, after(valid_t, own_a), code_index[None, :],
        bits, codes_here,
    )
    held_a = widen(after(held_a, valid), 1)
    held_b, rest_got = widen(got[:, :wide], 0), widen(got[:, wide:], 0)
    rest_own = widen(rest_own, 0, (rest_got,))
    early = jnp.concatenate(together(rest_own, rest_got), axis=1)
    held_b = widen(after(held_b, held_a), 1)
    for step in range(2, bits - 1):
        held_a = widen(held_a, step)
    a = (held_a, swap_core(held_a))
    held_b = after(held_b, held_a)
    for step in range(2, bits - 2):
        held_b = widen(held_b, step)

    book = None
    if not aligned:
        book = jnp.concatenate(a)[:, wide + 256 :].reshape(parts, rows, LO // rows, per * cdim)
        book = book.transpose(2, 1, 0, 3).reshape(LO, -1)
    hidden, looked, qkv_a, normed, normed_t, gains = enter(
        flag, code_column, patches, a, book, aligned, wide, patch, cdim, codes
    )
    mixed_0, log_0 = attend(qkv_a, 0, 1)
    held_b = widen(held_b, bits - 2, (mixed_0,))
    rest = widen(early, 1, (mixed_0,))
    qkv_a, rest, held_b = together(qkv_a, rest, held_b, mixed_0)[:3]
    b = (held_b, swap_core(held_b))
    mixed_1, log_1 = attend(qkv_a, 1, 1)
    for step in range(2, bits - 1):
        rest = widen(rest, step, (mixed_1,))
    qkv_b = project(after(normed, mixed_1), b)
    mixed_2, log_2 = attend(qkv_b, 0, 2)
    rest = after(rest, mixed_2)
    rest = (rest, swap_core(rest))

    go_a, go_b, g_middle, latent, keep_r, sent_r, g_head, stat = middle(
        flag, (mixed_0, mixed_1, mixed_2), hidden, patches, looked, valid, rest, a, gains, wide, patch, cdim
    )
    last = bits - 2
    grads_a0 = attend_back(qkv_a, mixed_0, go_a, log_0, 0, 0)
    latent_there = swap_mp(after(latent, *grads_a0))
    rest = halves(fold((keep_r, sent_r), None, grads_a0))
    grads_a1 = attend_back(after(qkv_a, *rest), mixed_1, go_a, log_1, 1, 0)
    grads_b0 = attend_back(after(qkv_b, *grads_a1), mixed_2, go_b, log_2, 0, 0)
    rest = halves(fold(rest, last, grads_b0))
    grads_b1 = attend_back(after(qkv_b, *rest), mixed_2, go_b, log_2, 1, 1)
    grads = grads_a0 + grads_a1 + grads_b0 + grads_b1
    keep_q, sent_q = project_grad(normed_t, grads)
    g_in, gin_t, gain_one = leave(grads, after(hidden, keep_q), g_middle, a, b, gains)
    pieces = [
        fold((keep_q[:, at : at + wide], sent_q[:, at : at + wide]), None, (gin_t,))
        for at in (0, wide)
    ]
    part = halves([jnp.concatenate(x, axis=1) for x in zip(*pieces)])
    for step in range(last - 1, 0, -1):
        rest = halves(fold(rest, step, (part[0],)))
    keep_s, sent_s, *g_book = finish(
        flag, code_column, code_row, after(g_in, *part, *rest), patches, looked, latent_there,
        a, gains, gin_t, g_head, stat, gain_one, wide, aligned, patch, cdim, codes,
    )
    if not aligned:
        g_book = g_book[0].reshape(LO // rows, rows, parts, per * cdim)
        g_book = g_book.transpose(2, 1, 0, 3).reshape(2, parts * rows // 2, -1)
        keep_s = jnp.concatenate([keep_s, g_book[0]], axis=1)
        sent_s = jnp.concatenate([sent_s, g_book[1]], axis=1)
    next_thin = halves(fold((keep_s, sent_s), None))
    part = fold(part, last, (keep_s,))
    for step in range(last, 0, -1):
        next_part = together(*halves(part), *next_thin)[:2]
        thin = fold(next_thin, step)
        next_thin = halves(thin)
        part = fold(next_part, step - 1, next_thin)
    rest = added(fold(rest, 0, next_thin))
    rest_got = swap_mp(rest[:, rest.shape[1] // 2 :])
    thin = fold(next_thin, 0)
    thin, part = added(thin), added(part)
    qkv_own, qkv_sent = part[:, :wide], part[:, wide:]
    rest_own, rest_sent = rest[:, : rest.shape[1] // 2], rest[:, rest.shape[1] // 2 :]
    last_own, totals = settle(rest_own, rest_sent, qkv_own, qkv_sent, thin, codebook.T, stat)
    totals = totals + swap_core(totals)
    last_got = swap_mp(after(last_own, totals))
    totals = all_sum(totals)
    thin_view = (0, 2, 1)
    weights = (
        attention_weight,
        attention_moment,
        attention_square,
        feedforward_weight,
        feedforward_moment,
        feedforward_square,
        pixel_weight.transpose(thin_view),
        pixel_moment.transpose(thin_view),
        pixel_square.transpose(thin_view),
        code_weight,
        code_moment,
        code_square,
        codebook.T,
        codebook_moment.T,
        codebook_square.T,
        norm_gains,
        gains_moment,
        gains_square,
    )
    grads = (
        totals, gains, rest_own, rest_got, qkv_own, last_own, last_got
    )
    *new, loss, count, norm = update(flag, grads, weights)
    new[6:9] = [x.transpose(thin_view) for x in new[6:9]]
    new[12:15] = [x.T for x in new[12:15]]
    return tuple(new) + tuple(x.reshape(()) for x in (loss, count, norm))


def solution(mesh):
    wide = P(None, None, "dp", "mp")
    thin = P(None, None, "dp")
    rows = P("dp", None)
    gain = P(None, "dp")
    weights = (wide,) * 6 + (thin,) * 6 + (rows,) * 3 + (gain,) * 3
    return jax.shard_map(
        body,
        mesh=mesh,
        in_specs=(rows, rows, P("dp")) + weights,
        out_specs=weights + (P(), P(), P()),
        check_vma=False,
    )
```
